32 devices in a mesh: dp: 8 (over y, x, core), tensor: 4 (over z).
Axes of the slice: x: 2, y: 2, z: 4, core: 2. Of those that a mesh axis runs over, the one named last changes fastest.
Arguments:
- hidden_in: bfloat16 [8192, 2560], P(('dp', 'tensor')), may hold values from -6 to 6
- attention_gain: bfloat16 [2560], P(('dp', 'tensor')), may hold values from 0.25 to 1.75
- query_down: bfloat16 [2560, 768], P(('dp', 'tensor')), may hold values from -0.125 to 0.125
- query_norm: bfloat16 [768], P(('dp', 'tensor')), may hold values from 0.25 to 1.75
- latent_down: bfloat16 [2560, 288], P(('dp', 'tensor')), may hold values from -0.125 to 0.125
- latent_norm: bfloat16 [256], P(('dp', 'tensor')), may hold values from 0.25 to 1.75
- query_up: bfloat16 [768, 3840], P('dp', 'tensor'), may hold values from -0.21875 to 0.21875
- latent_up: bfloat16 [256, 5120], P('dp', 'tensor'), may hold values from -0.375 to 0.375
- output_weight: bfloat16 [2560, 2560], P('tensor', 'dp'), may hold values from -2 to 2
- feed_gain: bfloat16 [2560], P(('dp', 'tensor')), may hold values from 0.25 to 1.75
- gate_weight: bfloat16 [2560, 6400], P('dp', 'tensor'), may hold values from -0.125 to 0.125
- up_weight: bfloat16 [2560, 6400], P('dp', 'tensor'), may hold values from -0.125 to 0.125
- down_weight: bfloat16 [6400, 2560], P('tensor', 'dp'), may hold values from -0.875 to 0.875
- cotangent: bfloat16 [8192, 2560], P(('dp', 'tensor')), may hold values from -6 to 6
- document_lengths: int32 [8, 4], P('dp'), may hold values from 0 to 1024, as said below
Outputs:
- layer_output: bfloat16 [8192, 2560], P(('dp', 'tensor'))
- input_gradient: bfloat16 [8192, 2560], P(('dp', 'tensor'))
- attention_gain_gradient: float32 [2560], P(('dp', 'tensor'))
- query_down_gradient: float32 [2560, 768], P(('dp', 'tensor'))
- query_norm_gradient: float32 [768], P(('dp', 'tensor'))
- latent_down_gradient: float32 [2560, 288], P(('dp', 'tensor'))
- latent_norm_gradient: float32 [256], P(('dp', 'tensor'))
- query_up_gradient: float32 [768, 3840], P('dp', 'tensor')
- latent_up_gradient: float32 [256, 5120], P('dp', 'tensor')
- output_weight_gradient: float32 [2560, 2560], P('tensor', 'dp')
- feed_gain_gradient: float32 [2560], P(('dp', 'tensor'))
- gate_gradient: float32 [2560, 6400], P('dp', 'tensor')
- up_gradient: float32 [2560, 6400], P('dp', 'tensor')
- down_gradient: float32 [6400, 2560], P('tensor', 'dp')
The draws below stay inside these ranges and needn't reach their ends.
Inputs may be any that keep to these rules, and one draw needn't show every extreme that they name: `document_lengths`: each row holds the lengths of the 4 documents of one data group in order; their sum is at most 1024 and the slots after it are padding, a segment of its own. Documents may be empty. In every group one document is longer than 768, and some group holds a single document of 1024 tokens.
All inputs are finite; a program needn't handle non-finite values.
Results may differ from the reference program's by a relative error of at most 0.02.
Values may be sent and summed in bfloat16 or wider, within the bound.
No kernel may reach another device: no remote copies, remote signals or barrier semaphores. Data moves between devices by JAX's collectives and lax.ppermute only.
A program may use at most 256 MiB of HBM per device.

```python
import math
import jax
import jax.numpy as jnp
from jax import lax

D = 2560
QR = 768
KVR = 256
ROPE = 32
NOPE = 64
VD = 64
H = 40
FF = 6400
GROUP_TOK = 1024
DOCS = 4
TOKENS = 8192
N_DP = 8


def draw_document_lengths(key, part):
    key = jax.random.fold_in(key, 11)
    keys = jax.random.split(key, 4)
    place = jax.random.randint(keys[0], (N_DP, 1), 0, DOCS)
    longest = jax.random.randint(keys[1], (N_DP, 1), 3 * GROUP_TOK // 4 + 1, 7 * GROUP_TOK // 8 + 1)
    short_top = GROUP_TOK // (8 * (DOCS - 1))
    shorts = jax.random.randint(keys[2], (N_DP, DOCS), 0, short_top + 1)
    chosen = jax.random.randint(keys[3], (), 0, N_DP)
    groups = jnp.arange(N_DP)[:, None]
    slots = jnp.arange(DOCS)[None, :]
    single = groups == chosen
    longest = jnp.where(single, GROUP_TOK, longest)
    shorts = jnp.where(single, 0, shorts)
    return jnp.where(slots == place, longest, shorts).astype(jnp.int32)


def steps_of(rng, dims, cuts, smallest, top_value):
    factor_of, own = 1.0, jax.random.fold_in(rng, 6)
    for axis_at, blocks in cuts:
        steps = jnp.exp(jax.random.uniform(jax.random.fold_in(own, axis_at), (blocks,), jnp.float32, smallest / len(cuts), top_value / len(cuts)))
        factor_of = factor_of * jnp.repeat(steps, dims[axis_at] // blocks).reshape([-1 if axis == axis_at else 1 for axis in range(len(dims))])
    return factor_of


def scatter_about(own_key, dims, scale, bound, cuts=(), held_as=jnp.bfloat16):
    array = jax.random.normal(own_key, dims, jnp.float32) * scale
    if len(cuts) > 0:
        array = steps_of(own_key, dims, cuts, -0.22, 0.18) * array
    return jnp.clip(array, min=-bound, max=bound).astype(held_as)


def setup_inputs(seed: int = 0) -> dict:
    key_of = jax.random.split(jax.random.key(seed), 16)
    hidden_in = scatter_about(key_of[0], (TOKENS, D), 1.0, 6.0, ((0, 32),))
    attention_gain = jnp.clip(1.0 + 0.15 * jax.random.normal(key_of[1], (D,), jnp.float32), 0.25, 1.75).astype(jnp.bfloat16)
    query_down = scatter_about(key_of[2], (D, QR), D ** -0.5, 0.125, ((0, 32),))
    query_norm = jnp.clip(1.0 + 0.15 * jax.random.normal(key_of[3], (QR,), jnp.float32), 0.25, 1.75).astype(jnp.bfloat16)
    latent_down = scatter_about(key_of[4], (D, KVR + ROPE), D ** -0.5, 0.125, ((0, 32),))
    latent_norm = jnp.clip(1.0 + 0.15 * jax.random.normal(key_of[5], (KVR,), jnp.float32), 0.25, 1.75).astype(jnp.bfloat16)
    query_up = scatter_about(key_of[6], (QR, H * (NOPE + ROPE)), QR ** -0.5, 0.21875, ((0, 8), (1, 4)))
    latent_up = scatter_about(key_of[7], (KVR, H * (NOPE + VD)), KVR ** -0.5, 0.375, ((0, 8), (1, 4)))
    output_weight = scatter_about(key_of[8], (H * VD, D), (max(D // 256, 2)) ** -0.5, 2.0, ((0, 4), (1, 8)))
    feed_gain = jnp.clip(1.0 + 0.15 * jax.random.normal(key_of[9], (D,), jnp.float32), 0.25, 1.75).astype(jnp.bfloat16)
    gate_weight = scatter_about(key_of[10], (D, FF), D ** -0.5, 0.125, ((0, 8), (1, 4)))
    up_weight = scatter_about(key_of[11], (D, FF), D ** -0.5, 0.125, ((0, 8), (1, 4)))
    down_weight = scatter_about(key_of[12], (FF, D), (max(FF // 128, 2)) ** -0.5, 0.875, ((0, 4), (1, 8)))
    cotangent = scatter_about(key_of[13], (TOKENS, D), 1.0, 6.0, ((0, 32),))
    document_lengths = draw_document_lengths(jax.random.fold_in(key_of[15], 71), 0)
    return {"hidden_in": hidden_in, "attention_gain": attention_gain, "query_down": query_down, "query_norm": query_norm, "latent_down": latent_down, "latent_norm": latent_norm, "query_up": query_up, "latent_up": latent_up, "output_weight": output_weight, "feed_gain": feed_gain, "gate_weight": gate_weight, "up_weight": up_weight, "down_weight": down_weight, "cotangent": cotangent, "document_lengths": document_lengths}


epsilon = 1e-05
residual_scale = 1.4 / math.sqrt(62.0)
rotary_base = 10000.0
highest = lax.Precision.HIGHEST

@jax.custom_vjp
def low(v):
    return lax.optimization_barrier(v.astype(jnp.bfloat16)).astype(jnp.float32)

@jax.custom_vjp
def low_back(v):
    return v

def low_keep(v):
    return (low(v), None)

def low_pass(kept, grad):
    return (grad,)

def back_keep(v):
    return (v, None)

def back_low(kept, grad):
    return (low(grad),)
low.defvjp(low_keep, low_pass)
low_back.defvjp(back_keep, back_low)

def matmul(left, right):
    return jnp.dot(left, right, precision=highest)

def normalize(values, gain):
    return values * lax.rsqrt(lax.optimization_barrier(jnp.mean(values * values, axis=-1, keepdims=True)) + epsilon) * gain

def rotate_half(values):
    half = values.shape[-1] // 2
    return jnp.concatenate([-values[..., half:], values[..., :half]], axis=-1)

def rotate(values, cosine, sine):
    return values * cosine + rotate_half(values) * sine

def rotary_tables(positions, width):
    steps = jnp.arange(width // 2, dtype=jnp.float32) * (2.0 / width)
    freqs = jnp.exp(steps * -math.log(rotary_base))
    angles = positions.astype(jnp.float32)[:, None] * freqs[None, :]
    cosine = jnp.cos(angles)
    sine = jnp.sin(angles)
    return (jnp.concatenate([cosine, cosine], axis=-1), jnp.concatenate([sine, sine], axis=-1))

def layout(lengths_row, group_tokens):
    slots = jnp.arange(group_tokens, dtype=jnp.int32)
    ends = jnp.cumsum(lengths_row).astype(jnp.int32)
    segment = lax.optimization_barrier(jnp.sum((slots[:, None] >= ends[None, :]).astype(jnp.int32), axis=1))
    starts = jnp.concatenate([jnp.zeros((1,), jnp.int32), ends])
    choose = segment[:, None] == jnp.arange(starts.shape[0], dtype=jnp.int32)[None, :]
    start_of = lax.optimization_barrier(jnp.sum(jnp.where(choose, starts[None, :], 0), axis=1)).astype(jnp.int32)
    return (segment, slots - start_of)

def block_attention(query_block, keys, values, segment_block, slot_block, segment_all, slot_all):
    softmax_scale = 1.0 / math.sqrt(NOPE + ROPE)
    scores = jnp.einsum('qhd,khd->hqk', query_block, keys, precision=highest) * softmax_scale
    scores = low_back(scores)
    allowed = (segment_block[:, None] == segment_all[None, :]) & (slot_all[None, :] <= slot_block[:, None])
    scores = jnp.where(allowed[None], scores, -1e+30)
    probs = jax.nn.softmax(scores, axis=-1)
    return jnp.einsum('hqk,khd->qhd', low(probs), values, precision=highest)

def attend_group(items):
    query_group, key_group, value_group, segment_group = items
    block = min(512, GROUP_TOK)
    count = GROUP_TOK // block
    slot_all = jnp.arange(GROUP_TOK, dtype=jnp.int32)

    def one_block(pieces):
        query_block, segment_block, slot_block = pieces
        return block_attention(query_block, key_group, value_group, segment_block, slot_block, segment_group, slot_all)
    result = lax.map(jax.checkpoint(one_block), (query_group.reshape(count, block, H, NOPE + ROPE), segment_group.reshape(count, block), slot_all.reshape(count, block)))
    return result.reshape(GROUP_TOK, H, VD)

def reference(hidden_in, attention_gain, query_down, query_norm, latent_down, latent_norm, query_up, latent_up, output_weight, feed_gain, gate_weight, up_weight, down_weight, cotangent, document_lengths):
    segments, positions = jax.vmap(lambda lengths_row: layout(lengths_row, GROUP_TOK))(document_lengths)
    cosine, sine = rotary_tables(positions.reshape(-1), ROPE)

    def forward(hidden, gain_in, query_down_w, query_gain, latent_down_w, latent_gain, query_up_w, latent_up_w, output_w, gain_feed, gate_w, up_w, down_w):
        tokens = hidden.shape[0]
        normed = low(normalize(hidden, gain_in))
        query_latent = low_back(matmul(normed, query_down_w))
        query_normed = low(normalize(query_latent, query_gain))
        joint = low_back(matmul(normed, latent_down_w))
        latent_normed = low(normalize(joint[:, :KVR], latent_gain))
        key_rotary = low(rotate(joint[:, KVR:], cosine, sine))
        raw_queries = low_back(matmul(query_normed, query_up_w)).reshape(tokens, H, NOPE + ROPE)
        queries = low(jnp.concatenate([raw_queries[..., :NOPE], rotate(raw_queries[..., NOPE:], cosine[:, None, :], sine[:, None, :])], axis=-1))
        expanded = low_back(matmul(latent_normed, latent_up_w)).reshape(tokens, H, NOPE + VD)
        keys = jnp.concatenate([low(expanded[..., :NOPE]), jnp.broadcast_to(key_rotary[:, None, :], (tokens, H, ROPE))], axis=-1)
        values = low(expanded[..., NOPE:])
        attended = lax.map(attend_group, (queries.reshape(N_DP, GROUP_TOK, H, NOPE + ROPE), keys.reshape(N_DP, GROUP_TOK, H, NOPE + ROPE), values.reshape(N_DP, GROUP_TOK, H, VD), segments))
        attended = low(low_back(attended.reshape(tokens, H * VD)))
        middle = hidden + residual_scale * low_back(matmul(attended, output_w))
        feed_in = low(normalize(middle, gain_feed))
        gate = low_back(matmul(feed_in, gate_w))
        upper = low_back(matmul(feed_in, up_w))
        inner = low(jax.nn.silu(gate) * upper)
        return middle + residual_scale * low_back(matmul(inner, down_w))
    primals = [value.astype(jnp.float32) for value in (hidden_in, attention_gain, query_down, query_norm, latent_down, latent_norm, query_up, latent_up, output_weight, feed_gain, gate_weight, up_weight, down_weight)]
    output, pullback = jax.vjp(forward, *primals)
    grads = pullback(cotangent.astype(jnp.float32))
    return (output.astype(jnp.bfloat16), grads[0].astype(jnp.bfloat16), grads[1], grads[2], grads[3], grads[4], grads[5], grads[6], grads[7], grads[8], grads[9], grads[10], grads[11], grads[12])
```

```python
import math, functools
import jax, jax.numpy as jnp
from jax import lax
from jax.experimental import pallas as pl
from jax.experimental.pallas import tpu as pltpu

KVR, ROPE, NOPE, VD = 256, 32, 64, 64
LANES = 128
softmax_scale = 1.0 / math.sqrt(NOPE + ROPE)
log2_scale = softmax_scale / math.log(2.0)


def nt(left, right):
    return lax.dot_general(left, right, (((1,), (1,)), ((), ())), preferred_element_type=jnp.float32)


def nn(left, right):
    return lax.dot_general(left, right, (((1,), (0,)), ((), ())), preferred_element_type=jnp.float32)


def tn(left, right):
    return lax.dot_general(left, right, (((0,), (0,)), ((), ())), preferred_element_type=jnp.float32)


def attention_forward_kernel(rank, block, latents, up_q, up_kv, cosine, sine_left, sine_right, segment_col, segment_row, attended, queries, expanded, log_total):
    pair = pl.program_id(0)
    group = latents.shape[0]
    lane = lax.broadcasted_iota(jnp.int32, (1, LANES), 1)
    rotary = latents[:, rank + KVR :].astype(jnp.float32)

    @pl.when(pair == 0)
    def _():
        log_total[...] = jnp.zeros_like(log_total)

    found = []
    for half in range(2):
        columns = slice(half * LANES, (half + 1) * LANES)
        raw = nn(latents[:, :rank], up_q[:, columns])
        turned = raw * cosine[...] + pltpu.roll(raw, LANES - ROPE // 2, 1) * sine_left[...] + pltpu.roll(raw, ROPE // 2, 1) * sine_right[...]
        query = turned.astype(jnp.bfloat16)
        queries[:, columns] = query
        both = nn(latents[:, rank : rank + KVR], up_kv[:, columns])
        key = jnp.where(lane < NOPE, both, rotary).astype(jnp.bfloat16)
        both = both.astype(jnp.bfloat16)
        expanded[:, columns] = both
        outs, sums = [], []
        for begin in range(0, group, block):
            end = begin + block
            scores = nt(query[begin:end], key[:end]) * log2_scale
            allowed = segment_col[begin:end, :] == segment_row[:, :end]
            row = lax.broadcasted_iota(jnp.int32, (block, end), 0) + begin
            column = lax.broadcasted_iota(jnp.int32, (block, end), 1)
            scores = jnp.where(allowed & (column <= row), scores, -1e30)
            peak = jnp.max(scores, axis=-1, keepdims=True)
            weights = jnp.exp2(scores - peak)
            total = jnp.sum(weights, axis=-1, keepdims=True)
            outs.append(nn(weights.astype(jnp.bfloat16), both[:end]) / total)
            sums.append(peak + jnp.log2(total))
        found.append(jnp.concatenate(outs, axis=0))
        log_total[...] = jnp.where(lane == 2 * pair + half, jnp.concatenate(sums, axis=0), log_total[...])
    attended[...] = jnp.where(lane < VD, pltpu.roll(found[0], VD, 1), found[1]).astype(jnp.bfloat16)


def attention_backward_kernel(block, queries, expanded, rotary_in, cosine, sine_left, sine_right, segment_col, segment_row, log_total, grad, query_grad, expanded_grad, rotary_grad, key_sum, value_sum):
    pair = pl.program_id(0)
    group = queries.shape[0]
    lane = lax.broadcasted_iota(jnp.int32, (1, LANES), 1)
    rotary = rotary_in[...].astype(jnp.float32)

    @pl.when(pair == 0)
    def _():
        rotary_grad[...] = jnp.zeros_like(rotary_grad)

    grads = grad[...].astype(jnp.float32)
    for half in range(2):
        columns = slice(half * LANES, (half + 1) * LANES)
        query = queries[:, columns]
        both = expanded[:, columns]
        key = jnp.where(lane < NOPE, both.astype(jnp.float32), rotary).astype(jnp.bfloat16)
        out_grad = pltpu.roll(grads, VD, 1) if half == 0 else grads
        out_grad = jnp.where(lane < NOPE, 0.0, out_grad).astype(jnp.bfloat16)
        log_row = log_total[pl.ds(2 * pair + half, 1), :]
        parts = []
        for begin in reversed(range(0, group, block)):
            end = begin + block
            scores = nt(key[:end], query[begin:end]) * log2_scale
            allowed = segment_col[:end, :] == segment_row[:, begin:end]
            row = lax.broadcasted_iota(jnp.int32, (end, block), 0)
            column = lax.broadcasted_iota(jnp.int32, (end, block), 1) + begin
            probs = jnp.where(allowed & (row <= column), jnp.exp2(scores - log_row[:, begin:end]), 0.0)
            prob_grad = nt(both[:end], out_grad[begin:end])
            center = jnp.sum(probs * prob_grad, axis=0, keepdims=True)
            score_grad = (probs * (prob_grad - center)).astype(jnp.bfloat16)
            key_part = nn(score_grad, query[begin:end])
            value_part = nn(probs.astype(jnp.bfloat16), out_grad[begin:end])
            if end == group:
                key_sum[...] = key_part
                value_sum[...] = value_part
            else:
                key_sum[:end] += key_part
                value_sum[:end] += value_part
            parts.append(tn(score_grad, key[:end]))
        found = jnp.concatenate(parts[::-1], axis=0) * softmax_scale
        back = found * cosine[...] - pltpu.roll(found, LANES - ROPE // 2, 1) * sine_left[...] - pltpu.roll(found, ROPE // 2, 1) * sine_right[...]
        query_grad[:, columns] = back.astype(jnp.bfloat16)
        keys = key_sum[...] * softmax_scale
        expanded_grad[:, columns] = jnp.where(lane < NOPE, keys, value_sum[...]).astype(jnp.bfloat16)
        rotary_grad[...] += jnp.where((lane >= NOPE) & (lane < NOPE + ROPE), keys, 0.0)


from jax.sharding import PartitionSpec as P

epsilon = 1e-05
residual_scale = 1.4 / math.sqrt(62.0)
rotary_base = 10000.0

RIGHT = [(i, (i + 1) % 4) for i in range(4)]
LEFT = [(i, (i - 1) % 4) for i in range(4)]
OPPOSITE = [(i, (i + 2) % 4) for i in range(4)]


def inverse_rms(values):
    return lax.rsqrt(jnp.mean(values * values, axis=-1, keepdims=True) + epsilon)


def norm_back(grad, unit, inverse, gain):
    scaled = grad * gain
    return inverse * (scaled - unit * jnp.mean(scaled * unit, axis=-1, keepdims=True))


def rotate_half(values):
    half = values.shape[-1] // 2
    return jnp.concatenate([-values[..., half:], values[..., :half]], axis=-1)


def rotate(values, cosine, sine):
    return values * cosine + rotate_half(values) * sine


def rotate_back(values, cosine, sine):
    return values * cosine - rotate_half(values) * sine


def rotary_tables(positions, width):
    steps = jnp.arange(width // 2, dtype=jnp.float32) * (2.0 / width)
    freqs = jnp.exp(steps * -math.log(rotary_base))
    angles = positions.astype(jnp.float32)[:, None] * freqs[None, :]
    return jnp.cos(angles), jnp.sin(angles)


def layout(lengths_row, group_tokens):
    slots = jnp.arange(group_tokens, dtype=jnp.int32)
    ends = jnp.cumsum(lengths_row)
    segment = jnp.sum((slots[:, None] >= ends[None, :]).astype(jnp.int32), axis=1)
    starts = jnp.concatenate([jnp.zeros((1,), jnp.int32), ends])
    choose = segment[:, None] == jnp.arange(starts.shape[0], dtype=jnp.int32)[None, :]
    start_of = jnp.sum(jnp.where(choose, starts[None, :], 0), axis=1)
    return (segment, slots - start_of)


def after(value, *earlier):
    return lax.optimization_barrier((value, *earlier))[0]


def gather_line(block):
    half = block.shape[0] // 2
    from_left = lax.ppermute(block, "tensor", RIGHT)
    from_right = lax.ppermute(block, "tensor", LEFT)
    far = [lax.ppermute(from_left[:half], "tensor", RIGHT), lax.ppermute(from_right[half:], "tensor", LEFT)]
    return [block, from_left, from_right, *far]


def scatter_line(own, to_left, to_right, far):
    half = own.shape[0] // 2
    low = jnp.bfloat16
    first = lax.ppermute(far[:half].astype(low), "tensor", LEFT)
    second = lax.ppermute(far[half:].astype(low), "tensor", RIGHT)
    to_left = jnp.concatenate([to_left[:half] + first, to_left[half:]]).astype(low)
    to_right = jnp.concatenate([to_right[:half], to_right[half:] + second]).astype(low)
    one = lax.ppermute(to_left, "tensor", LEFT)
    two = lax.ppermute(to_right, "tensor", RIGHT)
    return own.astype(jnp.float32) + one.astype(jnp.float32) + two.astype(jnp.float32)


def exchange_line(blocks):
    own, to_left, to_right, far = blocks
    return [own, lax.ppermute(to_right, "tensor", RIGHT), lax.ppermute(to_left, "tensor", LEFT), lax.ppermute(far, "tensor", OPPOSITE)]


def line_order():
    here = lax.axis_index("tensor")
    return [here, (here + 3) % 4, (here + 1) % 4, (here + 2) % 4]


def by_place(blocks, order, total):
    out = jnp.zeros((total, *blocks[0].shape), blocks[0].dtype)
    for block, place in zip(blocks, order, strict=True):
        out = lax.dynamic_update_index_in_dim(out, block, place, 0)
    return out


def flips(bit):
    return [(i, i ^ bit) for i in range(8)]


def gather_data(block):
    if lax.axis_size("dp") != 8:
        return lax.all_gather(block, "dp", axis=0)
    here = lax.axis_index("dp")
    half = block.shape[0] // 2
    across = lax.ppermute(block, "dp", flips(2))
    along = lax.ppermute(block, "dp", flips(4))
    corner = jnp.concatenate([lax.ppermute(across[:half], "dp", flips(4)), lax.ppermute(along[half:], "dp", flips(2))])
    blocks, order = [], []
    for value, place in ((block, 0), (across, 2), (along, 4), (corner, 6)):
        blocks += [value, lax.ppermute(value, "dp", flips(1))]
        order += [here ^ place, here ^ (place + 1)]
    return by_place(blocks, order, 8)


def scatter_data(blocks):
    if lax.axis_size("dp") != 8:
        count, rows, columns = blocks.shape
        return lax.psum_scatter(blocks.reshape(count * rows, columns), "dp", scatter_dimension=0, tiled=True).astype(jnp.float32)
    here = lax.axis_index("dp")
    half = blocks.shape[1] // 2

    def pick(place):
        return lax.dynamic_index_in_dim(blocks, here ^ place, 0, keepdims=False)

    def both(place):
        return pick(place).astype(jnp.float32) + lax.ppermute(pick(place ^ 1), "dp", flips(1)).astype(jnp.float32)

    corner, across, along, own = (both(6).astype(blocks.dtype), both(2), both(4), both(0))
    one = lax.ppermute(corner[:half], "dp", flips(2))
    two = lax.ppermute(corner[half:], "dp", flips(4))
    across = jnp.concatenate([across[:half], across[half:] + two]).astype(blocks.dtype)
    along = jnp.concatenate([along[:half] + one, along[half:]]).astype(blocks.dtype)
    return own + lax.ppermute(across, "dp", flips(2)).astype(jnp.float32) + lax.ppermute(along, "dp", flips(4)).astype(jnp.float32)


def local(hidden_in, attention_gain, query_down, query_norm, latent_down, latent_norm, query_up, latent_up, output_weight, feed_gain, gate_weight, up_weight, down_weight, cotangent, document_lengths):
    low, wide = jnp.bfloat16, jnp.float32
    replicas = lax.axis_size("dp")
    rows, width = hidden_in.shape
    group = rows * 4
    rank = query_down.shape[1]
    heads = query_up.shape[1] // (NOPE + ROPE)
    hidden_units = gate_weight.shape[1]
    slice_rows = query_down.shape[0]
    order = line_order()

    gains = jnp.concatenate([attention_gain, feed_gain, query_norm, latent_norm])
    joint_width = rank + KVR + ROPE
    gains = jnp.pad(gains, (0, joint_width - gains.shape[0]))[None]
    downs = jnp.concatenate([jnp.concatenate([query_down, latent_down], axis=1), gains], axis=0)
    downs = jnp.pad(downs, ((0, 96 - downs.shape[0] if downs.shape[0] < 96 else 0), (0, 0)))
    down_rows = downs.shape[0]
    downs = by_place(exchange_line([downs] * 4), order, 4).reshape(4 * down_rows, joint_width)
    downs_all = gather_data(downs)
    downs_all = downs_all.reshape(replicas * 4, down_rows, joint_width)
    weights_down = downs_all[:, :slice_rows].reshape(width, joint_width)
    gain_rows = downs_all[:, slice_rows].astype(wide)
    a, b, c, d = slice_rows, 2 * slice_rows, 2 * slice_rows + query_norm.shape[0], 2 * slice_rows + query_norm.shape[0] + latent_norm.shape[0]
    attention_scale = gain_rows[:, :a].reshape(width)
    feed_scale = gain_rows[:, a:b].reshape(width)
    query_scale = gain_rows[:, b:c].reshape(rank)
    latent_scale = gain_rows[:, c:d].reshape(KVR)

    query_up_wide = jnp.pad(query_up.reshape(-1, heads, NOPE + ROPE), ((0, 0), (0, 0), (0, LANES - NOPE - ROPE))).reshape(-1, heads * LANES)
    ups = jnp.concatenate([query_up_wide, latent_up], axis=0)
    ups = after(ups, downs_all)
    ups_all = gather_data(ups)
    up_q = ups_all[:, : query_up.shape[0]].reshape(rank, heads * LANES)
    up_kv = ups_all[:, query_up.shape[0] :].reshape(KVR, heads * LANES)

    out_block = jnp.concatenate([jnp.concatenate(p, axis=0) if isinstance(p, list) else p for p in grouped(gather_line(output_weight.T))], axis=1)
    out_all = gather_data(after(out_block, ups_all)).reshape(width, 4 * heads * VD)
    gate_all = gather_data(after(gate_weight, out_all)).reshape(width, hidden_units)
    upper_all = gather_data(after(up_weight, gate_all)).reshape(width, hidden_units)
    down_all = gather_data(after(down_weight.T, upper_all)).reshape(width, hidden_units)

    segment, position = layout(document_lengths[0], group)
    cosine_half, sine_half = rotary_tables(position, ROPE)
    cosine = jnp.concatenate([cosine_half, cosine_half], axis=-1)
    sine = jnp.concatenate([sine_half, sine_half], axis=-1)
    zeros = lambda n: jnp.zeros((group, n), wide)
    cosine_wide = jnp.concatenate([jnp.ones((group, NOPE), wide), cosine, zeros(ROPE)], axis=1)
    sine_left = jnp.concatenate([zeros(NOPE), -sine_half, zeros(ROPE // 2 + ROPE)], axis=1)
    sine_right = jnp.concatenate([zeros(NOPE + ROPE // 2), sine_half, zeros(ROPE)], axis=1)
    segment_col, segment_row = segment[:, None], segment[None, :]
    first_row = lax.axis_index("tensor") * rows
    local_cosine = lax.dynamic_slice_in_dim(cosine, first_row, rows, 0)
    local_sine = lax.dynamic_slice_in_dim(sine, first_row, rows, 0)

    hidden_float = hidden_in.astype(wide)
    inverse_in = inverse_rms(hidden_float)
    unit_in = hidden_float * inverse_in
    normed = (unit_in * attention_scale).astype(low)
    joint = nn(normed, weights_down)
    query_latent = joint[:, :rank]
    inverse_query = inverse_rms(query_latent)
    unit_query = query_latent * inverse_query
    query_normed = (unit_query * query_scale).astype(low)
    latent_part = joint[:, rank : rank + KVR]
    inverse_latent = inverse_rms(latent_part)
    unit_latent = latent_part * inverse_latent
    latent_normed = (unit_latent * latent_scale).astype(low)
    key_rotary = rotate(joint[:, rank + KVR :], local_cosine, local_sine).astype(low)
    gap = lambda n: jnp.zeros((rows, n), low)
    latents_own = jnp.concatenate([query_normed, latent_normed, gap(NOPE), key_rotary, gap(LANES - NOPE - ROPE)], axis=1)
    latent_width = latents_own.shape[1]
    latents = by_place([jnp.concatenate(p, axis=0) if isinstance(p, list) else p for p in grouped(gather_line(latents_own))], order, 4).reshape(group, latent_width)

    branch_two_grad = (residual_scale * cotangent.astype(wide)).astype(low)
    branch_two_group = jnp.concatenate(gather_line(after(branch_two_grad, latents)), axis=0)

    block = min(256, group)
    pairs = heads // 2
    whole = lambda *shape: pl.BlockSpec(shape, lambda i: (0,) * len(shape))
    by_pair = lambda r, w: pl.BlockSpec((r, w), lambda i: (0, i))
    attended, queries, expanded, log_total = pl.pallas_call(
        functools.partial(attention_forward_kernel, rank, block),
        grid=(pairs,),
        in_specs=[whole(group, latent_width), by_pair(rank, 2 * LANES), by_pair(KVR, 2 * LANES), whole(group, LANES), whole(group, LANES), whole(group, LANES), whole(group, 1), whole(1, group)],
        out_specs=[by_pair(group, LANES), by_pair(group, 2 * LANES), by_pair(group, 2 * LANES), whole(group, LANES)],
        out_shape=[
            jax.ShapeDtypeStruct((group, heads * VD), low),
            jax.ShapeDtypeStruct((group, heads * LANES), low),
            jax.ShapeDtypeStruct((group, heads * LANES), low),
            jax.ShapeDtypeStruct((group, LANES), wide),
        ],
        compiler_params=pltpu.CompilerParams(vmem_limit_bytes=48 * 2**20),
        cost_estimate=pl.CostEstimate(flops=10 * 10**9, bytes_accessed=15 * 10**6, transcendentals=heads * group * group),
        name="attention_forward",
    )(latents, up_q, up_kv, cosine_wide, sine_left, sine_right, segment_col, segment_row)
    log_rows = log_total[:, :16].T

    parts = attended.reshape(4, rows, heads * VD)
    attended_own = jnp.concatenate(exchange_line([lax.dynamic_index_in_dim(parts, p, 0, keepdims=False) for p in order]), axis=1)
    branch_one = nt(attended_own, out_all)
    middle = hidden_float + residual_scale * branch_one
    inverse_middle = inverse_rms(middle)
    unit_middle = middle * inverse_middle
    feed_in = (unit_middle * feed_scale).astype(low)
    feed_group = jnp.concatenate(gather_line(feed_in), axis=0)
    gate = nn(feed_group, gate_all)
    upper = nn(feed_group, upper_all)
    sigmoid_gate = jax.nn.sigmoid(gate)
    inner = (gate * sigmoid_gate * upper).astype(low)
    inner_grad = nn(branch_two_group, down_all)
    gate_low = (inner_grad * upper * sigmoid_gate * (1.0 + gate * (1.0 - sigmoid_gate))).astype(low)
    upper_low = (inner_grad * gate * sigmoid_gate).astype(low)
    feed_part = (nt(gate_low, gate_all) + nt(upper_low, upper_all)).reshape(4, rows, width)
    feed_in_grad = scatter_line(*feed_part)

    grad_out = cotangent.astype(wide)
    feed_gain_part = jnp.sum(feed_in_grad * unit_middle, axis=0)
    middle_grad = grad_out + norm_back(feed_in_grad, unit_middle, inverse_middle, feed_scale)
    branch_one_grad = (residual_scale * middle_grad).astype(low)
    attended_grad_own = nn(branch_one_grad, out_all).astype(low)
    got = exchange_line([attended_grad_own[:, k * heads * VD : (k + 1) * heads * VD] for k in range(4)])
    attended_grad = by_place(got, order, 4).reshape(group, heads * VD)

    branch_two_part = nt(inner, down_all).reshape(4, rows, width)
    branch_two = scatter_line(*after(branch_two_part, feed_in_grad))
    layer_output = (middle + residual_scale * branch_two).astype(low)
    gate_grad = tn(feed_group, gate_low).astype(low).reshape(replicas, -1, hidden_units)
    upper_grad = tn(feed_group, upper_low).astype(low).reshape(replicas, -1, hidden_units)
    down_grad = tn(branch_two_group, inner).astype(low).reshape(replicas, -1, hidden_units)
    gate_sum = scatter_data(gate_grad)
    upper_sum = scatter_data(upper_grad)
    down_sum = scatter_data(down_grad).T
    out_grad = tn(branch_one_grad, attended_own).astype(low).reshape(replicas, -1, 4 * heads * VD)
    out_part = scatter_data(out_grad)
    output_sum = scatter_line(*[out_part[:, k * heads * VD : (k + 1) * heads * VD] for k in range(4)]).T

    query_grad, expanded_grad, rotary_grad = pl.pallas_call(
        functools.partial(attention_backward_kernel, block),
        grid=(pairs,),
        in_specs=[by_pair(group, 2 * LANES), by_pair(group, 2 * LANES), pl.BlockSpec((group, LANES), lambda i: (0, (rank + KVR) // LANES)), whole(group, LANES), whole(group, LANES), whole(group, LANES), whole(group, 1), whole(1, group), whole(16, group), by_pair(group, LANES)],
        out_specs=[by_pair(group, 2 * LANES), by_pair(group, 2 * LANES), whole(group, LANES)],
        out_shape=[
            jax.ShapeDtypeStruct((group, heads * LANES), low),
            jax.ShapeDtypeStruct((group, heads * LANES), low),
            jax.ShapeDtypeStruct((group, LANES), wide),
        ],
        scratch_shapes=[pltpu.VMEM((group, LANES), wide), pltpu.VMEM((group, LANES), wide)],
        compiler_params=pltpu.CompilerParams(vmem_limit_bytes=48 * 2**20),
        cost_estimate=pl.CostEstimate(flops=20 * 10**9, bytes_accessed=15 * 10**6, transcendentals=heads * group * group),
        name="attention_backward",
    )(queries, expanded, latents, cosine_wide, sine_left, sine_right, segment_col, segment_row, log_rows, attended_grad)

    ups_grad = jnp.concatenate(
        [
            tn(latents[:, :rank], query_grad).astype(low).reshape(replicas, -1, heads * LANES),
            tn(latents[:, rank : rank + KVR], expanded_grad).astype(low).reshape(replicas, -1, heads * LANES),
        ],
        axis=1,
    )
    latents_part = jnp.concatenate([nt(query_grad, up_q).astype(low), nt(expanded_grad, up_kv).astype(low), rotary_grad[:, NOPE : NOPE + ROPE].astype(low)], axis=1).reshape(4, rows, joint_width)
    latents_grad = scatter_line(*[lax.dynamic_index_in_dim(latents_part, p, 0, keepdims=False) for p in order])
    query_normed_grad = latents_grad[:, :rank]
    latent_normed_grad = latents_grad[:, rank : rank + KVR]
    rotary_own = latents_grad[:, rank + KVR :]
    query_norm_part = jnp.sum(query_normed_grad * unit_query, axis=0)
    latent_norm_part = jnp.sum(latent_normed_grad * unit_latent, axis=0)
    joint_grad = jnp.concatenate(
        [
            norm_back(query_normed_grad, unit_query, inverse_query, query_scale),
            norm_back(latent_normed_grad, unit_latent, inverse_latent, latent_scale),
            rotate_back(rotary_own, local_cosine, local_sine),
        ],
        axis=-1,
    ).astype(low)
    downs_grad = tn(normed, joint_grad).astype(low)
    normed_grad = nt(joint_grad, weights_down)
    attention_gain_part = jnp.sum(normed_grad * unit_in, axis=0)
    input_gradient = (middle_grad + norm_back(normed_grad, unit_in, inverse_in, attention_scale)).astype(low)

    part_rows = replicas * 4
    gain_grads = jnp.concatenate([p.reshape(part_rows, -1) for p in (attention_gain_part, feed_gain_part, query_norm_part, latent_norm_part)], axis=1)
    gain_grads = jnp.pad(gain_grads, ((0, 0), (0, joint_width - gain_grads.shape[1]))).astype(low)[:, None]
    downs_grad = jnp.concatenate([downs_grad.reshape(part_rows, slice_rows, joint_width), gain_grads], axis=1)
    downs_grad = jnp.pad(downs_grad, ((0, 0), (0, down_rows - downs_grad.shape[1]), (0, 0))).reshape(replicas, 4 * down_rows, joint_width)
    downs_part = scatter_data(downs_grad).reshape(4, down_rows, joint_width).astype(low)
    mine = [lax.dynamic_index_in_dim(downs_part, p, 0, keepdims=False) for p in order]
    downs_sum = sum(p.astype(wide) for p in exchange_line(mine))
    gain_sum = downs_sum[slice_rows]
    ups_sum = scatter_data(ups_grad)
    query_up_sum = ups_sum[: query_up.shape[0]].reshape(-1, heads, LANES)[..., : NOPE + ROPE].reshape(query_up.shape)
    return (
        layer_output,
        input_gradient,
        gain_sum[:a],
        downs_sum[:slice_rows, :rank],
        gain_sum[b:c],
        downs_sum[:slice_rows, rank:],
        gain_sum[c:d],
        query_up_sum,
        ups_sum[query_up.shape[0] :],
        output_sum,
        gain_sum[a:b],
        gate_sum,
        upper_sum,
        down_sum,
    )


def grouped(found):
    return [*found[:3], list(found[3:])]


def solution(mesh):
    return jax.shard_map(
        local,
        mesh=mesh,
        in_specs=(
            P(("dp", "tensor"), None),
            P(("dp", "tensor")),
            P(("dp", "tensor"), None),
            P(("dp", "tensor")),
            P(("dp", "tensor"), None),
            P(("dp", "tensor")),
            P("dp", "tensor"),
            P("dp", "tensor"),
            P("tensor", "dp"),
            P(("dp", "tensor")),
            P("dp", "tensor"),
            P("dp", "tensor"),
            P("tensor", "dp"),
            P(("dp", "tensor"), None),
            P("dp", None),
        ),
        out_specs=(
            P(("dp", "tensor"), None),
            P(("dp", "tensor"), None),
            P(("dp", "tensor")),
            P(("dp", "tensor"), None),
            P(("dp", "tensor")),
            P(("dp", "tensor"), None),
            P(("dp", "tensor")),
            P("dp", "tensor"),
            P("dp", "tensor"),
            P("tensor", "dp"),
            P(("dp", "tensor")),
            P("dp", "tensor"),
            P("dp", "tensor"),
            P("tensor", "dp"),
        ),
        check_vma=False,
    )
```

```python
import math, functools
import jax, jax.numpy as jnp
from jax import lax
from jax.experimental import pallas as pl
from jax.experimental.pallas import tpu as pltpu
from jax.sharding import PartitionSpec as P

KVR, ROPE, NOPE, VD = 256, 32, 64, 64
LANES = 128
softmax_scale = 1.0 / math.sqrt(NOPE + ROPE)
log2_scale = softmax_scale / math.log(2.0)


def nt(left, right):
    return lax.dot_general(left, right, (((1,), (1,)), ((), ())), preferred_element_type=jnp.float32)


def nn(left, right):
    return lax.dot_general(left, right, (((1,), (0,)), ((), ())), preferred_element_type=jnp.float32)


def tn(left, right):
    return lax.dot_general(left, right, (((0,), (0,)), ((), ())), preferred_element_type=jnp.float32)


def attention_forward_kernel(rank, block, latents, up_q, up_kv, cosine, sine_left, sine_right, segment_col, segment_row, attended, queries, expanded, log_total):
    pair = pl.program_id(0)
    group = latents.shape[0]
    lane = lax.broadcasted_iota(jnp.int32, (1, LANES), 1)
    rotary = latents[:, rank + KVR :].astype(jnp.float32)

    @pl.when(pair == 0)
    def _():
        log_total[...] = jnp.zeros_like(log_total)

    found = []
    for half in range(2):
        columns = slice(half * LANES, (half + 1) * LANES)
        raw = nn(latents[:, :rank], up_q[:, columns])
        turned = raw * cosine[...] + pltpu.roll(raw, LANES - ROPE // 2, 1) * sine_left[...] + pltpu.roll(raw, ROPE // 2, 1) * sine_right[...]
        query = turned.astype(jnp.bfloat16)
        queries[:, columns] = query
        both = nn(latents[:, rank : rank + KVR], up_kv[:, columns])
        key = jnp.where(lane < NOPE, both, rotary).astype(jnp.bfloat16)
        both = both.astype(jnp.bfloat16)
        expanded[:, columns] = both
        outs, sums = [], []
        for begin in range(0, group, block):
            end = begin + block
            scores = nt(query[begin:end], key[:end]) * log2_scale
            allowed = segment_col[begin:end, :] == segment_row[:, :end]
            row = lax.broadcasted_iota(jnp.int32, (block, end), 0) + begin
            column = lax.broadcasted_iota(jnp.int32, (block, end), 1)
            scores = jnp.where(allowed & (column <= row), scores, -1e30)
            peak = jnp.max(scores, axis=-1, keepdims=True)
            weights = jnp.exp2(scores - peak)
            total = jnp.sum(weights, axis=-1, keepdims=True)
            outs.append(nn(weights.astype(jnp.bfloat16), both[:end]) / total)
            sums.append(peak + jnp.log2(total))
        found.append(jnp.concatenate(outs, axis=0))
        log_total[...] = jnp.where(lane == 2 * pair + half, jnp.concatenate(sums, axis=0), log_total[...])
    attended[...] = jnp.where(lane < VD, pltpu.roll(found[0], VD, 1), found[1]).astype(jnp.bfloat16)


def attention_backward_kernel(block, queries, expanded, rotary_in, cosine, sine_left, sine_right, segment_col, segment_row, log_total, grad, query_grad, expanded_grad, rotary_grad, key_sum, value_sum):
    pair = pl.program_id(0)
    group = queries.shape[0]
    lane = lax.broadcasted_iota(jnp.int32, (1, LANES), 1)
    rotary = rotary_in[...].astype(jnp.float32)

    @pl.when(pair == 0)
    def _():
        rotary_grad[...] = jnp.zeros_like(rotary_grad)

    grads = grad[...].astype(jnp.float32)
    for half in range(2):
        columns = slice(half * LANES, (half + 1) * LANES)
        query = queries[:, columns]
        both = expanded[:, columns]
        key = jnp.where(lane < NOPE, both.astype(jnp.float32), rotary).astype(jnp.bfloat16)
        out_grad = pltpu.roll(grads, VD, 1) if half == 0 else grads
        out_grad = jnp.where(lane < NOPE, 0.0, out_grad).astype(jnp.bfloat16)
        log_row = log_total[pl.ds(2 * pair + half, 1), :]
        parts = []
        for begin in reversed(range(0, group, block)):
            end = begin + block
            scores = nt(key[:end], query[begin:end]) * log2_scale
            allowed = segment_col[:end, :] == segment_row[:, begin:end]
            row = lax.broadcasted_iota(jnp.int32, (end, block), 0)
            column = lax.broadcasted_iota(jnp.int32, (end, block), 1) + begin
            probs = jnp.where(allowed & (row <= column), jnp.exp2(scores - log_row[:, begin:end]), 0.0)
            prob_grad = nt(both[:end], out_grad[begin:end])
            center = jnp.sum(probs * prob_grad, axis=0, keepdims=True)
            score_grad = (probs * (prob_grad - center)).astype(jnp.bfloat16)
            key_part = nn(score_grad, query[begin:end])
            value_part = nn(probs.astype(jnp.bfloat16), out_grad[begin:end])
            if end == group:
                key_sum[...] = key_part
                value_sum[...] = value_part
            else:
                key_sum[:end] += key_part
                value_sum[:end] += value_part
            parts.append(tn(score_grad, key[:end]))
        found = jnp.concatenate(parts[::-1], axis=0) * softmax_scale
        back = found * cosine[...] - pltpu.roll(found, LANES - ROPE // 2, 1) * sine_left[...] - pltpu.roll(found, ROPE // 2, 1) * sine_right[...]
        query_grad[:, columns] = back.astype(jnp.bfloat16)
        keys = key_sum[...] * softmax_scale
        expanded_grad[:, columns] = jnp.where(lane < NOPE, keys, value_sum[...]).astype(jnp.bfloat16)
        rotary_grad[...] += jnp.where((lane >= NOPE) & (lane < NOPE + ROPE), keys, 0.0)


epsilon = 1e-05
residual_scale = 1.4 / math.sqrt(62.0)
rotary_base = 10000.0

RIGHT = [(i, (i + 1) % 4) for i in range(4)]
LEFT = [(i, (i - 1) % 4) for i in range(4)]
OPPOSITE = [(i, (i + 2) % 4) for i in range(4)]


def inverse_rms(values):
    return lax.rsqrt(jnp.mean(values * values, axis=-1, keepdims=True) + epsilon)


def norm_back(grad, unit, inverse, gain):
    scaled = grad * gain
    return inverse * (scaled - unit * jnp.mean(scaled * unit, axis=-1, keepdims=True))


def rotate_half(values):
    half = values.shape[-1] // 2
    return jnp.concatenate([-values[..., half:], values[..., :half]], axis=-1)


def rotate(values, cosine, sine):
    return values * cosine + rotate_half(values) * sine


def rotate_back(values, cosine, sine):
    return values * cosine - rotate_half(values) * sine


def rotary_tables(positions, width):
    steps = jnp.arange(width // 2, dtype=jnp.float32) * (2.0 / width)
    freqs = jnp.exp(steps * -math.log(rotary_base))
    angles = positions.astype(jnp.float32)[:, None] * freqs[None, :]
    return jnp.cos(angles), jnp.sin(angles)


def layout(lengths_row, group_tokens):
    slots = jnp.arange(group_tokens, dtype=jnp.int32)
    ends = jnp.cumsum(lengths_row)
    segment = jnp.sum((slots[:, None] >= ends[None, :]).astype(jnp.int32), axis=1)
    starts = jnp.concatenate([jnp.zeros((1,), jnp.int32), ends])
    choose = segment[:, None] == jnp.arange(starts.shape[0], dtype=jnp.int32)[None, :]
    start_of = jnp.sum(jnp.where(choose, starts[None, :], 0), axis=1)
    return (segment, slots - start_of)


low, wide = jnp.bfloat16, jnp.float32
VMEM_LIMIT = 56 * 2**20


COST = 1


def call(kernel, name, flops, moved, **how):
    flops, moved = flops // COST, moved // COST
    return pl.pallas_call(
        kernel,
        name=name,
        compiler_params=pltpu.CompilerParams(vmem_limit_bytes=VMEM_LIMIT),
        cost_estimate=pl.CostEstimate(flops=flops, bytes_accessed=moved, transcendentals=0),
        **how,
    )


def whole(*shape):
    return pl.BlockSpec(shape, lambda *i: (0,) * len(shape))


def shaped(shape, dtype):
    return jax.ShapeDtypeStruct(shape, dtype)


def place(blocks, rows_of, total):
    count, width = len(blocks), blocks[0].shape[1]

    def kernel(*refs):
        ins, out, held, done = refs[:count], refs[count], refs[count + 1 : 2 * count + 1], refs[-1]
        arrive = [pltpu.make_async_copy(ref, slot, done.at[0, k]) for k, (ref, slot) in enumerate(zip(ins, held, strict=True))]
        leave = [
            pltpu.make_async_copy(slot, out.at[pl.ds(pl.multiple_of(row, 16), slot.shape[0])], done.at[1, k])
            for k, (slot, row) in enumerate(zip(held, rows_of(), strict=True))
        ]
        for copy in arrive:
            copy.start()
        for first, second in zip(arrive, leave, strict=True):
            first.wait()
            second.start()
        for copy in leave:
            copy.wait()

    return call(
        kernel,
        "place",
        0,
        4 * total * width,
        in_specs=[pl.BlockSpec(memory_space=pl.ANY)] * count,
        out_specs=pl.BlockSpec(memory_space=pl.ANY),
        out_shape=shaped((total, width), blocks[0].dtype),
        scratch_shapes=[*[pltpu.VMEM(b.shape, b.dtype) for b in blocks], pltpu.SemaphoreType.DMA((2, count))],
    )(*blocks)


def join(target, pieces):
    row = 0
    for piece in pieces:
        target[row : row + piece.shape[0]] = piece[...]
        row += piece.shape[0]


def down_kernel(rank, hidden, weights, chooser, cosine, sine_left, sine_right, joint, latents, gains):
    lane = lax.broadcasted_iota(jnp.int32, (1, LANES), 1)
    rows = weights[:, weights.shape[1] - LANES :].astype(wide).T[ROPE : ROPE + 8]
    gains[...] = rows
    chosen = nn(rows.astype(low), chooser[...])
    gains[2:3, : rank + KVR] = chosen[2:3]
    values = hidden[...].astype(wide)
    unit = values * lax.rsqrt(jnp.mean(values * values, axis=-1, keepdims=True) + epsilon)
    normed = (unit * rows[0:1]).astype(low)
    for begin in range(0, weights.shape[1], 384):
        joint[:, begin : begin + 384] = nn(normed, weights[:, begin : begin + 384])
    for begin, end in ((0, rank), (rank, rank + KVR)):
        part = joint[:, begin:end]
        latents[:, begin:end] = (part * lax.rsqrt(jnp.mean(part * part, axis=-1, keepdims=True) + epsilon) * chosen[2:3, begin:end]).astype(low)
    raw = pltpu.roll(joint[:, rank + KVR :], NOPE, 1)
    turned = raw * cosine[...] + pltpu.roll(raw, LANES - ROPE // 2, 1) * sine_left[...] + pltpu.roll(raw, ROPE // 2, 1) * sine_right[...]
    latents[:, rank + KVR :] = jnp.where((lane >= NOPE) & (lane < NOPE + ROPE), turned, 0.0).astype(low)


def down_projections(hidden, weights, chooser, rank, tables):
    rows, width = hidden.shape
    columns = weights.shape[1]
    operands = (hidden, weights, chooser, *tables)
    return call(
        functools.partial(down_kernel, rank),
        "down_projections",
        2 * rows * width * columns,
        2 * width * columns,
        in_specs=[whole(*value.shape) for value in operands],
        out_specs=[whole(rows, columns), whole(rows, columns), whole(8, width)],
        out_shape=[shaped((rows, columns), wide), shaped((rows, columns), low), shaped((8, width), wide)],
    )(*operands)


def feed_kernel(pieces, places, *refs):
    feeds, grads = refs[:pieces], refs[pieces : 2 * pieces]
    gate_w, upper_w, down_w, inner, gate_grad, upper_grad, feed, grad = refs[2 * pieces :]

    @pl.when(pl.program_id(0) == 0)
    def _():
        join(feed, feeds)
        join(grad, grads)

    for begin in range(0, feed.shape[0], 256):
        rows = slice(begin, begin + 256)
        gate = nn(feed[rows], gate_w[...])
        upper = nn(feed[rows], upper_w[...])
        back = nn(grad[rows], down_w[...])
        sigmoid = jax.nn.sigmoid(gate)
        silu = gate * sigmoid
        inner[rows] = (silu * upper).astype(low)
        gate_grad[rows] = (back * upper * sigmoid * (1.0 + gate * (1.0 - sigmoid))).astype(low)
        upper_grad[rows] = (back * silu).astype(low)


def feed_forward(chunk, places, feeds, grad_all, gate_w, upper_w, down_w):
    tokens = sum(p.shape[0] for p in feeds)
    width, hidden_units = gate_w.shape
    size = 256
    column = lambda r: pl.BlockSpec((r, size), lambda i, order: (0, i))
    fixed = lambda r: pl.BlockSpec((r, width), lambda i, order: (0, 0))
    third, half = feeds[0].shape[0], feeds[3].shape[0]
    near = [pl.BlockSpec((third, width), functools.partial(lambda k, i, order: (order[k] * 2 + chunk, 0), k)) for k in range(3)]
    far = [pl.BlockSpec((half, width), functools.partial(lambda k, i, order: (order[3] * 4 + 2 * chunk + k, 0), k)) for k in range(2)]
    return call(
        functools.partial(feed_kernel, len(feeds)),
        "feed_forward",
        6 * tokens * width * hidden_units,
        6 * width * hidden_units,
        grid_spec=pltpu.PrefetchScalarGridSpec(
            num_scalar_prefetch=1,
            grid=(pl.cdiv(hidden_units, size),),
            in_specs=[*[fixed(p.shape[0]) for p in feeds], *near, *far, column(width), column(width), column(width)],
            out_specs=[column(tokens), column(tokens), column(tokens), fixed(tokens), fixed(tokens)],
        ),
        out_shape=[shaped((tokens, hidden_units), low)] * 3 + [shaped((tokens, width), low)] * 2,
    )(places, *feeds, *[grad_all] * 5, gate_w, upper_w, down_w)


def back_kernel(factors, *refs):
    lefts, weights, outs = refs[:factors], refs[factors : 2 * factors], refs[2 * factors :]
    found = sum(nt(left[...], weight[...]) for left, weight in zip(lefts, weights, strict=True))
    row = 0
    for out in outs:
        out[...] = found[row : row + out.shape[0]].astype(low)
        row += out.shape[0]


def feed_back(name, lefts, weights):
    tokens, hidden_units = lefts[0].shape
    width = weights[0].shape[0]
    size = 256
    quarter = tokens // 4
    cuts = (quarter, quarter, quarter, quarter // 2, quarter // 2)
    return call(
        functools.partial(back_kernel, len(lefts)),
        name,
        2 * len(lefts) * tokens * width * hidden_units,
        2 * len(lefts) * width * hidden_units,
        grid=(width // size,),
        in_specs=[*[whole(*p.shape) for p in lefts], *[pl.BlockSpec((size, hidden_units), lambda i: (i, 0))] * len(weights)],
        out_specs=[pl.BlockSpec((r, size), lambda i: (0, i)) for r in cuts],
        out_shape=[shaped((r, width), low) for r in cuts],
    )(*lefts, *weights)


def weight_kernel(chunks, groups, *refs):
    lefts = refs[:chunks]
    outs = refs[chunks + chunks * groups :]
    for g, out in enumerate(outs):
        rights = refs[chunks + g * chunks : chunks + (g + 1) * chunks]
        out[...] = sum(tn(left[...], right[...]) for left, right in zip(lefts, rights, strict=True)).astype(low)


def weight_gradients(name, lefts, rights):
    chunks, groups = len(lefts), len(rights)
    tokens, width = lefts[0].shape
    columns = rights[0][0].shape[1]
    size = 256
    return call(
        functools.partial(weight_kernel, chunks, groups),
        name,
        2 * groups * chunks * tokens * width * columns,
        2 * (groups * (width + chunks * tokens) * columns + chunks * tokens * width),
        grid=(width // size,),
        in_specs=[*[pl.BlockSpec((tokens, size), lambda i: (0, i))] * chunks, *[whole(tokens, columns)] * (chunks * groups)],
        out_specs=[pl.BlockSpec((size, columns), lambda i: (i, 0))] * groups,
        out_shape=[shaped((width, columns), low)] * groups,
    )(*lefts, *[r for group in rights for r in group])


def latents_kernel(query_grad, expanded_grad, rotary, up_q, up_kv, out):
    rank = up_q.shape[0]
    out[:, :rank] = nt(query_grad[...], up_q[...]).astype(low)
    out[:, rank : rank + KVR] = nt(expanded_grad[...], up_kv[...]).astype(low)
    out[:, rank + KVR :] = rotary[...].astype(low)


def latents_back(query_grad, expanded_grad, rotary, up_q, up_kv):
    group, columns = query_grad.shape
    rank = up_q.shape[0]
    size = 256
    row = lambda w: pl.BlockSpec((size, w), lambda i: (i, 0))
    out_width = rank + KVR + LANES
    return call(
        latents_kernel,
        "latents_back",
        2 * group * columns * (rank + KVR),
        4 * group * columns,
        grid=(group // size,),
        in_specs=[row(columns), row(columns), row(LANES), whole(*up_q.shape), whole(*up_kv.shape)],
        out_specs=row(out_width),
        out_shape=shaped((group, out_width), low),
    )(query_grad, expanded_grad, rotary, up_q, up_kv)


def input_kernel(steps, joint_grad, weights, hidden, gain, feed_row, mixed_row, middle_grad, downs_grad, input_gradient, total):
    step = pl.program_id(0)
    size = weights.shape[0]
    lanes = pl.ds(pl.multiple_of(step * size, size), size)
    values = hidden[...].astype(wide)
    inverse = lax.rsqrt(jnp.mean(values * values, axis=-1, keepdims=True) + epsilon)
    unit = hidden[:, lanes].astype(wide) * inverse
    normed = (unit * gain[:, lanes]).astype(low)
    back = nt(joint_grad[...], weights[...])
    total[:, lanes] = back
    found = tn(normed, joint_grad[...])
    gain_row = jnp.sum(back * unit, axis=0, keepdims=True)
    gap = lambda n: jnp.zeros((n, size), wide)
    rows = jnp.concatenate([gap(ROPE), gain_row, feed_row[:, lanes], mixed_row[:, lanes], gap(LANES - ROPE - 3)], axis=0)
    columns = found.shape[1]
    downs_grad[:, : columns - LANES] = found[:, : columns - LANES].astype(low)
    downs_grad[:, columns - LANES :] = (found[:, columns - LANES :] + rows.T).astype(low)

    @pl.when(step == steps - 1)
    def _():
        whole_unit = values * inverse
        input_gradient[...] = (middle_grad[...] + norm_back(total[...], whole_unit, inverse, gain[...])).astype(low)


def input_back(joint_grad, weights, hidden, gain, feed_row, mixed_row, middle_grad):
    rows, width = hidden.shape
    columns = weights.shape[1]
    size = 256
    steps = width // size
    return call(
        functools.partial(input_kernel, steps),
        "input_back",
        4 * rows * width * columns,
        4 * width * columns,
        grid=(steps,),
        in_specs=[whole(rows, columns), pl.BlockSpec((size, columns), lambda i: (i, 0)), whole(rows, width), *[whole(1, width)] * 3, whole(rows, width)],
        out_specs=[pl.BlockSpec((size, columns), lambda i: (i, 0)), whole(rows, width)],
        out_shape=[shaped((width, columns), low), shaped((rows, width), low)],
        scratch_shapes=[pltpu.VMEM((rows, width), wide)],
    )(joint_grad, weights, hidden, gain, feed_row, mixed_row, middle_grad)


def after(value, *earlier):
    return lax.optimization_barrier((value, *earlier))[0]


def after_all(values, *earlier):
    return list(lax.optimization_barrier((tuple(values), earlier))[0])


def gather_near(block):
    return [block, lax.ppermute(block, "tensor", RIGHT), lax.ppermute(block, "tensor", LEFT)]


def gather_far(near):
    half = near[0].shape[0] // 2
    return [lax.ppermute(near[1][:half], "tensor", RIGHT), lax.ppermute(near[2][half:], "tensor", LEFT)]


def scatter_first(own, to_left, to_right, far_first, far_second):
    half = own.shape[0] // 2
    first = lax.ppermute(far_first, "tensor", LEFT)
    second = lax.ppermute(far_second, "tensor", RIGHT)
    return [jnp.concatenate([to_left[:half] + first, to_left[half:]]), jnp.concatenate([to_right[:half], to_right[half:] + second])]


def scatter_second(sent):
    return [lax.ppermute(sent[0], "tensor", LEFT), lax.ppermute(sent[1], "tensor", RIGHT)]


def add_up(*terms):
    return sum(term.astype(wide) for term in terms)


def exchange_line(blocks):
    own, to_left, to_right, far = blocks
    return [own, lax.ppermute(to_right, "tensor", RIGHT), lax.ppermute(to_left, "tensor", LEFT), lax.ppermute(far, "tensor", OPPOSITE)]


def line_order():
    here = lax.axis_index("tensor")
    return [here, (here + 3) % 4, (here + 1) % 4, (here + 2) % 4]


def flips(bit):
    return [(i, i ^ bit) for i in range(8)]


def cube_near(block):
    return [block, lax.ppermute(block, "dp", flips(2)), lax.ppermute(block, "dp", flips(4))]


def cube_far(near):
    half = near[0].shape[0] // 2
    return [lax.ppermute(near[1][:half], "dp", flips(4)), lax.ppermute(near[2][half:], "dp", flips(2))]


def cube_place(mine):
    rows = mine[0].shape[0]
    other = [lax.ppermute(value, "dp", flips(1)) for value in mine]

    def rows_of():
        here = lax.axis_index("dp")
        places = [here, here ^ 2, here ^ 4, here ^ 6]
        first = [p * rows for p in (*places, places[3])]
        second = [(p ^ 1) * rows for p in (*places, places[3])]
        first[4] += rows // 2
        second[4] += rows // 2
        return first + second

    return place(mine + other, rows_of, 8 * rows)


def scatter_core(blocks):
    count, rows, columns = blocks.shape
    if count != 8:
        return [blocks]
    core = lax.axis_index("dp") % 2
    other = lax.dynamic_index_in_dim(blocks.reshape(4, 2, rows, columns), 1 - core, 1, keepdims=False)
    return [blocks, lax.ppermute(other, "dp", flips(1))]


def scatter_pair(halves, place):
    here = lax.axis_index("dp")
    pick = lambda array, at: lax.dynamic_index_in_dim(array, at, 0, keepdims=False)
    return add_up(pick(halves[0], here ^ (2 * place)), pick(halves[1], (here // 2) ^ place))


def scatter_corner(halves):
    if len(halves) == 1:
        return halves
    half = halves[0].shape[1] // 2
    corner = scatter_pair(halves, 3).astype(low)
    return [lax.ppermute(corner[:half], "dp", flips(2)), lax.ppermute(corner[half:], "dp", flips(4))]


def scatter_rest(halves, corners):
    if len(halves) == 1:
        count, rows, columns = halves[0].shape
        return lax.psum_scatter(corners[0].reshape(count * rows, columns), "dp", scatter_dimension=0, tiled=True).astype(wide)
    half = halves[0].shape[1] // 2
    across, along = scatter_pair(halves, 1), scatter_pair(halves, 2)
    across = jnp.concatenate([across[:half], across[half:] + corners[1]]).astype(low)
    along = jnp.concatenate([along[:half] + corners[0], along[half:]]).astype(low)
    return add_up(scatter_pair(halves, 0), lax.ppermute(across, "dp", flips(2)), lax.ppermute(along, "dp", flips(4)))


def local(hidden_in, attention_gain, query_down, query_norm, latent_down, latent_norm, query_up, latent_up, output_weight, feed_gain, gate_weight, up_weight, down_weight, cotangent, document_lengths):
    replicas = lax.axis_size("dp")
    rows, width = hidden_in.shape
    group = rows * 4
    rank = query_down.shape[1]
    heads = query_up.shape[1] // (NOPE + ROPE)
    slice_rows = query_down.shape[0]
    order = line_order()
    joint_width = rank + KVR + LANES
    by_line = lambda array: [lax.dynamic_index_in_dim(array, p, 0, keepdims=False) for p in order]

    def column(value):
        return jnp.pad(value, (0, slice_rows - value.shape[0]))[:, None]

    norms = jnp.concatenate([query_norm, latent_norm])
    downs = jnp.concatenate([query_down, latent_down, column(attention_gain), column(feed_gain), column(norms)], axis=1)
    downs = jnp.pad(downs, ((0, 0), (0, joint_width - downs.shape[1])))
    if replicas == 8:
        downs = place(exchange_line([downs] * 4), lambda: [p * slice_rows for p in line_order()], 4 * slice_rows)
    out_near = gather_near(after(output_weight.T, downs))

    query_up_wide = jnp.pad(query_up.reshape(-1, heads, NOPE + ROPE), ((0, 0), (0, 0), (0, LANES - NOPE - ROPE))).reshape(-1, heads * LANES)
    ups_all = lax.all_gather(jnp.concatenate([query_up_wide, latent_up], axis=0), "dp", axis=0)
    up_q = ups_all[:, : query_up.shape[0]].reshape(rank, heads * LANES)
    up_kv = ups_all[:, query_up.shape[0] :].reshape(KVR, heads * LANES)
    gate_all = lax.all_gather(after(gate_weight, downs), "dp", axis=0, tiled=True)
    upper_all = lax.all_gather(after(up_weight, downs), "dp", axis=0, tiled=True)
    down_all = lax.all_gather(after(down_weight.T, downs), "dp", axis=0, tiled=True)

    parts = [slice(k * rows // 2, (k + 1) * rows // 2) for k in range(2)]
    branch_two_grad = (residual_scale * cotangent.astype(wide)).astype(low)
    grad_all = lax.all_gather(branch_two_grad, "tensor", axis=0, tiled=True)

    segment, position = layout(document_lengths[0], group)
    cosine_half, sine_half = rotary_tables(position, ROPE)
    zeros = lambda n: jnp.zeros((group, n), wide)
    cosine_wide = jnp.concatenate([jnp.ones((group, NOPE), wide), cosine_half, cosine_half, zeros(ROPE)], axis=1)
    sine_left = jnp.concatenate([zeros(NOPE), -sine_half, zeros(ROPE // 2 + ROPE)], axis=1)
    sine_right = jnp.concatenate([zeros(NOPE + ROPE // 2), sine_half, zeros(ROPE)], axis=1)
    segment_col, segment_row = segment[:, None], segment[None, :]
    first_row = lax.axis_index("tensor") * rows
    local_tables = [lax.dynamic_slice_in_dim(t, first_row, rows, 0) for t in (cosine_wide, sine_left, sine_right)]
    local_cosine = local_tables[0][:, NOPE : NOPE + ROPE]
    local_sine = local_tables[2][:, NOPE + ROPE // 2 : NOPE + ROPE]
    local_sine = jnp.concatenate([local_sine, local_sine], axis=-1)

    a, b = query_norm.shape[0], norms.shape[0]
    lanes = jnp.arange(rank + KVR)
    source = jnp.where(lanes < rank, lanes // a * slice_rows + lanes % a, (lanes - rank) // (b - a) * slice_rows + a + (lanes - rank) % (b - a))
    chooser = (jnp.arange(width)[:, None] == source[None, :]).astype(low)
    ready = (chooser, cosine_wide, sine_left, sine_right, segment_col, *local_tables)
    if replicas == 8:
        near = cube_near(downs)
        weights_down = cube_place(after_all(near + cube_far(near), *ready, *out_near[1:]))
    else:
        weights_down = lax.all_gather(downs, ("dp", "tensor"), axis=0, tiled=True)
    joint, latents_own, gains = down_projections(hidden_in, weights_down, chooser, rank, local_tables)
    attention_scale, feed_scale = gains[0:1], gains[1:2]
    query_scale, latent_scale = gains[2:3, :rank], gains[2:3, rank : rank + KVR]
    out_near = after_all(out_near, weights_down)
    out_block = jnp.concatenate([*out_near, jnp.concatenate(gather_far(out_near), axis=0)], axis=1)
    if replicas == 8:
        out_blocks = cube_near(out_block)
        out_soon = out_blocks[1:]
    else:
        out_all = lax.all_gather(out_block, "dp", axis=0, tiled=True)
        out_soon = [out_all]

    latents_near = gather_near(latents_own)
    latents_near = after_all(latents_near, up_q, up_kv)
    latents_far = gather_far(latents_near)

    def latent_rows():
        here = line_order()
        return [here[0] * rows, here[1] * rows, here[2] * rows, here[3] * rows, here[3] * rows + rows // 2]

    latents = place(after_all(latents_near + latents_far, *out_soon), latent_rows, group)
    if replicas == 8:
        out_blocks = after_all(out_blocks, *latents_far)
        out_all = cube_place(out_blocks + cube_far(out_blocks))

    block = min(256, group)
    pairs = heads // 2
    by_pair = lambda r, w: pl.BlockSpec((r, w), lambda i: (0, i))
    attended, queries, expanded, log_total = call(
        functools.partial(attention_forward_kernel, rank, block),
        "attention_forward",
        20 * 10**9,
        15 * 10**6,
        grid=(pairs,),
        in_specs=[whole(group, joint_width), by_pair(rank, 2 * LANES), by_pair(KVR, 2 * LANES), whole(group, LANES), whole(group, LANES), whole(group, LANES), whole(group, 1), whole(1, group)],
        out_specs=[by_pair(group, LANES), by_pair(group, 2 * LANES), by_pair(group, 2 * LANES), whole(group, LANES)],
        out_shape=[shaped((group, heads * VD), low), shaped((group, heads * LANES), low), shaped((group, heads * LANES), low), shaped((group, LANES), wide)],
    )(latents, up_q, up_kv, cosine_wide, sine_left, sine_right, segment_col, segment_row)
    log_rows = log_total[:, :16].T

    attended_parts = exchange_line(by_line(attended.reshape(4, rows, heads * VD)))
    attended_own = jnp.concatenate(attended_parts, axis=1)
    middle = hidden_in.astype(wide) + residual_scale * nt(attended_own, out_all)
    inverse_middle = inverse_rms(middle)
    unit_middle = middle * inverse_middle
    feed_in = (unit_middle * feed_scale).astype(low)

    near_0 = gather_near(feed_in[parts[0]])
    far_0 = gather_far(near_0)
    near_1 = gather_near(after(feed_in[parts[1]], *far_0))
    places = jnp.stack(order).astype(jnp.int32)
    inner_0, gate_0, upper_0, feed_0, grad_0 = feed_forward(0, places, near_0 + far_0, grad_all, gate_all, upper_all, down_all)
    gate_0, upper_0 = after_all([gate_0, upper_0], *near_1)
    far_1 = gather_far(near_1)
    blocks_0 = feed_back("feed_back", [gate_0, upper_0], [gate_all, upper_all])
    sent_0 = scatter_first(*blocks_0)
    inner_1, gate_1, upper_1, feed_1, grad_1 = feed_forward(1, places, after_all(near_1 + far_1, blocks_0[0]), grad_all, gate_all, upper_all, down_all)
    gate_1, upper_1 = after_all([gate_1, upper_1], *sent_0)
    got_0 = scatter_second(sent_0)
    blocks_1 = feed_back("feed_back", [gate_1, upper_1], [gate_all, upper_all])
    sent_1 = scatter_first(*blocks_1)
    (down_grad,) = weight_gradients("down_gradient", after_all([grad_0, grad_1], blocks_1[0]), [[inner_0, inner_1]])
    feeds = after_all([feed_0, feed_1], down_grad, *sent_1, *got_0)
    got_1 = scatter_second(sent_1)
    gate_grad, upper_grad = weight_gradients("gate_gradient", feeds, [[gate_0, gate_1], [upper_0, upper_1]])
    down_sum = lax.psum_scatter(down_grad, "dp", scatter_dimension=0, tiled=True).astype(wide).T
    gate_sum = lax.psum_scatter(gate_grad, "dp", scatter_dimension=0, tiled=True).astype(wide)
    upper_sum = lax.psum_scatter(upper_grad, "dp", scatter_dimension=0, tiled=True).astype(wide)
    got_1 = after_all(got_1, gate_grad)
    feed_in_grad = jnp.concatenate([add_up(blocks_0[0], *got_0), add_up(blocks_1[0], *got_1)])

    feed_gain_part = jnp.sum(feed_in_grad * unit_middle, axis=0, keepdims=True)
    middle_grad = cotangent.astype(wide) + norm_back(feed_in_grad, unit_middle, inverse_middle, feed_scale)
    branch_one_grad = (residual_scale * middle_grad).astype(low)
    attended_grad_own = nn(branch_one_grad, out_all).astype(low)
    attended_grads = [attended_grad_own[:, k * heads * VD : (k + 1) * heads * VD] for k in range(4)]
    attended_grad = place(exchange_line(attended_grads), lambda: [p * rows for p in line_order()], group)

    late_0, late_1 = after_all([inner_0, inner_1], attended_grad_own)
    outs_0 = feed_back("branch_two", [late_0], [down_all])
    out_grad = tn(after(branch_one_grad, outs_0[0]), attended_own).astype(low)
    outs_1 = feed_back("branch_two", [after(late_1, out_grad)], [down_all])
    out_core = scatter_core(out_grad.reshape(replicas, -1, 4 * heads * VD))
    attended_grad = after(attended_grad, outs_1[0], *out_core)
    out_corner = scatter_corner(out_core)

    query_grad, expanded_grad, rotary_grad = call(
        functools.partial(attention_backward_kernel, block),
        "attention_backward",
        30 * 10**9,
        15 * 10**6,
        grid=(pairs,),
        in_specs=[by_pair(group, 2 * LANES), by_pair(group, 2 * LANES), pl.BlockSpec((group, LANES), lambda i: (0, (rank + KVR) // LANES)), whole(group, LANES), whole(group, LANES), whole(group, LANES), whole(group, 1), whole(1, group), whole(16, group), by_pair(group, LANES)],
        out_specs=[by_pair(group, 2 * LANES), by_pair(group, 2 * LANES), whole(group, LANES)],
        out_shape=[shaped((group, heads * LANES), low), shaped((group, heads * LANES), low), shaped((group, LANES), wide)],
        scratch_shapes=[pltpu.VMEM((group, LANES), wide), pltpu.VMEM((group, LANES), wide)],
    )(queries, expanded, latents, cosine_wide, sine_left, sine_right, segment_col, segment_row, log_rows, attended_grad)

    latents_part = latents_back(*after_all([query_grad, expanded_grad, rotary_grad], *out_corner, down_sum), up_q, up_kv).reshape(4, rows, joint_width)
    cut = by_line(latents_part)
    sent = scatter_first(*cut[:3], cut[3][: rows // 2], cut[3][rows // 2 :])

    out_part = scatter_rest(after_all(out_core, latents_part), out_corner).astype(low)
    (query_up_grad,) = weight_gradients("query_up_gradient", [latents[:, :rank]], [[query_grad]])
    (latent_up_grad,) = weight_gradients("latent_up_gradient", [latents[:, rank : rank + KVR]], [[expanded_grad]])
    ups_grad = jnp.concatenate([query_up_grad.reshape(replicas, -1, heads * LANES), latent_up_grad.reshape(replicas, -1, heads * LANES)], axis=1)
    ups_core = scatter_core(ups_grad)
    ups_sum = scatter_rest(ups_core, scatter_corner(ups_core))
    latents_grad = add_up(cut[0], *scatter_second(sent))
    def branch_rows():
        here, half, quarter = line_order(), rows // 2, rows // 4
        return [p * rows + chunk * half for chunk in range(2) for p in here[:3]] + [here[3] * rows + k * quarter for k in range(4)]

    outs = place(after_all([*outs_0[:3], *outs_1[:3], *outs_0[3:], *outs_1[3:]], latents_grad), branch_rows, group)
    branch_two = lax.psum_scatter(outs, "tensor", scatter_dimension=0, tiled=True)
    layer_output = (middle + residual_scale * branch_two.astype(wide)).astype(low)
    query_latent = joint[:, :rank]
    inverse_query = inverse_rms(query_latent)
    unit_query = query_latent * inverse_query
    latent_part = joint[:, rank : rank + KVR]
    inverse_latent = inverse_rms(latent_part)
    unit_latent = latent_part * inverse_latent
    query_normed_grad = latents_grad[:, :rank]
    latent_normed_grad = latents_grad[:, rank : rank + KVR]
    rotary_own = latents_grad[:, rank + KVR + NOPE : rank + KVR + NOPE + ROPE]
    query_norm_part = jnp.sum(query_normed_grad * unit_query, axis=0)
    latent_norm_part = jnp.sum(latent_normed_grad * unit_latent, axis=0)
    joint_grad = jnp.concatenate(
        [
            norm_back(query_normed_grad, unit_query, inverse_query, query_scale),
            norm_back(latent_normed_grad, unit_latent, inverse_latent, latent_scale),
            rotate_back(rotary_own, local_cosine, local_sine),
            jnp.zeros((rows, LANES - ROPE), wide),
        ],
        axis=-1,
    ).astype(low)
    part_rows = replicas * 4
    mixed_part = jnp.concatenate([query_norm_part.reshape(part_rows, -1), latent_norm_part.reshape(part_rows, -1)], axis=1)
    mixed_part = jnp.pad(mixed_part, ((0, 0), (0, slice_rows - mixed_part.shape[1]))).reshape(1, width)
    joint_grad = after(joint_grad, ups_sum, out_part, gate_sum)
    downs_grad, input_gradient = input_back(joint_grad, weights_down, hidden_in, attention_scale, feed_gain_part, mixed_part, middle_grad)
    if replicas == 8:
        downs_core = scatter_core(downs_grad.reshape(replicas, 4 * slice_rows, joint_width))
        downs_part = scatter_rest(downs_core, scatter_corner(downs_core)).astype(low).reshape(4, slice_rows, joint_width)
        downs_sum = sum(p.astype(wide) for p in exchange_line(by_line(downs_part)))
    else:
        downs_sum = lax.psum_scatter(downs_grad, ("dp", "tensor"), scatter_dimension=0, tiled=True).astype(wide)
    gain_sums = downs_sum[:, rank + KVR + ROPE : rank + KVR + ROPE + 3].T

    pieces = [out_part[:, k * heads * VD : (k + 1) * heads * VD] for k in range(4)]
    half = pieces[3].shape[0] // 2
    output_sum = add_up(pieces[0], *scatter_second(scatter_first(*pieces[:3], pieces[3][:half], pieces[3][half:]))).T
    query_up_sum = ups_sum[: query_up.shape[0]].reshape(-1, heads, LANES)[..., : NOPE + ROPE].reshape(query_up.shape)
    return (
        layer_output,
        input_gradient,
        gain_sums[0],
        downs_sum[:, :rank],
        gain_sums[2, :a],
        downs_sum[:, rank : rank + KVR + ROPE],
        gain_sums[2, a:b],
        query_up_sum,
        ups_sum[query_up.shape[0] :],
        output_sum,
        gain_sums[1],
        gate_sum,
        upper_sum,
        down_sum,
    )


def solution(mesh):
    return jax.shard_map(
        local,
        mesh=mesh,
        in_specs=(
            P(("dp", "tensor"), None),
            P(("dp", "tensor")),
            P(("dp", "tensor"), None),
            P(("dp", "tensor")),
            P(("dp", "tensor"), None),
            P(("dp", "tensor")),
            P("dp", "tensor"),
            P("dp", "tensor"),
            P("tensor", "dp"),
            P(("dp", "tensor")),
            P("dp", "tensor"),
            P("dp", "tensor"),
            P("tensor", "dp"),
            P(("dp", "tensor"), None),
            P("dp", None),
        ),
        out_specs=(
            P(("dp", "tensor"), None),
            P(("dp", "tensor"), None),
            P(("dp", "tensor")),
            P(("dp", "tensor"), None),
            P(("dp", "tensor")),
            P(("dp", "tensor"), None),
            P(("dp", "tensor")),
            P("dp", "tensor"),
            P("dp", "tensor"),
            P("tensor", "dp"),
            P(("dp", "tensor")),
            P("dp", "tensor"),
            P("dp", "tensor"),
            P("tensor", "dp"),
        ),
        check_vma=False,
    )
```

```python
import math, functools
import jax, jax.numpy as jnp
from jax import lax
from jax.experimental import pallas as pl
from jax.experimental.pallas import tpu as pltpu
from jax.sharding import PartitionSpec as P

KVR, ROPE, NOPE, VD = 256, 32, 64, 64
LANES = 128
softmax_scale = 1.0 / math.sqrt(NOPE + ROPE)
log2_scale = softmax_scale / math.log(2.0)


def nt(left, right):
    return lax.dot_general(left, right, (((1,), (1,)), ((), ())), preferred_element_type=jnp.float32)


def nn(left, right):
    return lax.dot_general(left, right, (((1,), (0,)), ((), ())), preferred_element_type=jnp.float32)


def tn(left, right):
    return lax.dot_general(left, right, (((0,), (0,)), ((), ())), preferred_element_type=jnp.float32)


def attention_forward_kernel(rank, block, latents, up_q, up_kv, cosine, sine_left, sine_right, segment_col, segment_row, attended, queries, expanded, log_total):
    pair = pl.program_id(0)
    group = latents.shape[0]
    lane = lax.broadcasted_iota(jnp.int32, (1, LANES), 1)
    rotary = latents[:, rank + KVR :].astype(jnp.float32)

    @pl.when(pair == 0)
    def _():
        log_total[...] = jnp.zeros_like(log_total)

    found = []
    for half in range(2):
        columns = slice(half * LANES, (half + 1) * LANES)
        raw = nn(latents[:, :rank], up_q[:, columns])
        turned = raw * cosine[...] + pltpu.roll(raw, LANES - ROPE // 2, 1) * sine_left[...] + pltpu.roll(raw, ROPE // 2, 1) * sine_right[...]
        query = turned.astype(jnp.bfloat16)
        queries[:, columns] = query
        both = nn(latents[:, rank : rank + KVR], up_kv[:, columns])
        key = jnp.where(lane < NOPE, both, rotary).astype(jnp.bfloat16)
        both = both.astype(jnp.bfloat16)
        expanded[:, columns] = both
        outs, sums = [], []
        for begin in range(0, group, block):
            end = begin + block
            scores = nt(query[begin:end], key[:end]) * log2_scale
            allowed = segment_col[begin:end, :] == segment_row[:, :end]
            row = lax.broadcasted_iota(jnp.int32, (block, end), 0) + begin
            column = lax.broadcasted_iota(jnp.int32, (block, end), 1)
            scores = jnp.where(allowed & (column <= row), scores, -1e30)
            peak = jnp.max(scores, axis=-1, keepdims=True)
            weights = jnp.exp2(scores - peak)
            total = jnp.sum(weights, axis=-1, keepdims=True)
            outs.append(nn(weights.astype(jnp.bfloat16), both[:end]) / total)
            sums.append(peak + jnp.log2(total))
        found.append(jnp.concatenate(outs, axis=0))
        log_total[...] = jnp.where(lane == 2 * pair + half, jnp.concatenate(sums, axis=0), log_total[...])
    attended[...] = jnp.where(lane < VD, pltpu.roll(found[0], VD, 1), found[1]).astype(jnp.bfloat16)


def attention_backward_kernel(block, queries, expanded, rotary_in, cosine, sine_left, sine_right, segment_col, segment_row, log_total, grad, query_grad, expanded_grad, rotary_grad, key_sum, value_sum):
    pair = pl.program_id(0)
    group = queries.shape[0]
    lane = lax.broadcasted_iota(jnp.int32, (1, LANES), 1)
    rotary = rotary_in[...].astype(jnp.float32)

    @pl.when(pair == 0)
    def _():
        rotary_grad[...] = jnp.zeros_like(rotary_grad)

    grads = grad[...].astype(jnp.float32)
    for half in range(2):
        columns = slice(half * LANES, (half + 1) * LANES)
        query = queries[:, columns]
        both = expanded[:, columns]
        key = jnp.where(lane < NOPE, both.astype(jnp.float32), rotary).astype(jnp.bfloat16)
        out_grad = pltpu.roll(grads, VD, 1) if half == 0 else grads
        out_grad = jnp.where(lane < NOPE, 0.0, out_grad).astype(jnp.bfloat16)
        log_row = log_total[pl.ds(2 * pair + half, 1), :]
        parts = []
        for begin in reversed(range(0, group, block)):
            end = begin + block
            scores = nt(key[:end], query[begin:end]) * log2_scale
            allowed = segment_col[:end, :] == segment_row[:, begin:end]
            row = lax.broadcasted_iota(jnp.int32, (end, block), 0)
            column = lax.broadcasted_iota(jnp.int32, (end, block), 1) + begin
            probs = jnp.where(allowed & (row <= column), jnp.exp2(scores - log_row[:, begin:end]), 0.0)
            prob_grad = nt(both[:end], out_grad[begin:end])
            center = jnp.sum(probs * prob_grad, axis=0, keepdims=True)
            score_grad = (probs * (prob_grad - center)).astype(jnp.bfloat16)
            key_part = nn(score_grad, query[begin:end])
            value_part = nn(probs.astype(jnp.bfloat16), out_grad[begin:end])
            if end == group:
                key_sum[...] = key_part
                value_sum[...] = value_part
            else:
                key_sum[:end] += key_part
                value_sum[:end] += value_part
            parts.append(tn(score_grad, key[:end]))
        found = jnp.concatenate(parts[::-1], axis=0) * softmax_scale
        back = found * cosine[...] - pltpu.roll(found, LANES - ROPE // 2, 1) * sine_left[...] - pltpu.roll(found, ROPE // 2, 1) * sine_right[...]
        query_grad[:, columns] = back.astype(jnp.bfloat16)
        keys = key_sum[...] * softmax_scale
        expanded_grad[:, columns] = jnp.where(lane < NOPE, keys, value_sum[...]).astype(jnp.bfloat16)
        rotary_grad[...] += jnp.where((lane >= NOPE) & (lane < NOPE + ROPE), keys, 0.0)


epsilon = 1e-05
residual_scale = 1.4 / math.sqrt(62.0)
rotary_base = 10000.0

RIGHT = [(i, (i + 1) % 4) for i in range(4)]
LEFT = [(i, (i - 1) % 4) for i in range(4)]
OPPOSITE = [(i, (i + 2) % 4) for i in range(4)]


def inverse_rms(values):
    return lax.rsqrt(jnp.mean(values * values, axis=-1, keepdims=True) + epsilon)


def norm_back(grad, unit, inverse, gain):
    scaled = grad * gain
    return inverse * (scaled - unit * jnp.mean(scaled * unit, axis=-1, keepdims=True))


def rotary_tables(positions, width):
    steps = jnp.arange(width // 2, dtype=jnp.float32) * (2.0 / width)
    freqs = jnp.exp(steps * -math.log(rotary_base))
    angles = positions.astype(jnp.float32)[:, None] * freqs[None, :]
    return jnp.cos(angles), jnp.sin(angles)


def layout(lengths_row, group_tokens):
    slots = jnp.arange(group_tokens, dtype=jnp.int32)
    ends = jnp.cumsum(lengths_row)
    segment = jnp.sum((slots[:, None] >= ends[None, :]).astype(jnp.int32), axis=1)
    starts = jnp.concatenate([jnp.zeros((1,), jnp.int32), ends])
    choose = segment[:, None] == jnp.arange(starts.shape[0], dtype=jnp.int32)[None, :]
    start_of = jnp.sum(jnp.where(choose, starts[None, :], 0), axis=1)
    return (segment, slots - start_of)


low, wide = jnp.bfloat16, jnp.float32
VMEM_LIMIT = 56 * 2**20


def call(kernel, name, flops, moved, **how):
    return pl.pallas_call(
        kernel,
        name=name,
        compiler_params=pltpu.CompilerParams(vmem_limit_bytes=VMEM_LIMIT),
        cost_estimate=pl.CostEstimate(flops=flops, bytes_accessed=moved, transcendentals=0),
        **how,
    )


def whole(*shape):
    return pl.BlockSpec(shape, lambda *i: (0,) * len(shape))


def shaped(shape, dtype):
    return jax.ShapeDtypeStruct(shape, dtype)


def place(blocks, rows_of, total):
    count, width = len(blocks), blocks[0].shape[1]

    def kernel(*refs):
        ins, out, held, done = refs[:count], refs[count], refs[count + 1 : 2 * count + 1], refs[-1]
        arrive = [pltpu.make_async_copy(ref, slot, done.at[0, k]) for k, (ref, slot) in enumerate(zip(ins, held, strict=True))]
        leave = [
            pltpu.make_async_copy(slot, out.at[pl.ds(pl.multiple_of(row, 16), slot.shape[0])], done.at[1, k])
            for k, (slot, row) in enumerate(zip(held, rows_of(), strict=True))
        ]
        for copy in arrive:
            copy.start()
        for first, second in zip(arrive, leave, strict=True):
            first.wait()
            second.start()
        for copy in leave:
            copy.wait()

    return call(
        kernel,
        "place",
        0,
        4 * total * width,
        in_specs=[pl.BlockSpec(memory_space=pl.ANY)] * count,
        out_specs=pl.BlockSpec(memory_space=pl.ANY),
        out_shape=shaped((total, width), blocks[0].dtype),
        scratch_shapes=[*[pltpu.VMEM(b.shape, b.dtype) for b in blocks], pltpu.SemaphoreType.DMA((2, count))],
    )(*blocks)


def join(target, pieces):
    row = 0
    for piece in pieces:
        target[row : row + piece.shape[0]] = piece[...]
        row += piece.shape[0]


def down_kernel(rank, places, hidden, *refs):
    pieces, (chooser, cosine, sine_left, sine_right, weights, joint, latents, gains) = refs[:-8], refs[-8:]
    for k, piece in enumerate(pieces):
        weights[pl.ds(pl.multiple_of(places[k], 16), piece.shape[0])] = piece[...]
    lane = lax.broadcasted_iota(jnp.int32, (1, LANES), 1)
    rows = weights[:, weights.shape[1] - LANES :].astype(wide).T[ROPE : ROPE + 8]
    gains[...] = rows
    chosen = nn(rows.astype(low), chooser[...])
    gains[2:3, : rank + KVR] = chosen[2:3]
    values = hidden[...].astype(wide)
    unit = values * lax.rsqrt(jnp.mean(values * values, axis=-1, keepdims=True) + epsilon)
    normed = (unit * rows[0:1]).astype(low)
    for begin in range(0, weights.shape[1], 384):
        joint[:, begin : begin + 384] = nn(normed, weights[:, begin : begin + 384])
    for begin, end in ((0, rank), (rank, rank + KVR)):
        part = joint[:, begin:end]
        latents[:, begin:end] = (part * lax.rsqrt(jnp.mean(part * part, axis=-1, keepdims=True) + epsilon) * chosen[2:3, begin:end]).astype(low)
    raw = pltpu.roll(joint[:, rank + KVR :], NOPE, 1)
    turned = raw * cosine[...] + pltpu.roll(raw, LANES - ROPE // 2, 1) * sine_left[...] + pltpu.roll(raw, ROPE // 2, 1) * sine_right[...]
    latents[:, rank + KVR :] = jnp.where((lane >= NOPE) & (lane < NOPE + ROPE), turned, 0.0).astype(low)


def down_projections(hidden, pieces, places, chooser, rank, tables):
    rows, width = hidden.shape
    columns = pieces[0].shape[1]
    operands = (hidden, *pieces, chooser, *tables)
    return call(
        functools.partial(down_kernel, rank),
        "down_projections",
        2 * rows * width * columns,
        2 * width * columns,
        grid_spec=pltpu.PrefetchScalarGridSpec(
            num_scalar_prefetch=1,
            grid=(1,),
            in_specs=[whole(*value.shape) for value in operands],
            out_specs=[whole(width, columns), whole(rows, columns), whole(rows, columns), whole(8, width)],
        ),
        out_shape=[shaped((width, columns), low), shaped((rows, columns), wide), shaped((rows, columns), low), shaped((8, width), wide)],
    )(places, *operands)


def feed_kernel(pieces, *refs):
    feeds, (gate_w, upper_w, gate_out, upper_out, inner, feed) = refs[:pieces], refs[pieces:]

    @pl.when(pl.program_id(0) == 0)
    def _():
        join(feed, feeds)

    for begin in range(0, feed.shape[0], 256):
        rows = slice(begin, begin + 256)
        gate = nn(feed[rows], gate_w[...])
        upper = nn(feed[rows], upper_w[...])
        gate_out[rows] = gate.astype(low)
        upper_out[rows] = upper.astype(low)
        inner[rows] = (gate * jax.nn.sigmoid(gate) * upper).astype(low)


def feed_forward(feeds, gate_w, upper_w):
    tokens = sum(p.shape[0] for p in feeds)
    width, hidden_units = gate_w.shape
    size = 256
    column = lambda r: pl.BlockSpec((r, size), lambda i: (0, i))
    return call(
        functools.partial(feed_kernel, len(feeds)),
        "feed_forward",
        4 * tokens * width * hidden_units,
        4 * width * hidden_units,
        grid=(pl.cdiv(hidden_units, size),),
        in_specs=[*[whole(*p.shape) for p in feeds], column(width), column(width)],
        out_specs=[column(tokens), column(tokens), column(tokens), whole(tokens, width)],
        out_shape=[shaped((tokens, hidden_units), low)] * 3 + [shaped((tokens, width), low)],
    )(*feeds, gate_w, upper_w)


def unit_kernel(pieces, places, *refs):
    grads, (gate_in, upper_in, down_w, gate_grad, upper_grad, grad) = refs[:pieces], refs[pieces:]

    @pl.when(pl.program_id(0) == 0)
    def _():
        row = 0
        for piece in grads:
            grad[row : row + piece.shape[0]] = (residual_scale * piece[...].astype(wide)).astype(low)
            row += piece.shape[0]

    for begin in range(0, grad.shape[0], 256):
        rows = slice(begin, begin + 256)
        back = nn(grad[rows], down_w[...])
        gate = gate_in[rows].astype(wide)
        sigmoid = jax.nn.sigmoid(gate)
        gate_grad[rows] = (back * upper_in[rows].astype(wide) * sigmoid * (1.0 + gate * (1.0 - sigmoid))).astype(low)
        upper_grad[rows] = (back * gate * sigmoid).astype(low)


def unit_back(chunk, places, gate, upper, grad_all, down_w):
    tokens, hidden_units = gate.shape
    width = down_w.shape[0]
    size = 256
    column = lambda r: pl.BlockSpec((r, size), lambda i, order: (0, i))
    third, half = tokens // 4, tokens // 8
    near = [pl.BlockSpec((third, width), functools.partial(lambda k, i, order: (order[k] * 2 + chunk, 0), k)) for k in range(3)]
    far = [pl.BlockSpec((half, width), functools.partial(lambda k, i, order: (order[3] * 4 + 2 * chunk + k, 0), k)) for k in range(2)]
    return call(
        functools.partial(unit_kernel, 5),
        "unit_back",
        2 * tokens * width * hidden_units,
        2 * width * hidden_units,
        grid_spec=pltpu.PrefetchScalarGridSpec(
            num_scalar_prefetch=1,
            grid=(pl.cdiv(hidden_units, size),),
            in_specs=[*near, *far, column(tokens), column(tokens), column(width)],
            out_specs=[column(tokens), column(tokens), pl.BlockSpec((tokens, width), lambda i, order: (0, 0))],
        ),
        out_shape=[shaped((tokens, hidden_units), low)] * 2 + [shaped((tokens, width), low)],
    )(places, *[grad_all] * 5, gate, upper, down_w)


def back_kernel(factors, chunks, places, *refs):
    lefts, weights, outs = refs[: factors * chunks], refs[factors * chunks : factors * chunks + factors], refs[factors * chunks + factors :]
    for chunk, out in enumerate(outs):
        found = sum(nt(lefts[f * chunks + chunk][...], weights[f][...]) for f in range(factors)).astype(low)
        rows = out.shape[0] // 4
        for k in range(4):
            out[pl.ds(pl.multiple_of(places[k] * rows, 128), rows)] = found[k * rows : (k + 1) * rows]


def feed_back(name, places, lefts, weights):
    chunks = len(lefts[0])
    flat = [chunk for factor in lefts for chunk in factor]
    tokens, hidden_units = flat[0].shape
    width = weights[0].shape[0]
    size = 256
    return call(
        functools.partial(back_kernel, len(lefts), chunks),
        name,
        2 * len(flat) * tokens * width * hidden_units,
        2 * len(lefts) * width * hidden_units,
        grid_spec=pltpu.PrefetchScalarGridSpec(
            num_scalar_prefetch=1,
            grid=(width // size,),
            in_specs=[*[pl.BlockSpec(p.shape, lambda i, order: (0, 0)) for p in flat], *[pl.BlockSpec((size, hidden_units), lambda i, order: (i, 0))] * len(weights)],
            out_specs=[pl.BlockSpec((tokens, size), lambda i, order: (0, i))] * chunks,
        ),
        out_shape=[shaped((tokens, width), low)] * chunks,
    )(places, *flat, *weights)


def weight_kernel(chunks, groups, *refs):
    lefts = refs[:chunks]
    outs = refs[chunks + chunks * groups :]
    for g, out in enumerate(outs):
        rights = refs[chunks + g * chunks : chunks + (g + 1) * chunks]
        out[...] = sum(tn(left[...], right[...]) for left, right in zip(lefts, rights, strict=True)).astype(low)


def weight_gradients(name, lefts, rights, first=0, width=None):
    chunks, groups = len(lefts), len(rights)
    tokens = lefts[0].shape[0]
    width = width or lefts[0].shape[1]
    columns = rights[0][0].shape[1]
    size = 256
    return call(
        functools.partial(weight_kernel, chunks, groups),
        name,
        2 * groups * chunks * tokens * width * columns,
        2 * (groups * (width + chunks * tokens) * columns + chunks * tokens * width),
        grid=(width // size,),
        in_specs=[*[pl.BlockSpec((tokens, size), lambda i: (0, first // size + i))] * chunks, *[whole(tokens, columns)] * (chunks * groups)],
        out_specs=[pl.BlockSpec((size, columns), lambda i: (i, 0))] * groups,
        out_shape=[shaped((width, columns), low)] * groups,
    )(*lefts, *[r for group in rights for r in group])


def split_cores(core, found, own, other):
    rows = own.shape[1]

    @pl.when(core[0] == 0)
    def _():
        own[0] = found[:rows]
        other[0] = found[rows:]

    @pl.when(core[0] != 0)
    def _():
        own[0] = found[rows:]
        other[0] = found[:rows]


def split_kernel(chunks, core, *refs):
    lefts, rights, outs = refs[:chunks], refs[chunks : 2 * chunks], refs[2 * chunks :]
    split_cores(core, sum(tn(left[...], right[...]) for left, right in zip(lefts, rights, strict=True)).astype(low), *outs)


def split_gradient(name, lefts, rights):
    chunks = len(lefts)
    tokens, width = lefts[0].shape
    columns = rights[0].shape[1]
    size = width // 4
    return call(
        functools.partial(split_kernel, chunks),
        name,
        2 * chunks * tokens * width * columns,
        2 * (width * columns + chunks * tokens * (width + columns)),
        grid_spec=pltpu.PrefetchScalarGridSpec(
            num_scalar_prefetch=1,
            grid=(4,),
            in_specs=[*[pl.BlockSpec((tokens, size), lambda i, core: (0, i))] * chunks, *[pl.BlockSpec((tokens, columns), lambda i, core: (0, 0))] * chunks],
            out_specs=[pl.BlockSpec((1, size // 2, columns), lambda i, core: (i, 0, 0))] * 2,
        ),
        out_shape=[shaped((4, size // 2, columns), low)] * 2,
    )(this_core(), *lefts, *rights)


def latents_kernel(query_grad, expanded_grad, rotary, up_q, up_kv, out):
    rank = up_q.shape[0]
    out[:, :rank] = nt(query_grad[...], up_q[...]).astype(low)
    out[:, rank : rank + KVR] = nt(expanded_grad[...], up_kv[...]).astype(low)
    out[:, rank + KVR :] = rotary[...].astype(low)


def latents_back(query_grad, expanded_grad, rotary, up_q, up_kv):
    group, columns = query_grad.shape
    rank = up_q.shape[0]
    size = 256
    row = lambda w: pl.BlockSpec((size, w), lambda i: (i, 0))
    out_width = rank + KVR + LANES
    return call(
        latents_kernel,
        "latents_back",
        2 * group * columns * (rank + KVR),
        4 * group * columns,
        grid=(group // size,),
        in_specs=[row(columns), row(columns), row(LANES), whole(*up_q.shape), whole(*up_kv.shape)],
        out_specs=row(out_width),
        out_shape=shaped((group, out_width), low),
    )(query_grad, expanded_grad, rotary, up_q, up_kv)


def input_kernel(steps, rank, core, own, one, two, joint, gains, chooser, cosine, sine_left, sine_right, weights, hidden, feed_row, middle_grad, *refs):
    downs_grad, (input_gradient, joint_grad, mixed_row, inverse, total) = refs[:-5], refs[-5:]
    step = pl.program_id(0)
    size, columns = weights.shape
    lanes = pl.ds(pl.multiple_of(step * size, size), size)

    @pl.when(step == 0)
    def _():
        values = hidden[...].astype(wide)
        inverse[...] = jnp.broadcast_to(lax.rsqrt(jnp.mean(values * values, axis=-1, keepdims=True) + epsilon), inverse.shape)
        parts = []
        for begin, end in ((0, rank), (rank, rank + KVR)):
            grad = own[:, begin:end].astype(wide) + one[:, begin:end].astype(wide) + two[:, begin:end].astype(wide)
            part = joint[:, begin:end]
            turn = lax.rsqrt(jnp.mean(part * part, axis=-1, keepdims=True) + epsilon)
            unit = part * turn
            parts.append(jnp.sum(grad * unit, axis=0, keepdims=True))
            joint_grad[:, begin:end] = norm_back(grad, unit, turn, gains[2:3, begin:end]).astype(low)
        lane = lax.broadcasted_iota(jnp.int32, (1, LANES), 1)
        last = slice(rank + KVR, rank + KVR + LANES)
        grad = own[:, last].astype(wide) + one[:, last].astype(wide) + two[:, last].astype(wide)
        back = grad * cosine[...] - pltpu.roll(grad, LANES - ROPE // 2, 1) * sine_left[...] - pltpu.roll(grad, ROPE // 2, 1) * sine_right[...]
        back = jnp.where((lane >= NOPE) & (lane < NOPE + ROPE), back, 0.0)
        joint_grad[:, last] = pltpu.roll(back, LANES - NOPE, 1).astype(low)
        norms = jnp.broadcast_to(jnp.concatenate(parts, axis=1), (8, rank + KVR)).astype(low)
        mixed_row[...] = nt(norms, chooser[...])

    unit = hidden[:, lanes].astype(wide) * inverse[:, :1]
    normed = (unit * gains[0:1, lanes]).astype(low)
    back = nt(joint_grad[...], weights[...])
    total[:, lanes] = back
    found = tn(normed, joint_grad[...])
    gain_row = jnp.sum(back * unit, axis=0, keepdims=True)
    gap = lambda n: jnp.zeros((n, size), wide)
    rows = jnp.concatenate([gap(ROPE), gain_row, feed_row[:, lanes], mixed_row[0:1, lanes], gap(LANES - ROPE - 3)], axis=0)
    found = jnp.concatenate([found[:, : columns - LANES], found[:, columns - LANES :] + rows.T], axis=1).astype(low)
    if len(downs_grad) == 1:
        downs_grad[0][...] = found
    else:
        split_cores(core, found, *downs_grad)

    @pl.when(step == steps - 1)
    def _():
        turn = inverse[:, :1]
        input_gradient[...] = (middle_grad[...] + norm_back(total[...], hidden[...].astype(wide) * turn, turn, gains[0:1])).astype(low)


def input_back(terms, joint, gains, chooser, tables, weights, hidden, feed_row, middle_grad, split):
    rows, width = hidden.shape
    columns = weights.shape[1]
    steps = 4
    size = width // steps
    before = (*terms, joint, gains, chooser, *tables)
    if split:
        out_specs = [pl.BlockSpec((1, size // 2, columns), lambda i, core: (i, 0, 0))] * 2
        out_shape = [shaped((4, size // 2, columns), low)] * 2
    else:
        out_specs = [pl.BlockSpec((size, columns), lambda i, core: (i, 0))]
        out_shape = [shaped((width, columns), low)]
    return call(
        functools.partial(input_kernel, steps, columns - KVR - LANES),
        "input_back",
        4 * rows * width * columns,
        4 * width * columns,
        grid_spec=pltpu.PrefetchScalarGridSpec(
            num_scalar_prefetch=1,
            grid=(steps,),
            in_specs=[*[whole(*p.shape) for p in before], pl.BlockSpec((size, columns), lambda i, core: (i, 0)), whole(rows, width), whole(1, width), whole(rows, width)],
            out_specs=[*out_specs, whole(rows, width)],
            scratch_shapes=[pltpu.VMEM((rows, columns), low), pltpu.VMEM((8, width), wide), pltpu.VMEM((rows, LANES), wide), pltpu.VMEM((rows, width), wide)],
        ),
        out_shape=[*out_shape, shaped((rows, width), low)],
    )(this_core(), *before, weights, hidden, feed_row, middle_grad)


def after(value, *earlier):
    return lax.optimization_barrier((value, *earlier))[0]


def after_all(values, *earlier):
    return list(lax.optimization_barrier((tuple(values), earlier))[0])


def gather_near(block):
    return [block, lax.ppermute(block, "tensor", RIGHT), lax.ppermute(block, "tensor", LEFT)]


def gather_far(near):
    half = near[0].shape[0] // 2
    return [lax.ppermute(near[1][:half], "tensor", RIGHT), lax.ppermute(near[2][half:], "tensor", LEFT)]


def scatter_first(own, to_left, to_right, far_first, far_second):
    half = own.shape[0] // 2
    first = lax.ppermute(far_first, "tensor", LEFT)
    second = lax.ppermute(far_second, "tensor", RIGHT)
    return [jnp.concatenate([to_left[:half] + first, to_left[half:]]), jnp.concatenate([to_right[:half], to_right[half:] + second])]


def scatter_second(sent):
    return [lax.ppermute(sent[0], "tensor", LEFT), lax.ppermute(sent[1], "tensor", RIGHT)]


def add_up(*terms):
    return sum(term.astype(wide) for term in terms)


def exchange_line(blocks):
    own, to_left, to_right, far = blocks
    return [own, lax.ppermute(to_right, "tensor", RIGHT), lax.ppermute(to_left, "tensor", LEFT), lax.ppermute(far, "tensor", OPPOSITE)]


def line_order():
    here = lax.axis_index("tensor")
    return [here, (here + 3) % 4, (here + 1) % 4, (here + 2) % 4]


def this_core():
    return lax.axis_index("dp").astype(jnp.int32)[None] % 2


def flips(bit):
    return [(i, i ^ bit) for i in range(8)]


def cube_near(block):
    return [block, lax.ppermute(block, "dp", flips(2)), lax.ppermute(block, "dp", flips(4))]


def cube_far(near):
    half = near[0].shape[0] // 2
    return [lax.ppermute(near[1][:half], "dp", flips(4)), lax.ppermute(near[2][half:], "dp", flips(2))]


def cube_rows(rows):
    here = lax.axis_index("dp")
    places = [here, here ^ 2, here ^ 4, here ^ 6]
    first = [p * rows for p in (*places, places[3])]
    second = [(p ^ 1) * rows for p in (*places, places[3])]
    first[4] += rows // 2
    second[4] += rows // 2
    return first + second


def swap_cores(blocks):
    return [lax.ppermute(value, "dp", flips(1)) for value in blocks]


def scatter_chips(blocks):
    if blocks.ndim == 2:
        return lax.psum_scatter(blocks, "dp", scatter_dimension=0, tiled=True)
    chips, rows, columns = blocks.shape
    return lax.psum_scatter(blocks.reshape(chips * rows, columns), "dp", scatter_dimension=0, tiled=True, axis_index_groups=[[0, 2, 4, 6], [1, 3, 5, 7]])


def scatter_core(blocks):
    count, rows, columns = blocks.shape
    if count != 8:
        return [blocks]
    core = lax.axis_index("dp") % 2
    other = lax.dynamic_index_in_dim(blocks.reshape(4, 2, rows, columns), 1 - core, 1, keepdims=False)
    return [blocks, lax.ppermute(other, "dp", flips(1))]


def scatter_pair(halves, place):
    here = lax.axis_index("dp")
    pick = lambda array, at: lax.dynamic_index_in_dim(array, at, 0, keepdims=False)
    first = here ^ (2 * place) if halves[0].shape[0] == 8 else (here // 2) ^ place
    return add_up(pick(halves[0], first), pick(halves[1], (here // 2) ^ place))


def scatter_corner(halves):
    if len(halves) == 1:
        return halves
    half = halves[0].shape[1] // 2
    corner = scatter_pair(halves, 3).astype(low)
    return [lax.ppermute(corner[:half], "dp", flips(2)), lax.ppermute(corner[half:], "dp", flips(4))]


def scatter_sides(halves, corners):
    half = halves[0].shape[1] // 2
    across, along = scatter_pair(halves, 1), scatter_pair(halves, 2)
    across = jnp.concatenate([across[:half], across[half:] + corners[1]]).astype(low)
    along = jnp.concatenate([along[:half] + corners[0], along[half:]]).astype(low)
    return [across, along]


def scatter_swap(sides):
    return [lax.ppermute(sides[0], "dp", flips(2)), lax.ppermute(sides[1], "dp", flips(4))]


def scatter_last(halves, swapped):
    return add_up(scatter_pair(halves, 0), *swapped)


def scatter_rest(halves, corners):
    if len(halves) == 1:
        count, rows, columns = halves[0].shape
        return lax.psum_scatter(corners[0].reshape(count * rows, columns), "dp", scatter_dimension=0, tiled=True).astype(wide)
    return scatter_last(halves, scatter_swap(scatter_sides(halves, corners)))


def local(hidden_in, attention_gain, query_down, query_norm, latent_down, latent_norm, query_up, latent_up, output_weight, feed_gain, gate_weight, up_weight, down_weight, cotangent, document_lengths):
    replicas = lax.axis_size("dp")
    rows, width = hidden_in.shape
    group = rows * 4
    rank = query_down.shape[1]
    heads = query_up.shape[1] // (NOPE + ROPE)
    slice_rows = query_down.shape[0]
    order = line_order()
    joint_width = rank + KVR + LANES
    by_line = lambda array: [lax.dynamic_index_in_dim(array, p, 0, keepdims=False) for p in order]

    def column(value):
        return jnp.pad(value, (0, slice_rows - value.shape[0]))[:, None]

    norms = jnp.concatenate([query_norm, latent_norm])
    downs = jnp.concatenate([query_down, latent_down, column(attention_gain), column(feed_gain), column(norms)], axis=1)
    downs = jnp.pad(downs, ((0, 0), (0, joint_width - downs.shape[1])))
    parts = [slice(k * rows // 2, (k + 1) * rows // 2) for k in range(2)]
    if replicas == 8:
        downs = place(exchange_line([downs] * 4), lambda: [p * slice_rows for p in line_order()], 4 * slice_rows)
    out_near = gather_near(after(output_weight.T, downs))

    query_up_wide = jnp.pad(query_up.reshape(-1, heads, NOPE + ROPE), ((0, 0), (0, 0), (0, LANES - NOPE - ROPE))).reshape(-1, heads * LANES)
    ups_all = lax.all_gather(jnp.concatenate([query_up_wide, latent_up], axis=0), "dp", axis=0)
    up_q = ups_all[:, : query_up.shape[0]].reshape(rank, heads * LANES)
    up_kv = ups_all[:, query_up.shape[0] :].reshape(KVR, heads * LANES)

    grad_all = lax.all_gather(cotangent, "tensor", axis=0, tiled=True)
    segment, position = layout(document_lengths[0], group)
    cosine_half, sine_half = rotary_tables(position, ROPE)
    zeros = lambda n: jnp.zeros((group, n), wide)
    cosine_wide = jnp.concatenate([jnp.ones((group, NOPE), wide), cosine_half, cosine_half, zeros(ROPE)], axis=1)
    sine_left = jnp.concatenate([zeros(NOPE), -sine_half, zeros(ROPE // 2 + ROPE)], axis=1)
    sine_right = jnp.concatenate([zeros(NOPE + ROPE // 2), sine_half, zeros(ROPE)], axis=1)
    segment_col, segment_row = segment[:, None], segment[None, :]
    first_row = lax.axis_index("tensor") * rows
    local_tables = [lax.dynamic_slice_in_dim(t, first_row, rows, 0) for t in (cosine_wide, sine_left, sine_right)]
    a, b = query_norm.shape[0], norms.shape[0]
    lanes = jnp.arange(rank + KVR)
    source = jnp.where(lanes < rank, lanes // a * slice_rows + lanes % a, (lanes - rank) // (b - a) * slice_rows + a + (lanes - rank) % (b - a))
    chooser = (jnp.arange(width)[:, None] == source[None, :]).astype(low)
    ready = (chooser, cosine_wide, sine_left, sine_right, segment_col, *local_tables)
    if replicas == 8:
        near = after_all(cube_near(downs), *out_near)
        out_far = gather_far(after_all(out_near, near[1]))
        near = after_all(near + cube_far(near), *out_far)
        down_pieces = after_all(near + swap_cores(near), *ready)
        down_places = jnp.stack(cube_rows(near[0].shape[0])).astype(jnp.int32)
    else:
        down_pieces = [lax.all_gather(downs, ("dp", "tensor"), axis=0, tiled=True)]
        down_places = jnp.zeros((1,), jnp.int32)
        out_far = gather_far(out_near)
    gate_all = lax.all_gather(after(gate_weight, down_pieces[0]), "dp", axis=0, tiled=True)
    weights_down, joint, latents_own, gains = down_projections(hidden_in, down_pieces, down_places, chooser, rank, local_tables)
    feed_scale = gains[1:2]
    latents_near = gather_near(latents_own)
    latents_near = after_all(latents_near, up_q, up_kv)

    out_block = after(jnp.concatenate([*out_near, jnp.concatenate(out_far, axis=0)], axis=1), down_pieces[0])
    if replicas == 8:
        out_blocks = cube_near(out_block)
        latents_near = after_all(latents_near, *out_blocks)
        out_blocks += cube_far(out_blocks)
        out_soon = out_blocks
    else:
        out_all = lax.all_gather(out_block, "dp", axis=0, tiled=True)
        out_soon = [out_all]
    latents_far = gather_far(latents_near)

    def latent_rows():
        here = line_order()
        return [here[0] * rows, here[1] * rows, here[2] * rows, here[3] * rows, here[3] * rows + rows // 2]

    latents = place(after_all(latents_near + latents_far, *out_soon), latent_rows, group)
    upper_all = lax.all_gather(after(up_weight, latents), "dp", axis=0, tiled=True)
    down_all = lax.all_gather(after(down_weight.T, latents), "dp", axis=0, tiled=True)

    block = min(256, group)
    pairs = heads // 2
    by_pair = lambda r, w: pl.BlockSpec((r, w), lambda i: (0, i))
    attended, queries, expanded, log_total = call(
        functools.partial(attention_forward_kernel, rank, block),
        "attention_forward",
        20 * 10**9,
        15 * 10**6,
        grid=(pairs,),
        in_specs=[whole(group, joint_width), by_pair(rank, 2 * LANES), by_pair(KVR, 2 * LANES), whole(group, LANES), whole(group, LANES), whole(group, LANES), whole(group, 1), whole(1, group)],
        out_specs=[by_pair(group, LANES), by_pair(group, 2 * LANES), by_pair(group, 2 * LANES), whole(group, LANES)],
        out_shape=[shaped((group, heads * VD), low), shaped((group, heads * LANES), low), shaped((group, heads * LANES), low), shaped((group, LANES), wide)],
    )(latents, up_q, up_kv, cosine_wide, sine_left, sine_right, segment_col, segment_row)
    log_rows = log_total[:, :16].T

    if replicas == 8:
        out_other = after_all(swap_cores(out_blocks), attended)
        out_all = place(out_blocks + out_other, lambda: cube_rows(out_block.shape[0]), 8 * out_block.shape[0])

    attended_parts = lax.all_to_all(attended.reshape(4, rows, heads * VD), "tensor", 0, 0)
    attended_own = jnp.concatenate(by_line(attended_parts), axis=1)
    attended_own = after(attended_own, grad_all)
    middle = hidden_in.astype(wide) + residual_scale * nt(attended_own, out_all)
    inverse_middle = inverse_rms(middle)
    unit_middle = middle * inverse_middle
    feed_in = (unit_middle * feed_scale).astype(low)

    near_0 = gather_near(feed_in[parts[0]])
    far_0 = gather_far(near_0)
    near_1 = gather_near(after(feed_in[parts[1]], *far_0))
    places = jnp.stack(order).astype(jnp.int32)
    gate, upper, inner_0, feed_0 = feed_forward(near_0 + far_0, gate_all, upper_all)
    far_1 = gather_far(after_all(near_1, inner_0))
    gate_0, upper_0, grad_0 = unit_back(0, places, *after_all([gate, upper], *far_1), grad_all, down_all)
    (part_0,) = feed_back("feed_back", places, [[gate_0], [upper_0]], [gate_all, upper_all])
    gate, upper, inner_1, feed_1 = feed_forward(after_all(near_1 + far_1, part_0), gate_all, upper_all)
    gate_1, upper_1, grad_1 = unit_back(1, places, gate, upper, grad_all, down_all)
    (part_1,) = feed_back("feed_back", places, [[gate_1], [upper_1]], [gate_all, upper_all])
    down_lefts = after_all([grad_0, grad_1], part_1)
    if replicas == 8:
        down_own, down_grad = split_gradient("down_gradient", down_lefts, [inner_0, inner_1])
        down_core = [down_own, *swap_cores([down_grad])]
    else:
        (down_grad,) = weight_gradients("down_gradient", down_lefts, [[inner_0, inner_1]])
        down_core = scatter_core(down_grad.reshape(replicas, -1, down_grad.shape[1]))
    gate_lefts = after_all([feed_0, feed_1], down_grad)
    if replicas == 8:
        gate_own, gate_grad = split_gradient("gate_gradient", gate_lefts, [gate_0, gate_1])
        upper_own, upper_grad = split_gradient("upper_gradient", after_all(gate_lefts, gate_grad), [upper_0, upper_1])
        gate_chips = add_up(gate_own, *swap_cores([gate_grad])).astype(low)
        upper_halves = [upper_own, *swap_cores([upper_grad])]
    else:
        gate_grad, upper_grad = weight_gradients("gate_gradient", gate_lefts, [[gate_0, gate_1], [upper_0, upper_1]])
        gate_chips, upper_halves = gate_grad, [upper_grad]
    got_0 = lax.psum_scatter(part_0, "tensor", scatter_dimension=0, tiled=True)
    got_1 = lax.psum_scatter(part_1, "tensor", scatter_dimension=0, tiled=True)
    down_corner = scatter_corner(down_core)
    down_sides = scatter_sides(down_core, down_corner) if replicas == 8 else down_corner
    gate_sum = scatter_chips(after(gate_chips, part_1))
    got_0, got_1 = after_all([got_0, got_1], gate_chips)
    feed_in_grad = jnp.concatenate([got_0, got_1]).astype(wide)

    feed_gain_part = jnp.sum(feed_in_grad * unit_middle, axis=0, keepdims=True)
    middle_grad = cotangent.astype(wide) + norm_back(feed_in_grad, unit_middle, inverse_middle, feed_scale)
    branch_one_grad = (residual_scale * middle_grad).astype(low)
    attended_grad_own = nn(branch_one_grad, out_all).astype(low)
    attended_grads = jnp.zeros((4, rows, heads * VD), low)
    for k, p in enumerate(order):
        attended_grads = lax.dynamic_update_index_in_dim(attended_grads, attended_grad_own[:, k * heads * VD : (k + 1) * heads * VD], p, 0)
    out_left = after(branch_one_grad, attended_grad_own)
    if replicas == 8:
        out_own, out_grad = split_gradient("out_gradient", [out_left], [attended_own])
        out_core = [out_own, *swap_cores([out_grad])]
    else:
        out_grad = tn(out_left, attended_own).astype(low)
        out_core = scatter_core(out_grad.reshape(replicas, -1, 4 * heads * VD))
    attended_grad = lax.all_to_all(after(attended_grads, out_grad), "tensor", 0, 0).reshape(group, heads * VD)
    upper_chips = add_up(*after_all(upper_halves, attended_grads)).astype(low) if replicas == 8 else upper_halves[0]
    upper_sum = scatter_chips(upper_chips)
    attended_grad = after(attended_grad, upper_chips, *out_core)
    out_corner = scatter_corner(out_core)
    down_swapped = scatter_swap(down_sides) if replicas == 8 else down_corner

    query_grad, expanded_grad, rotary_grad = call(
        functools.partial(attention_backward_kernel, block),
        "attention_backward",
        30 * 10**9,
        15 * 10**6,
        grid=(pairs,),
        in_specs=[by_pair(group, 2 * LANES), by_pair(group, 2 * LANES), pl.BlockSpec((group, LANES), lambda i: (0, (rank + KVR) // LANES)), whole(group, LANES), whole(group, LANES), whole(group, LANES), whole(group, 1), whole(1, group), whole(16, group), by_pair(group, LANES)],
        out_specs=[by_pair(group, 2 * LANES), by_pair(group, 2 * LANES), whole(group, LANES)],
        out_shape=[shaped((group, heads * LANES), low), shaped((group, heads * LANES), low), shaped((group, LANES), wide)],
        scratch_shapes=[pltpu.VMEM((group, LANES), wide), pltpu.VMEM((group, LANES), wide)],
    )(queries, expanded, latents, cosine_wide, sine_left, sine_right, segment_col, segment_row, log_rows, attended_grad)

    latents_part = latents_back(*after_all([query_grad, expanded_grad, rotary_grad], *down_swapped, *out_corner), up_q, up_kv)
    cut = by_line(latents_part.reshape(4, rows, joint_width))
    sent = scatter_first(*cut[:3], cut[3][: rows // 2], cut[3][rows // 2 :])

    turn = after(latents, *sent)
    outs = feed_back("branch_two", places, [after_all([inner_0, inner_1], *sent)], [down_all])
    (query_up_grad,) = weight_gradients("query_up_gradient", [turn], [[query_grad]], 0, rank)
    (latent_up_grad,) = weight_gradients("latent_up_gradient", [turn], [[expanded_grad]], rank, KVR)
    ups_grad = jnp.concatenate([query_up_grad.reshape(replicas, -1, heads * LANES), latent_up_grad.reshape(replicas, -1, heads * LANES)], axis=1)
    ups_core = scatter_core(ups_grad)
    out_swapped = scatter_swap(scatter_sides(after_all(out_core, cut[0]), out_corner)) if replicas == 8 else out_corner
    latents_terms = after_all([cut[0], *scatter_second(sent)], *ups_core, *out_swapped, *outs)
    branch_two = [lax.psum_scatter(after(out, *latents_terms), "tensor", scatter_dimension=0, tiled=True) for out in outs]
    ups_corner = scatter_corner(ups_core)
    *downs_grad, input_gradient = input_back(latents_terms, joint, gains, chooser, local_tables, weights_down, hidden_in, feed_gain_part, middle_grad, replicas == 8)
    downs_grad = after_all(downs_grad, *ups_corner)
    if replicas == 8:
        downs_core = [downs_grad[0], *swap_cores(downs_grad[1:])]
        downs_part = scatter_rest(downs_core, scatter_corner(downs_core)).astype(low).reshape(4, slice_rows, joint_width)
        downs_sum = sum(p.astype(wide) for p in exchange_line(by_line(downs_part)))
        out_part = scatter_last(out_core, out_swapped).astype(low)
    else:
        downs_sum = lax.psum_scatter(downs_grad[0], ("dp", "tensor"), scatter_dimension=0, tiled=True).astype(wide)
        out_part = scatter_rest(out_core, out_corner).astype(low)
    out_got = exchange_line([out_part[:, k * heads * VD : (k + 1) * heads * VD] for k in range(4)])
    ups_sum = scatter_rest(ups_core, ups_corner)
    gain_sums = downs_sum[:, rank + KVR + ROPE : rank + KVR + ROPE + 3].T

    output_sum = add_up(*out_got).T

    gate_sum, upper_sum, *branch_two = [v.astype(wide) for v in after_all([gate_sum, upper_sum, *branch_two], downs_sum)]
    layer_output = (middle + residual_scale * jnp.concatenate(branch_two)).astype(low)
    if replicas == 8:
        down_sum = scatter_last(after_all(down_core, *downs_grad), down_swapped).T
    else:
        down_sum = scatter_rest(down_core, down_corner).T
    query_up_sum = ups_sum[: query_up.shape[0]].reshape(-1, heads, LANES)[..., : NOPE + ROPE].reshape(query_up.shape)
    return (
        layer_output,
        input_gradient,
        gain_sums[0],
        downs_sum[:, :rank],
        gain_sums[2, :a],
        downs_sum[:, rank : rank + KVR + ROPE],
        gain_sums[2, a:b],
        query_up_sum,
        ups_sum[query_up.shape[0] :],
        output_sum,
        gain_sums[1],
        gate_sum,
        upper_sum,
        down_sum,
    )


def solution(mesh):
    return jax.shard_map(
        local,
        mesh=mesh,
        in_specs=(
            P(("dp", "tensor"), None),
            P(("dp", "tensor")),
            P(("dp", "tensor"), None),
            P(("dp", "tensor")),
            P(("dp", "tensor"), None),
            P(("dp", "tensor")),
            P("dp", "tensor"),
            P("dp", "tensor"),
            P("tensor", "dp"),
            P(("dp", "tensor")),
            P("dp", "tensor"),
            P("dp", "tensor"),
            P("tensor", "dp"),
            P(("dp", "tensor"), None),
            P("dp", None),
        ),
        out_specs=(
            P(("dp", "tensor"), None),
            P(("dp", "tensor"), None),
            P(("dp", "tensor")),
            P(("dp", "tensor"), None),
            P(("dp", "tensor")),
            P(("dp", "tensor"), None),
            P(("dp", "tensor")),
            P("dp", "tensor"),
            P("dp", "tensor"),
            P("tensor", "dp"),
            P(("dp", "tensor")),
            P("dp", "tensor"),
            P("dp", "tensor"),
            P("tensor", "dp"),
        ),
        check_vma=False,
    )
```

```python
import math, functools
import jax, jax.numpy as jnp
from jax import lax
from jax.experimental import pallas as pl
from jax.experimental.pallas import tpu as pltpu
from jax.sharding import PartitionSpec as P

KVR, ROPE, NOPE, VD = 256, 32, 64, 64
LANES = 128
softmax_scale = 1.0 / math.sqrt(NOPE + ROPE)
log2_scale = softmax_scale / math.log(2.0)


def nt(left, right):
    return lax.dot_general(left, right, (((1,), (1,)), ((), ())), preferred_element_type=jnp.float32)


def nn(left, right):
    return lax.dot_general(left, right, (((1,), (0,)), ((), ())), preferred_element_type=jnp.float32)


def tn(left, right):
    return lax.dot_general(left, right, (((0,), (0,)), ((), ())), preferred_element_type=jnp.float32)


def attention_forward_kernel(rank, block, latents, up_q, up_kv, cosine, sine_left, sine_right, segment_col, segment_row, attended, queries, expanded, log_total):
    pair = pl.program_id(0)
    group = latents.shape[0]
    lane = lax.broadcasted_iota(jnp.int32, (1, LANES), 1)
    rotary = latents[:, rank + KVR :].astype(jnp.float32)

    @pl.when(pair == 0)
    def _():
        log_total[...] = jnp.zeros_like(log_total)

    found = []
    for half in range(2):
        columns = slice(half * LANES, (half + 1) * LANES)
        raw = nn(latents[:, :rank], up_q[:, columns])
        turned = raw * cosine[...] + pltpu.roll(raw, LANES - ROPE // 2, 1) * sine_left[...] + pltpu.roll(raw, ROPE // 2, 1) * sine_right[...]
        query = turned.astype(jnp.bfloat16)
        queries[:, columns] = query
        both = nn(latents[:, rank : rank + KVR], up_kv[:, columns])
        key = jnp.where(lane < NOPE, both, rotary).astype(jnp.bfloat16)
        both = both.astype(jnp.bfloat16)
        expanded[:, columns] = both
        outs, sums = [], []
        for begin in range(0, group, block):
            end = begin + block
            scores = nt(query[begin:end], key[:end]) * log2_scale
            allowed = segment_col[begin:end, :] == segment_row[:, :end]
            row = lax.broadcasted_iota(jnp.int32, (block, end), 0) + begin
            column = lax.broadcasted_iota(jnp.int32, (block, end), 1)
            scores = jnp.where(allowed & (column <= row), scores, -1e30)
            peak = jnp.max(scores, axis=-1, keepdims=True)
            weights = jnp.exp2(scores - peak)
            total = jnp.sum(weights, axis=-1, keepdims=True)
            outs.append(nn(weights.astype(jnp.bfloat16), both[:end]) / total)
            sums.append(peak + jnp.log2(total))
        found.append(jnp.concatenate(outs, axis=0))
        log_total[...] = jnp.where(lane == 2 * pair + half, jnp.concatenate(sums, axis=0), log_total[...])
    attended[...] = jnp.where(lane < VD, pltpu.roll(found[0], VD, 1), found[1]).astype(jnp.bfloat16)


def attention_backward_kernel(block, queries, expanded, rotary_in, cosine, sine_left, sine_right, segment_col, segment_row, log_total, grad, query_grad, expanded_grad, rotary_grad, key_sum, value_sum):
    pair = pl.program_id(0)
    group = queries.shape[0]
    lane = lax.broadcasted_iota(jnp.int32, (1, LANES), 1)
    rotary = rotary_in[...].astype(jnp.float32)

    @pl.when(pair == 0)
    def _():
        rotary_grad[...] = jnp.zeros_like(rotary_grad)

    grads = grad[...].astype(jnp.float32)
    for half in range(2):
        columns = slice(half * LANES, (half + 1) * LANES)
        query = queries[:, columns]
        both = expanded[:, columns]
        key = jnp.where(lane < NOPE, both.astype(jnp.float32), rotary).astype(jnp.bfloat16)
        out_grad = pltpu.roll(grads, VD, 1) if half == 0 else grads
        out_grad = jnp.where(lane < NOPE, 0.0, out_grad).astype(jnp.bfloat16)
        log_row = log_total[pl.ds(2 * pair + half, 1), :]
        parts = []
        for begin in reversed(range(0, group, block)):
            end = begin + block
            scores = nt(key[:end], query[begin:end]) * log2_scale
            allowed = segment_col[:end, :] == segment_row[:, begin:end]
            row = lax.broadcasted_iota(jnp.int32, (end, block), 0)
            column = lax.broadcasted_iota(jnp.int32, (end, block), 1) + begin
            probs = jnp.where(allowed & (row <= column), jnp.exp2(scores - log_row[:, begin:end]), 0.0)
            prob_grad = nt(both[:end], out_grad[begin:end])
            center = jnp.sum(probs * prob_grad, axis=0, keepdims=True)
            score_grad = (probs * (prob_grad - center)).astype(jnp.bfloat16)
            key_part = nn(score_grad, query[begin:end])
            value_part = nn(probs.astype(jnp.bfloat16), out_grad[begin:end])
            if end == group:
                key_sum[...] = key_part
                value_sum[...] = value_part
            else:
                key_sum[:end] += key_part
                value_sum[:end] += value_part
            parts.append(tn(score_grad, key[:end]))
        found = jnp.concatenate(parts[::-1], axis=0) * softmax_scale
        back = found * cosine[...] - pltpu.roll(found, LANES - ROPE // 2, 1) * sine_left[...] - pltpu.roll(found, ROPE // 2, 1) * sine_right[...]
        query_grad[:, columns] = back.astype(jnp.bfloat16)
        keys = key_sum[...] * softmax_scale
        expanded_grad[:, columns] = jnp.where(lane < NOPE, keys, value_sum[...]).astype(jnp.bfloat16)
        rotary_grad[...] += jnp.where((lane >= NOPE) & (lane < NOPE + ROPE), keys, 0.0)


epsilon = 1e-05
residual_scale = 1.4 / math.sqrt(62.0)
rotary_base = 10000.0

RIGHT = [(i, (i + 1) % 4) for i in range(4)]
LEFT = [(i, (i - 1) % 4) for i in range(4)]
OPPOSITE = [(i, (i + 2) % 4) for i in range(4)]


def inverse_rms(values):
    return lax.rsqrt(jnp.mean(values * values, axis=-1, keepdims=True) + epsilon)


def norm_back(grad, unit, inverse, gain):
    scaled = grad * gain
    return inverse * (scaled - unit * jnp.mean(scaled * unit, axis=-1, keepdims=True))


def rotary_tables(positions, width):
    steps = jnp.arange(width // 2, dtype=jnp.float32) * (2.0 / width)
    freqs = jnp.exp(steps * -math.log(rotary_base))
    angles = positions.astype(jnp.float32)[:, None] * freqs[None, :]
    return jnp.cos(angles), jnp.sin(angles)


def layout(lengths_row, group_tokens):
    slots = jnp.arange(group_tokens, dtype=jnp.int32)
    ends = jnp.cumsum(lengths_row)
    segment = jnp.sum((slots[:, None] >= ends[None, :]).astype(jnp.int32), axis=1)
    starts = jnp.concatenate([jnp.zeros((1,), jnp.int32), ends])
    choose = segment[:, None] == jnp.arange(starts.shape[0], dtype=jnp.int32)[None, :]
    start_of = jnp.sum(jnp.where(choose, starts[None, :], 0), axis=1)
    return (segment, slots - start_of)


low, wide = jnp.bfloat16, jnp.float32
VMEM_LIMIT = 56 * 2**20


def call(kernel, name, flops, moved, **how):
    return pl.pallas_call(
        kernel,
        name=name,
        compiler_params=pltpu.CompilerParams(vmem_limit_bytes=VMEM_LIMIT),
        cost_estimate=pl.CostEstimate(flops=0, bytes_accessed=0, transcendentals=0),
        **how,
    )


def whole(*shape):
    return pl.BlockSpec(shape, lambda *i: (0,) * len(shape))


def shaped(shape, dtype):
    return jax.ShapeDtypeStruct(shape, dtype)


def place(blocks, rows_of, total):
    count, width = len(blocks), blocks[0].shape[1]

    def kernel(*refs):
        ins, out, held, done = refs[:count], refs[count], refs[count + 1 : 2 * count + 1], refs[-1]
        arrive = [pltpu.make_async_copy(ref, slot, done.at[0, k]) for k, (ref, slot) in enumerate(zip(ins, held, strict=True))]
        leave = [
            pltpu.make_async_copy(slot, out.at[pl.ds(pl.multiple_of(row, 16), slot.shape[0])], done.at[1, k])
            for k, (slot, row) in enumerate(zip(held, rows_of(), strict=True))
        ]
        for copy in arrive:
            copy.start()
        for first, second in zip(arrive, leave, strict=True):
            first.wait()
            second.start()
        for copy in leave:
            copy.wait()

    return call(
        kernel,
        "place",
        0,
        4 * total * width,
        in_specs=[pl.BlockSpec(memory_space=pl.ANY)] * count,
        out_specs=pl.BlockSpec(memory_space=pl.ANY),
        out_shape=shaped((total, width), blocks[0].dtype),
        scratch_shapes=[*[pltpu.VMEM(b.shape, b.dtype) for b in blocks], pltpu.SemaphoreType.DMA((2, count))],
    )(*blocks)


def join(target, pieces):
    row = 0
    for piece in pieces:
        target[row : row + piece.shape[0]] = piece[...]
        row += piece.shape[0]


def down_kernel(rank, places, hidden, *refs):
    pieces, (chooser, cosine, sine_left, sine_right, weights, joint, latents, gains) = refs[:-8], refs[-8:]
    for k, piece in enumerate(pieces):
        weights[pl.ds(pl.multiple_of(places[k], 16), piece.shape[0])] = piece[...]
    lane = lax.broadcasted_iota(jnp.int32, (1, LANES), 1)
    rows = weights[:, weights.shape[1] - LANES :].astype(wide).T[ROPE : ROPE + 8]
    gains[...] = rows
    chosen = nn(rows.astype(low), chooser[...])
    gains[2:3, : rank + KVR] = chosen[2:3]
    values = hidden[...].astype(wide)
    unit = values * lax.rsqrt(jnp.mean(values * values, axis=-1, keepdims=True) + epsilon)
    normed = (unit * rows[0:1]).astype(low)
    for begin in range(0, weights.shape[1], 384):
        joint[:, begin : begin + 384] = nn(normed, weights[:, begin : begin + 384])
    for begin, end in ((0, rank), (rank, rank + KVR)):
        part = joint[:, begin:end]
        latents[:, begin:end] = (part * lax.rsqrt(jnp.mean(part * part, axis=-1, keepdims=True) + epsilon) * chosen[2:3, begin:end]).astype(low)
    raw = pltpu.roll(joint[:, rank + KVR :], NOPE, 1)
    turned = raw * cosine[...] + pltpu.roll(raw, LANES - ROPE // 2, 1) * sine_left[...] + pltpu.roll(raw, ROPE // 2, 1) * sine_right[...]
    latents[:, rank + KVR :] = jnp.where((lane >= NOPE) & (lane < NOPE + ROPE), turned, 0.0).astype(low)


def down_projections(hidden, pieces, places, chooser, rank, tables):
    rows, width = hidden.shape
    columns = pieces[0].shape[1]
    operands = (hidden, *pieces, chooser, *tables)
    return call(
        functools.partial(down_kernel, rank),
        "down_projections",
        2 * rows * width * columns,
        2 * width * columns,
        grid_spec=pltpu.PrefetchScalarGridSpec(
            num_scalar_prefetch=1,
            grid=(1,),
            in_specs=[whole(*value.shape) for value in operands],
            out_specs=[whole(width, columns), whole(rows, columns), whole(rows, columns), whole(8, width)],
        ),
        out_shape=[shaped((width, columns), low), shaped((rows, columns), wide), shaped((rows, columns), low), shaped((8, width), wide)],
    )(places, *operands)


def feed_kernel(pieces, *refs):
    feeds, (gate_w, upper_w, gate_out, upper_out, inner, feed) = refs[:pieces], refs[pieces:]

    @pl.when(pl.program_id(0) == 0)
    def _():
        join(feed, feeds)

    for begin in range(0, feed.shape[0], 256):
        rows = slice(begin, begin + 256)
        gate = nn(feed[rows], gate_w[...])
        upper = nn(feed[rows], upper_w[...])
        gate_out[rows] = gate.astype(low)
        upper_out[rows] = upper.astype(low)
        inner[rows] = (gate * jax.nn.sigmoid(gate) * upper).astype(low)


def feed_forward(feeds, gate_w, upper_w):
    tokens = sum(p.shape[0] for p in feeds)
    width, hidden_units = gate_w.shape
    size = 256
    column = lambda r: pl.BlockSpec((r, size), lambda i: (0, i))
    return call(
        functools.partial(feed_kernel, len(feeds)),
        "feed_forward",
        4 * tokens * width * hidden_units,
        4 * width * hidden_units,
        grid=(pl.cdiv(hidden_units, size),),
        in_specs=[*[whole(*p.shape) for p in feeds], column(width), column(width)],
        out_specs=[column(tokens), column(tokens), column(tokens), whole(tokens, width)],
        out_shape=[shaped((tokens, hidden_units), low)] * 3 + [shaped((tokens, width), low)],
    )(*feeds, gate_w, upper_w)


def unit_kernel(pieces, places, *refs):
    grads, (gate_in, upper_in, down_w, gate_grad, upper_grad, grad) = refs[:pieces], refs[pieces:]

    @pl.when(pl.program_id(0) == 0)
    def _():
        row = 0
        for piece in grads:
            grad[row : row + piece.shape[0]] = (residual_scale * piece[...].astype(wide)).astype(low)
            row += piece.shape[0]

    for begin in range(0, grad.shape[0], 256):
        rows = slice(begin, begin + 256)
        back = nn(grad[rows], down_w[...])
        gate = gate_in[rows].astype(wide)
        sigmoid = jax.nn.sigmoid(gate)
        gate_grad[rows] = (back * upper_in[rows].astype(wide) * sigmoid * (1.0 + gate * (1.0 - sigmoid))).astype(low)
        upper_grad[rows] = (back * gate * sigmoid).astype(low)


def unit_back(chunk, places, gate, upper, grad_all, down_w):
    tokens, hidden_units = gate.shape
    width = down_w.shape[0]
    size = 256
    column = lambda r: pl.BlockSpec((r, size), lambda i, order: (0, i))
    third, half = tokens // 4, tokens // 8
    near = [pl.BlockSpec((third, width), functools.partial(lambda k, i, order: (order[k] * 2 + chunk, 0), k)) for k in range(3)]
    far = [pl.BlockSpec((half, width), functools.partial(lambda k, i, order: (order[3] * 4 + 2 * chunk + k, 0), k)) for k in range(2)]
    return call(
        functools.partial(unit_kernel, 5),
        "unit_back",
        2 * tokens * width * hidden_units,
        2 * width * hidden_units,
        grid_spec=pltpu.PrefetchScalarGridSpec(
            num_scalar_prefetch=1,
            grid=(pl.cdiv(hidden_units, size),),
            in_specs=[*near, *far, column(tokens), column(tokens), column(width)],
            out_specs=[column(tokens), column(tokens), pl.BlockSpec((tokens, width), lambda i, order: (0, 0))],
        ),
        out_shape=[shaped((tokens, hidden_units), low)] * 2 + [shaped((tokens, width), low)],
    )(places, *[grad_all] * 5, gate, upper, down_w)


def back_kernel(factors, chunks, places, *refs):
    lefts, weights, outs = refs[: factors * chunks], refs[factors * chunks : factors * chunks + factors], refs[factors * chunks + factors :]
    for chunk, out in enumerate(outs):
        found = sum(nt(lefts[f * chunks + chunk][...], weights[f][...]) for f in range(factors)).astype(low)
        rows = out.shape[0] // 4
        for k in range(4):
            out[pl.ds(pl.multiple_of(places[k] * rows, 128), rows)] = found[k * rows : (k + 1) * rows]


def feed_back(name, places, lefts, weights):
    chunks = len(lefts[0])
    flat = [chunk for factor in lefts for chunk in factor]
    tokens, hidden_units = flat[0].shape
    width = weights[0].shape[0]
    size = 256
    return call(
        functools.partial(back_kernel, len(lefts), chunks),
        name,
        2 * len(flat) * tokens * width * hidden_units,
        2 * len(lefts) * width * hidden_units,
        grid_spec=pltpu.PrefetchScalarGridSpec(
            num_scalar_prefetch=1,
            grid=(width // size,),
            in_specs=[*[pl.BlockSpec(p.shape, lambda i, order: (0, 0)) for p in flat], *[pl.BlockSpec((size, hidden_units), lambda i, order: (i, 0))] * len(weights)],
            out_specs=[pl.BlockSpec((tokens, size), lambda i, order: (0, i))] * chunks,
        ),
        out_shape=[shaped((tokens, width), low)] * chunks,
    )(places, *flat, *weights)


def weight_kernel(chunks, groups, *refs):
    lefts = refs[:chunks]
    outs = refs[chunks + chunks * groups :]
    for g, out in enumerate(outs):
        rights = refs[chunks + g * chunks : chunks + (g + 1) * chunks]
        out[...] = sum(tn(left[...], right[...]) for left, right in zip(lefts, rights, strict=True)).astype(low)


def weight_gradients(name, lefts, rights, first=0, width=None):
    chunks, groups = len(lefts), len(rights)
    tokens = lefts[0].shape[0]
    width = width or lefts[0].shape[1]
    columns = rights[0][0].shape[1]
    size = 256
    return call(
        functools.partial(weight_kernel, chunks, groups),
        name,
        2 * groups * chunks * tokens * width * columns,
        2 * (groups * (width + chunks * tokens) * columns + chunks * tokens * width),
        grid=(width // size,),
        in_specs=[*[pl.BlockSpec((tokens, size), lambda i: (0, first // size + i))] * chunks, *[whole(tokens, columns)] * (chunks * groups)],
        out_specs=[pl.BlockSpec((size, columns), lambda i: (i, 0))] * groups,
        out_shape=[shaped((width, columns), low)] * groups,
    )(*lefts, *[r for group in rights for r in group])


def split_cores(core, found, own, other):
    rows = own.shape[1]

    @pl.when(core[0] == 0)
    def _():
        own[0] = found[:rows]
        other[0] = found[rows:]

    @pl.when(core[0] != 0)
    def _():
        own[0] = found[rows:]
        other[0] = found[:rows]


def split_kernel(chunks, core, *refs):
    lefts, rights, outs = refs[:chunks], refs[chunks : 2 * chunks], refs[2 * chunks :]
    split_cores(core, sum(tn(left[...], right[...]) for left, right in zip(lefts, rights, strict=True)).astype(low), *outs)


def split_gradient(name, lefts, rights):
    chunks = len(lefts)
    tokens, width = lefts[0].shape
    columns = rights[0].shape[1]
    size = width // 4
    return call(
        functools.partial(split_kernel, chunks),
        name,
        2 * chunks * tokens * width * columns,
        2 * (width * columns + chunks * tokens * (width + columns)),
        grid_spec=pltpu.PrefetchScalarGridSpec(
            num_scalar_prefetch=1,
            grid=(4,),
            in_specs=[*[pl.BlockSpec((tokens, size), lambda i, core: (0, i))] * chunks, *[pl.BlockSpec((tokens, columns), lambda i, core: (0, 0))] * chunks],
            out_specs=[pl.BlockSpec((1, size // 2, columns), lambda i, core: (i, 0, 0))] * 2,
        ),
        out_shape=[shaped((4, size // 2, columns), low)] * 2,
    )(this_core(), *lefts, *rights)


def latents_kernel(query_grad, expanded_grad, rotary, up_q, up_kv, out):
    rank = up_q.shape[0]
    out[:, :rank] = nt(query_grad[...], up_q[...]).astype(low)
    out[:, rank : rank + KVR] = nt(expanded_grad[...], up_kv[...]).astype(low)
    out[:, rank + KVR :] = rotary[...].astype(low)


def latents_back(query_grad, expanded_grad, rotary, up_q, up_kv):
    group, columns = query_grad.shape
    rank = up_q.shape[0]
    size = 256
    row = lambda w: pl.BlockSpec((size, w), lambda i: (i, 0))
    out_width = rank + KVR + LANES
    return call(
        latents_kernel,
        "latents_back",
        2 * group * columns * (rank + KVR),
        4 * group * columns,
        grid=(group // size,),
        in_specs=[row(columns), row(columns), row(LANES), whole(*up_q.shape), whole(*up_kv.shape)],
        out_specs=row(out_width),
        out_shape=shaped((group, out_width), low),
    )(query_grad, expanded_grad, rotary, up_q, up_kv)


def input_kernel(steps, rank, core, own, one, two, joint, gains, chooser, cosine, sine_left, sine_right, weights, hidden, feed_row, middle_grad, *refs):
    downs_grad, (input_gradient, joint_grad, mixed_row, inverse, total) = refs[:-5], refs[-5:]
    step = pl.program_id(0)
    size, columns = weights.shape
    lanes = pl.ds(pl.multiple_of(step * size, size), size)

    @pl.when(step == 0)
    def _():
        values = hidden[...].astype(wide)
        inverse[...] = jnp.broadcast_to(lax.rsqrt(jnp.mean(values * values, axis=-1, keepdims=True) + epsilon), inverse.shape)
        parts = []
        for begin, end in ((0, rank), (rank, rank + KVR)):
            grad = own[:, begin:end].astype(wide) + one[:, begin:end].astype(wide) + two[:, begin:end].astype(wide)
            part = joint[:, begin:end]
            turn = lax.rsqrt(jnp.mean(part * part, axis=-1, keepdims=True) + epsilon)
            unit = part * turn
            parts.append(jnp.sum(grad * unit, axis=0, keepdims=True))
            joint_grad[:, begin:end] = norm_back(grad, unit, turn, gains[2:3, begin:end]).astype(low)
        lane = lax.broadcasted_iota(jnp.int32, (1, LANES), 1)
        last = slice(rank + KVR, rank + KVR + LANES)
        grad = own[:, last].astype(wide) + one[:, last].astype(wide) + two[:, last].astype(wide)
        back = grad * cosine[...] - pltpu.roll(grad, LANES - ROPE // 2, 1) * sine_left[...] - pltpu.roll(grad, ROPE // 2, 1) * sine_right[...]
        back = jnp.where((lane >= NOPE) & (lane < NOPE + ROPE), back, 0.0)
        joint_grad[:, last] = pltpu.roll(back, LANES - NOPE, 1).astype(low)
        norms = jnp.broadcast_to(jnp.concatenate(parts, axis=1), (8, rank + KVR)).astype(low)
        mixed_row[...] = nt(norms, chooser[...])

    unit = hidden[:, lanes].astype(wide) * inverse[:, :1]
    normed = (unit * gains[0:1, lanes]).astype(low)
    back = nt(joint_grad[...], weights[...])
    total[:, lanes] = back
    found = tn(normed, joint_grad[...])
    gain_row = jnp.sum(back * unit, axis=0, keepdims=True)
    gap = lambda n: jnp.zeros((n, size), wide)
    rows = jnp.concatenate([gap(ROPE), gain_row, feed_row[:, lanes], mixed_row[0:1, lanes], gap(LANES - ROPE - 3)], axis=0)
    found = jnp.concatenate([found[:, : columns - LANES], found[:, columns - LANES :] + rows.T], axis=1).astype(low)
    if len(downs_grad) == 1:
        downs_grad[0][...] = found
    else:
        split_cores(core, found, *downs_grad)

    @pl.when(step == steps - 1)
    def _():
        turn = inverse[:, :1]
        input_gradient[...] = (middle_grad[...] + norm_back(total[...], hidden[...].astype(wide) * turn, turn, gains[0:1])).astype(low)


def input_back(terms, joint, gains, chooser, tables, weights, hidden, feed_row, middle_grad, split):
    rows, width = hidden.shape
    columns = weights.shape[1]
    steps = 4
    size = width // steps
    before = (*terms, joint, gains, chooser, *tables)
    if split:
        out_specs = [pl.BlockSpec((1, size // 2, columns), lambda i, core: (i, 0, 0))] * 2
        out_shape = [shaped((4, size // 2, columns), low)] * 2
    else:
        out_specs = [pl.BlockSpec((size, columns), lambda i, core: (i, 0))]
        out_shape = [shaped((width, columns), low)]
    return call(
        functools.partial(input_kernel, steps, columns - KVR - LANES),
        "input_back",
        4 * rows * width * columns,
        4 * width * columns,
        grid_spec=pltpu.PrefetchScalarGridSpec(
            num_scalar_prefetch=1,
            grid=(steps,),
            in_specs=[*[whole(*p.shape) for p in before], pl.BlockSpec((size, columns), lambda i, core: (i, 0)), whole(rows, width), whole(1, width), whole(rows, width)],
            out_specs=[*out_specs, whole(rows, width)],
            scratch_shapes=[pltpu.VMEM((rows, columns), low), pltpu.VMEM((8, width), wide), pltpu.VMEM((rows, LANES), wide), pltpu.VMEM((rows, width), wide)],
        ),
        out_shape=[*out_shape, shaped((rows, width), low)],
    )(this_core(), *before, weights, hidden, feed_row, middle_grad)


def after(value, *earlier):
    return lax.optimization_barrier((value, *earlier))[0]


def after_all(values, *earlier):
    return list(lax.optimization_barrier((tuple(values), earlier))[0])


def gather_near(block):
    return [block, lax.ppermute(block, "tensor", RIGHT), lax.ppermute(block, "tensor", LEFT)]


def gather_far(near):
    half = near[0].shape[0] // 2
    return [lax.ppermute(near[1][:half], "tensor", RIGHT), lax.ppermute(near[2][half:], "tensor", LEFT)]


def scatter_first(own, to_left, to_right, far_first, far_second):
    half = own.shape[0] // 2
    first = lax.ppermute(far_first, "tensor", LEFT)
    second = lax.ppermute(far_second, "tensor", RIGHT)
    return [jnp.concatenate([to_left[:half] + first, to_left[half:]]), jnp.concatenate([to_right[:half], to_right[half:] + second])]


def scatter_second(sent):
    return [lax.ppermute(sent[0], "tensor", LEFT), lax.ppermute(sent[1], "tensor", RIGHT)]


def add_up(*terms):
    return sum(term.astype(wide) for term in terms)


def exchange_line(blocks):
    own, to_left, to_right, far = blocks
    return [own, lax.ppermute(to_right, "tensor", RIGHT), lax.ppermute(to_left, "tensor", LEFT), lax.ppermute(far, "tensor", OPPOSITE)]


def line_order():
    here = lax.axis_index("tensor")
    return [here, (here + 3) % 4, (here + 1) % 4, (here + 2) % 4]


def this_core():
    return lax.axis_index("dp").astype(jnp.int32)[None] % 2


def flips(bit):
    return [(i, i ^ bit) for i in range(8)]


def cube_near(block):
    return [block, lax.ppermute(block, "dp", flips(2)), lax.ppermute(block, "dp", flips(4))]


def cube_far(near):
    half = near[0].shape[0] // 2
    return [lax.ppermute(near[1][:half], "dp", flips(4)), lax.ppermute(near[2][half:], "dp", flips(2))]


def cube_rows(rows):
    here = lax.axis_index("dp")
    places = [here, here ^ 2, here ^ 4, here ^ 6]
    first = [p * rows for p in (*places, places[3])]
    second = [(p ^ 1) * rows for p in (*places, places[3])]
    first[4] += rows // 2
    second[4] += rows // 2
    return first + second


def swap_cores(blocks):
    return [lax.ppermute(value, "dp", flips(1)) for value in blocks]


def scatter_chips(blocks):
    if blocks.ndim == 2:
        return lax.psum_scatter(blocks, "dp", scatter_dimension=0, tiled=True)
    chips, rows, columns = blocks.shape
    return lax.psum_scatter(blocks.reshape(chips * rows, columns), "dp", scatter_dimension=0, tiled=True, axis_index_groups=[[0, 2, 4, 6], [1, 3, 5, 7]])


def scatter_core(blocks):
    count, rows, columns = blocks.shape
    if count != 8:
        return [blocks]
    core = lax.axis_index("dp") % 2
    other = lax.dynamic_index_in_dim(blocks.reshape(4, 2, rows, columns), 1 - core, 1, keepdims=False)
    return [blocks, lax.ppermute(other, "dp", flips(1))]


def scatter_pair(halves, place):
    here = lax.axis_index("dp")
    pick = lambda array, at: lax.dynamic_index_in_dim(array, at, 0, keepdims=False)
    first = here ^ (2 * place) if halves[0].shape[0] == 8 else (here // 2) ^ place
    return add_up(pick(halves[0], first), pick(halves[1], (here // 2) ^ place))


def mix_kernel(one, two, out):
    out[...] = (one[...].astype(wide) + two[...].astype(wide)).astype(low)


def mix(one, two):
    chips, rows, columns = one.shape
    part = pl.BlockSpec((1, rows, columns), lambda i: (i, 0, 0))
    return call(mix_kernel, "mix", 0, 0, grid=(chips,), in_specs=[part, part], out_specs=part, out_shape=shaped(one.shape, low))(one, two)


def corner_kernel(chip, one, two, first, second):
    half = first.shape[0]
    found = (one[0].astype(wide) + two[0].astype(wide)).astype(low)
    first[...] = found[:half]
    second[...] = found[half:]


def side_kernel(lower, chip, one, two, extra, out):
    half = extra.shape[0]
    found = one[0].astype(wide) + two[0].astype(wide)
    more = extra[...].astype(wide)
    if lower:
        out[:half] = found[:half].astype(low)
        out[half:] = (found[half:] + more).astype(low)
    else:
        out[:half] = (found[:half] + more).astype(low)
        out[half:] = found[half:].astype(low)


def pick_call(kernel, name, halves, place, extras, outs):
    _, rows, columns = halves[0].shape
    chip = (lax.axis_index("dp").astype(jnp.int32) // 2) ^ place
    pick = pl.BlockSpec((1, rows, columns), lambda i, chip: (chip[0], 0, 0))
    fixed = lambda shape: pl.BlockSpec(shape, lambda i, chip: (0, 0))
    spec = pltpu.PrefetchScalarGridSpec(
        num_scalar_prefetch=1,
        grid=(1,),
        in_specs=[pick, pick, *[fixed(e.shape) for e in extras]],
        out_specs=[fixed(shape) for shape in outs],
    )
    return call(kernel, name, 0, 0, grid_spec=spec, out_shape=[shaped(shape, low) for shape in outs])(chip[None], *halves, *extras)


def corner_swap(corner):
    return [lax.ppermute(corner[0], "dp", flips(2)), lax.ppermute(corner[1], "dp", flips(4))]


def corner_sum(halves):
    _, rows, columns = halves[0].shape
    if halves[0].shape[0] == 4:
        return pick_call(corner_kernel, "corner", halves, 3, [], [(rows // 2, columns)] * 2)
    corner = scatter_pair(halves, 3).astype(low)
    return [corner[: rows // 2], corner[rows // 2 :]]


def scatter_corner(halves):
    if len(halves) == 1:
        return halves
    return corner_swap(corner_sum(halves))


def scatter_sides(halves, corners):
    if halves[0].shape[0] == 4:
        shape = halves[0].shape[1:]
        return [
            *pick_call(functools.partial(side_kernel, True), "side", halves, 1, [corners[1]], [shape]),
            *pick_call(functools.partial(side_kernel, False), "side", halves, 2, [corners[0]], [shape]),
        ]
    half = halves[0].shape[1] // 2
    across, along = scatter_pair(halves, 1), scatter_pair(halves, 2)
    across = jnp.concatenate([across[:half], across[half:] + corners[1]]).astype(low)
    along = jnp.concatenate([along[:half] + corners[0], along[half:]]).astype(low)
    return [across, along]


def scatter_swap(sides):
    return [lax.ppermute(sides[0], "dp", flips(2)), lax.ppermute(sides[1], "dp", flips(4))]


def scatter_last(halves, swapped):
    return add_up(scatter_pair(halves, 0), *swapped)


def scatter_rest(halves, corners):
    if len(halves) == 1:
        count, rows, columns = halves[0].shape
        return lax.psum_scatter(corners[0].reshape(count * rows, columns), "dp", scatter_dimension=0, tiled=True).astype(wide)
    return scatter_last(halves, scatter_swap(scatter_sides(halves, corners)))


def local(hidden_in, attention_gain, query_down, query_norm, latent_down, latent_norm, query_up, latent_up, output_weight, feed_gain, gate_weight, up_weight, down_weight, cotangent, document_lengths):
    replicas = lax.axis_size("dp")
    rows, width = hidden_in.shape
    group = rows * 4
    rank = query_down.shape[1]
    heads = query_up.shape[1] // (NOPE + ROPE)
    slice_rows = query_down.shape[0]
    order = line_order()
    joint_width = rank + KVR + LANES
    by_line = lambda array: [lax.dynamic_index_in_dim(array, p, 0, keepdims=False) for p in order]

    def column(value):
        return jnp.pad(value, (0, slice_rows - value.shape[0]))[:, None]

    norms = jnp.concatenate([query_norm, latent_norm])
    downs = jnp.concatenate([query_down, latent_down, column(attention_gain), column(feed_gain), column(norms)], axis=1)
    downs = jnp.pad(downs, ((0, 0), (0, joint_width - downs.shape[1])))
    parts = [slice(k * rows // 2, (k + 1) * rows // 2) for k in range(2)]
    if replicas == 8:
        downs = place(exchange_line([downs] * 4), lambda: [p * slice_rows for p in line_order()], 4 * slice_rows)
    out_near = gather_near(after(output_weight.T, downs))

    query_up_wide = jnp.pad(query_up.reshape(-1, heads, NOPE + ROPE), ((0, 0), (0, 0), (0, LANES - NOPE - ROPE))).reshape(-1, heads * LANES)
    ups_all = lax.all_gather(jnp.concatenate([query_up_wide, latent_up], axis=0), "dp", axis=0)
    up_q = ups_all[:, : query_up.shape[0]].reshape(rank, heads * LANES)
    up_kv = ups_all[:, query_up.shape[0] :].reshape(KVR, heads * LANES)

    grad_all = lax.all_gather(cotangent, "tensor", axis=0, tiled=True)
    segment, position = layout(document_lengths[0], group)
    cosine_half, sine_half = rotary_tables(position, ROPE)
    zeros = lambda n: jnp.zeros((group, n), wide)
    cosine_wide = jnp.concatenate([jnp.ones((group, NOPE), wide), cosine_half, cosine_half, zeros(ROPE)], axis=1)
    sine_left = jnp.concatenate([zeros(NOPE), -sine_half, zeros(ROPE // 2 + ROPE)], axis=1)
    sine_right = jnp.concatenate([zeros(NOPE + ROPE // 2), sine_half, zeros(ROPE)], axis=1)
    segment_col, segment_row = segment[:, None], segment[None, :]
    first_row = lax.axis_index("tensor") * rows
    local_tables = [lax.dynamic_slice_in_dim(t, first_row, rows, 0) for t in (cosine_wide, sine_left, sine_right)]
    a, b = query_norm.shape[0], norms.shape[0]
    lanes = jnp.arange(rank + KVR)
    source = jnp.where(lanes < rank, lanes // a * slice_rows + lanes % a, (lanes - rank) // (b - a) * slice_rows + a + (lanes - rank) % (b - a))
    chooser = (jnp.arange(width)[:, None] == source[None, :]).astype(low)
    ready = (chooser, cosine_wide, sine_left, sine_right, segment_col, *local_tables)
    if replicas == 8:
        near = after_all(cube_near(downs), *out_near)
        out_far = gather_far(after_all(out_near, near[1]))
        near = after_all(near + cube_far(near), *out_far)
        down_pieces = after_all(near + swap_cores(near), *ready)
        down_places = jnp.stack(cube_rows(near[0].shape[0])).astype(jnp.int32)
    else:
        down_pieces = [lax.all_gather(downs, ("dp", "tensor"), axis=0, tiled=True)]
        down_places = jnp.zeros((1,), jnp.int32)
        out_far = gather_far(out_near)
    gate_all = lax.all_gather(after(gate_weight, down_pieces[0]), "dp", axis=0, tiled=True)
    weights_down, joint, latents_own, gains = down_projections(hidden_in, down_pieces, down_places, chooser, rank, local_tables)
    feed_scale = gains[1:2]
    latents_near = gather_near(latents_own)
    latents_near = after_all(latents_near, up_q, up_kv)

    out_block = after(jnp.concatenate([*out_near, jnp.concatenate(out_far, axis=0)], axis=1), down_pieces[0])
    if replicas == 8:
        out_blocks = cube_near(out_block)
        latents_near = after_all(latents_near, *out_blocks)
        out_blocks += cube_far(out_blocks)
        out_soon = out_blocks
    else:
        out_all = lax.all_gather(out_block, "dp", axis=0, tiled=True)
        out_soon = [out_all]
    latents_far = gather_far(latents_near)

    def latent_rows():
        here = line_order()
        return [here[0] * rows, here[1] * rows, here[2] * rows, here[3] * rows, here[3] * rows + rows // 2]

    latents = place(after_all(latents_near + latents_far, *out_soon), latent_rows, group)
    upper_all = lax.all_gather(after(up_weight, latents), "dp", axis=0, tiled=True)
    down_all = lax.all_gather(after(down_weight.T, latents), "dp", axis=0, tiled=True)

    block = min(256, group)
    pairs = heads // 2
    by_pair = lambda r, w: pl.BlockSpec((r, w), lambda i: (0, i))
    attended, queries, expanded, log_total = call(
        functools.partial(attention_forward_kernel, rank, block),
        "attention_forward",
        20 * 10**9,
        15 * 10**6,
        grid=(pairs,),
        in_specs=[whole(group, joint_width), by_pair(rank, 2 * LANES), by_pair(KVR, 2 * LANES), whole(group, LANES), whole(group, LANES), whole(group, LANES), whole(group, 1), whole(1, group)],
        out_specs=[by_pair(group, LANES), by_pair(group, 2 * LANES), by_pair(group, 2 * LANES), whole(group, LANES)],
        out_shape=[shaped((group, heads * VD), low), shaped((group, heads * LANES), low), shaped((group, heads * LANES), low), shaped((group, LANES), wide)],
    )(latents, up_q, up_kv, cosine_wide, sine_left, sine_right, segment_col, segment_row)
    log_rows = log_total[:, :16].T

    if replicas == 8:
        out_other = after_all(swap_cores(out_blocks), attended)
        out_all = place(out_blocks + out_other, lambda: cube_rows(out_block.shape[0]), 8 * out_block.shape[0])

    attended_parts = lax.all_to_all(attended.reshape(4, rows, heads * VD), "tensor", 0, 0)
    attended_own = jnp.concatenate(by_line(attended_parts), axis=1)
    attended_own = after(attended_own, grad_all)
    middle = hidden_in.astype(wide) + residual_scale * nt(attended_own, out_all)
    inverse_middle = inverse_rms(middle)
    unit_middle = middle * inverse_middle
    feed_in = (unit_middle * feed_scale).astype(low)

    near_0 = gather_near(feed_in[parts[0]])
    far_0 = gather_far(near_0)
    near_1 = gather_near(after(feed_in[parts[1]], *far_0))
    places = jnp.stack(order).astype(jnp.int32)
    gate, upper, inner_0, feed_0 = feed_forward(near_0 + far_0, gate_all, upper_all)
    far_1 = gather_far(after_all(near_1, inner_0))
    gate_0, upper_0, grad_0 = unit_back(0, places, *after_all([gate, upper], *far_1), grad_all, down_all)
    (part_0,) = feed_back("feed_back", places, [[gate_0], [upper_0]], [gate_all, upper_all])
    gate, upper, inner_1, feed_1 = feed_forward(after_all(near_1 + far_1, part_0), gate_all, upper_all)
    gate_1, upper_1, grad_1 = unit_back(1, places, gate, upper, grad_all, down_all)
    (part_1,) = feed_back("feed_back", places, [[gate_1], [upper_1]], [gate_all, upper_all])
    down_lefts = after_all([grad_0, grad_1], part_1)
    if replicas == 8:
        down_own, down_grad = split_gradient("down_gradient", down_lefts, [inner_0, inner_1])
        down_core = [down_own, *swap_cores([down_grad])]
    else:
        (down_grad,) = weight_gradients("down_gradient", down_lefts, [[inner_0, inner_1]])
        down_core = scatter_core(down_grad.reshape(replicas, -1, down_grad.shape[1]))
    gate_lefts = after_all([feed_0, feed_1], down_grad)
    if replicas == 8:
        gate_own, gate_grad = split_gradient("gate_gradient", gate_lefts, [gate_0, gate_1])
        upper_own, upper_grad = split_gradient("upper_gradient", after_all(gate_lefts, gate_grad), [upper_0, upper_1])
        gate_chips = mix(gate_own, *swap_cores([gate_grad]))
        upper_chips = mix(upper_own, *swap_cores([upper_grad]))
    else:
        gate_grad, upper_grad = weight_gradients("gate_gradient", gate_lefts, [[gate_0, gate_1], [upper_0, upper_1]])
        gate_chips, upper_chips = gate_grad, upper_grad
    got_0 = lax.psum_scatter(part_0, "tensor", scatter_dimension=0, tiled=True)
    got_1 = lax.psum_scatter(part_1, "tensor", scatter_dimension=0, tiled=True)
    down_mixed = corner_sum(down_core) if replicas == 8 else down_core
    down_corner = corner_swap(down_mixed) if replicas == 8 else down_core
    down_sides = scatter_sides(down_core, down_corner) if replicas == 8 else down_corner
    gate_sum = scatter_chips(gate_chips)
    got_0, got_1 = after_all([got_0, got_1], gate_chips, upper_chips, *down_mixed)
    feed_in_grad = jnp.concatenate([got_0, got_1]).astype(wide)

    feed_gain_part = jnp.sum(feed_in_grad * unit_middle, axis=0, keepdims=True)
    middle_grad = cotangent.astype(wide) + norm_back(feed_in_grad, unit_middle, inverse_middle, feed_scale)
    branch_one_grad = (residual_scale * middle_grad).astype(low)
    attended_grad_own = nn(branch_one_grad, out_all).astype(low)
    attended_grads = jnp.zeros((4, rows, heads * VD), low)
    for k, p in enumerate(order):
        attended_grads = lax.dynamic_update_index_in_dim(attended_grads, attended_grad_own[:, k * heads * VD : (k + 1) * heads * VD], p, 0)
    out_left = after(branch_one_grad, attended_grad_own)
    if replicas == 8:
        out_own, out_grad = split_gradient("out_gradient", [out_left], [attended_own])
        out_core = [out_own, *swap_cores([out_grad])]
    else:
        out_grad = tn(out_left, attended_own).astype(low)
        out_core = scatter_core(out_grad.reshape(replicas, -1, 4 * heads * VD))
    attended_grad = lax.all_to_all(after(attended_grads, out_grad), "tensor", 0, 0).reshape(group, heads * VD)
    outs = feed_back("branch_two", places, [after_all([inner_0, inner_1], attended_grad_own)], [down_all])
    attended_grad = after(attended_grad, *outs, *out_core)
    branch_two = [lax.psum_scatter(after(outs[0], attended_grad), "tensor", scatter_dimension=0, tiled=True)]
    upper_sum = scatter_chips(after(upper_chips, attended_grad))
    out_corner = scatter_corner(out_core)
    down_swapped = scatter_swap(down_sides) if replicas == 8 else down_corner

    query_grad, expanded_grad, rotary_grad = call(
        functools.partial(attention_backward_kernel, block),
        "attention_backward",
        30 * 10**9,
        15 * 10**6,
        grid=(pairs,),
        in_specs=[by_pair(group, 2 * LANES), by_pair(group, 2 * LANES), pl.BlockSpec((group, LANES), lambda i: (0, (rank + KVR) // LANES)), whole(group, LANES), whole(group, LANES), whole(group, LANES), whole(group, 1), whole(1, group), whole(16, group), by_pair(group, LANES)],
        out_specs=[by_pair(group, 2 * LANES), by_pair(group, 2 * LANES), whole(group, LANES)],
        out_shape=[shaped((group, heads * LANES), low), shaped((group, heads * LANES), low), shaped((group, LANES), wide)],
        scratch_shapes=[pltpu.VMEM((group, LANES), wide), pltpu.VMEM((group, LANES), wide)],
    )(queries, expanded, latents, cosine_wide, sine_left, sine_right, segment_col, segment_row, log_rows, attended_grad)

    latents_part = latents_back(*after_all([query_grad, expanded_grad, rotary_grad], *down_swapped, *out_corner), up_q, up_kv)
    cut = by_line(latents_part.reshape(4, rows, joint_width))
    sent = scatter_first(*cut[:3], cut[3][: rows // 2], cut[3][rows // 2 :])

    turn = after(latents, *sent)
    (query_up_grad,) = weight_gradients("query_up_gradient", [turn], [[query_grad]], 0, rank)
    (latent_up_grad,) = weight_gradients("latent_up_gradient", [turn], [[expanded_grad]], rank, KVR)
    ups_grad = jnp.concatenate([query_up_grad.reshape(replicas, -1, heads * LANES), latent_up_grad.reshape(replicas, -1, heads * LANES)], axis=1)
    ups_core = scatter_core(ups_grad)
    out_swapped = scatter_swap(scatter_sides(after_all(out_core, cut[0]), out_corner)) if replicas == 8 else out_corner
    latents_terms = after_all([cut[0], *scatter_second(sent)], *ups_core, *out_swapped, *outs)
    branch_two.append(lax.psum_scatter(after(outs[1], *latents_terms), "tensor", scatter_dimension=0, tiled=True))
    ups_corner = scatter_corner(ups_core)
    *downs_grad, input_gradient = input_back(latents_terms, joint, gains, chooser, local_tables, weights_down, hidden_in, feed_gain_part, middle_grad, replicas == 8)
    downs_grad = after_all(downs_grad, *ups_corner)
    if replicas == 8:
        downs_core = [downs_grad[0], *swap_cores(downs_grad[1:])]
        downs_part = scatter_rest(downs_core, scatter_corner(downs_core)).astype(low).reshape(4, slice_rows, joint_width)
        downs_sum = sum(p.astype(wide) for p in exchange_line(by_line(downs_part)))
        out_part = scatter_last(out_core, out_swapped).astype(low)
    else:
        downs_sum = lax.psum_scatter(downs_grad[0], ("dp", "tensor"), scatter_dimension=0, tiled=True).astype(wide)
        out_part = scatter_rest(out_core, out_corner).astype(low)
    out_got = exchange_line([out_part[:, k * heads * VD : (k + 1) * heads * VD] for k in range(4)])
    ups_sum = scatter_rest(ups_core, ups_corner)
    gain_sums = downs_sum[:, rank + KVR + ROPE : rank + KVR + ROPE + 3].T

    output_sum = add_up(*out_got).T

    gate_sum, upper_sum, *branch_two = [v.astype(wide) for v in after_all([gate_sum, upper_sum, *branch_two], downs_sum)]
    layer_output = (middle + residual_scale * jnp.concatenate(branch_two)).astype(low)
    if replicas == 8:
        down_sum = scatter_last(after_all(down_core, *downs_grad), down_swapped).T
    else:
        down_sum = scatter_rest(down_core, down_corner).T
    query_up_sum = ups_sum[: query_up.shape[0]].reshape(-1, heads, LANES)[..., : NOPE + ROPE].reshape(query_up.shape)
    return (
        layer_output,
        input_gradient,
        gain_sums[0],
        downs_sum[:, :rank],
        gain_sums[2, :a],
        downs_sum[:, rank : rank + KVR + ROPE],
        gain_sums[2, a:b],
        query_up_sum,
        ups_sum[query_up.shape[0] :],
        output_sum,
        gain_sums[1],
        gate_sum,
        upper_sum,
        down_sum,
    )


def solution(mesh):
    return jax.shard_map(
        local,
        mesh=mesh,
        in_specs=(
            P(("dp", "tensor"), None),
            P(("dp", "tensor")),
            P(("dp", "tensor"), None),
            P(("dp", "tensor")),
            P(("dp", "tensor"), None),
            P(("dp", "tensor")),
            P("dp", "tensor"),
            P("dp", "tensor"),
            P("tensor", "dp"),
            P(("dp", "tensor")),
            P("dp", "tensor"),
            P("dp", "tensor"),
            P("tensor", "dp"),
            P(("dp", "tensor"), None),
            P("dp", None),
        ),
        out_specs=(
            P(("dp", "tensor"), None),
            P(("dp", "tensor"), None),
            P(("dp", "tensor")),
            P(("dp", "tensor"), None),
            P(("dp", "tensor")),
            P(("dp", "tensor"), None),
            P(("dp", "tensor")),
            P("dp", "tensor"),
            P("dp", "tensor"),
            P("tensor", "dp"),
            P(("dp", "tensor")),
            P("dp", "tensor"),
            P("dp", "tensor"),
            P("tensor", "dp"),
        ),
        check_vma=False,
    )
```

```python
import math, functools
import jax, jax.numpy as jnp
from jax import lax
from jax.experimental import pallas as pl
from jax.experimental.pallas import tpu as pltpu
from jax.sharding import PartitionSpec as P

KVR, ROPE, NOPE, VD = 256, 32, 64, 64
LANES = 128
softmax_scale = 1.0 / math.sqrt(NOPE + ROPE)
log2_scale = softmax_scale / math.log(2.0)


def nt(left, right):
    return lax.dot_general(left, right, (((1,), (1,)), ((), ())), preferred_element_type=jnp.float32)


def nn(left, right):
    return lax.dot_general(left, right, (((1,), (0,)), ((), ())), preferred_element_type=jnp.float32)


def tn(left, right):
    return lax.dot_general(left, right, (((0,), (0,)), ((), ())), preferred_element_type=jnp.float32)


def attention_forward_kernel(rank, block, latents, up_q, up_kv, cosine, sine_left, sine_right, segment_col, segment_row, attended, queries, expanded, log_total):
    pair = pl.program_id(0)
    group = latents.shape[0]
    lane = lax.broadcasted_iota(jnp.int32, (1, LANES), 1)
    rotary = latents[:, rank + KVR :].astype(jnp.float32)

    @pl.when(pair == 0)
    def _():
        log_total[...] = jnp.zeros_like(log_total)

    found = []
    for half in range(2):
        columns = slice(half * LANES, (half + 1) * LANES)
        raw = nn(latents[:, :rank], up_q[:, columns])
        turned = raw * cosine[...] + pltpu.roll(raw, LANES - ROPE // 2, 1) * sine_left[...] + pltpu.roll(raw, ROPE // 2, 1) * sine_right[...]
        query = turned.astype(jnp.bfloat16)
        queries[:, columns] = query
        both = nn(latents[:, rank : rank + KVR], up_kv[:, columns])
        key = jnp.where(lane < NOPE, both, rotary).astype(jnp.bfloat16)
        both = both.astype(jnp.bfloat16)
        expanded[:, columns] = both
        outs, sums = [], []
        for begin in range(0, group, block):
            end = begin + block
            scores = nt(query[begin:end], key[:end]) * log2_scale
            allowed = segment_col[begin:end, :] == segment_row[:, :end]
            row = lax.broadcasted_iota(jnp.int32, (block, end), 0) + begin
            column = lax.broadcasted_iota(jnp.int32, (block, end), 1)
            scores = jnp.where(allowed & (column <= row), scores, -1e30)
            peak = jnp.max(scores, axis=-1, keepdims=True)
            weights = jnp.exp2(scores - peak)
            total = jnp.sum(weights, axis=-1, keepdims=True)
            outs.append(nn(weights.astype(jnp.bfloat16), both[:end]) / total)
            sums.append(peak + jnp.log2(total))
        found.append(jnp.concatenate(outs, axis=0))
        log_total[...] = jnp.where(lane == 2 * pair + half, jnp.concatenate(sums, axis=0), log_total[...])
    attended[...] = jnp.where(lane < VD, pltpu.roll(found[0], VD, 1), found[1]).astype(jnp.bfloat16)


def attention_backward_kernel(block, queries, expanded, rotary_in, cosine, sine_left, sine_right, segment_col, segment_row, log_total, grad, query_grad, expanded_grad, rotary_grad, key_sum, value_sum):
    pair = pl.program_id(0)
    group = queries.shape[0]
    lane = lax.broadcasted_iota(jnp.int32, (1, LANES), 1)
    rotary = rotary_in[...].astype(jnp.float32)

    @pl.when(pair == 0)
    def _():
        rotary_grad[...] = jnp.zeros_like(rotary_grad)

    grads = grad[...].astype(jnp.float32)
    for half in range(2):
        columns = slice(half * LANES, (half + 1) * LANES)
        query = queries[:, columns]
        both = expanded[:, columns]
        key = jnp.where(lane < NOPE, both.astype(jnp.float32), rotary).astype(jnp.bfloat16)
        out_grad = pltpu.roll(grads, VD, 1) if half == 0 else grads
        out_grad = jnp.where(lane < NOPE, 0.0, out_grad).astype(jnp.bfloat16)
        log_row = log_total[pl.ds(2 * pair + half, 1), :]
        parts = []
        for begin in reversed(range(0, group, block)):
            end = begin + block
            scores = nt(key[:end], query[begin:end]) * log2_scale
            allowed = segment_col[:end, :] == segment_row[:, begin:end]
            row = lax.broadcasted_iota(jnp.int32, (end, block), 0)
            column = lax.broadcasted_iota(jnp.int32, (end, block), 1) + begin
            probs = jnp.where(allowed & (row <= column), jnp.exp2(scores - log_row[:, begin:end]), 0.0)
            prob_grad = nt(both[:end], out_grad[begin:end])
            center = jnp.sum(probs * prob_grad, axis=0, keepdims=True)
            score_grad = (probs * (prob_grad - center)).astype(jnp.bfloat16)
            key_part = nn(score_grad, query[begin:end])
            value_part = nn(probs.astype(jnp.bfloat16), out_grad[begin:end])
            if end == group:
                key_sum[...] = key_part
                value_sum[...] = value_part
            else:
                key_sum[:end] += key_part
                value_sum[:end] += value_part
            parts.append(tn(score_grad, key[:end]))
        found = jnp.concatenate(parts[::-1], axis=0) * softmax_scale
        back = found * cosine[...] - pltpu.roll(found, LANES - ROPE // 2, 1) * sine_left[...] - pltpu.roll(found, ROPE // 2, 1) * sine_right[...]
        query_grad[:, columns] = back.astype(jnp.bfloat16)
        keys = key_sum[...] * softmax_scale
        expanded_grad[:, columns] = jnp.where(lane < NOPE, keys, value_sum[...]).astype(jnp.bfloat16)
        rotary_grad[...] += jnp.where((lane >= NOPE) & (lane < NOPE + ROPE), keys, 0.0)


epsilon = 1e-05
residual_scale = 1.4 / math.sqrt(62.0)
rotary_base = 10000.0

RIGHT = [(i, (i + 1) % 4) for i in range(4)]
LEFT = [(i, (i - 1) % 4) for i in range(4)]
OPPOSITE = [(i, (i + 2) % 4) for i in range(4)]


def inverse_rms(values):
    return lax.rsqrt(jnp.mean(values * values, axis=-1, keepdims=True) + epsilon)


def norm_back(grad, unit, inverse, gain):
    scaled = grad * gain
    return inverse * (scaled - unit * jnp.mean(scaled * unit, axis=-1, keepdims=True))


def rotary_tables(positions, width):
    steps = jnp.arange(width // 2, dtype=jnp.float32) * (2.0 / width)
    freqs = jnp.exp(steps * -math.log(rotary_base))
    angles = positions.astype(jnp.float32)[:, None] * freqs[None, :]
    return jnp.cos(angles), jnp.sin(angles)


def layout(lengths_row, group_tokens):
    slots = jnp.arange(group_tokens, dtype=jnp.int32)
    ends = jnp.cumsum(lengths_row)
    segment = jnp.sum((slots[:, None] >= ends[None, :]).astype(jnp.int32), axis=1)
    starts = jnp.concatenate([jnp.zeros((1,), jnp.int32), ends])
    choose = segment[:, None] == jnp.arange(starts.shape[0], dtype=jnp.int32)[None, :]
    start_of = jnp.sum(jnp.where(choose, starts[None, :], 0), axis=1)
    return (segment, slots - start_of)


low, wide = jnp.bfloat16, jnp.float32
VMEM_LIMIT = 56 * 2**20


def call(kernel, name, flops, moved, **how):
    return pl.pallas_call(
        kernel,
        name=name,
        compiler_params=pltpu.CompilerParams(vmem_limit_bytes=VMEM_LIMIT),
        cost_estimate=pl.CostEstimate(flops=0, bytes_accessed=0, transcendentals=0),
        **how,
    )


def whole(*shape):
    return pl.BlockSpec(shape, lambda *i: (0,) * len(shape))


def shaped(shape, dtype):
    return jax.ShapeDtypeStruct(shape, dtype)


def place(blocks, rows_of, total):
    count, width = len(blocks), blocks[0].shape[1]

    def kernel(*refs):
        ins, out, held, done = refs[:count], refs[count], refs[count + 1 : 2 * count + 1], refs[-1]
        arrive = [pltpu.make_async_copy(ref, slot, done.at[0, k]) for k, (ref, slot) in enumerate(zip(ins, held, strict=True))]
        leave = [
            pltpu.make_async_copy(slot, out.at[pl.ds(pl.multiple_of(row, 16), slot.shape[0])], done.at[1, k])
            for k, (slot, row) in enumerate(zip(held, rows_of(), strict=True))
        ]
        for copy in arrive:
            copy.start()
        for first, second in zip(arrive, leave, strict=True):
            first.wait()
            second.start()
        for copy in leave:
            copy.wait()

    return call(
        kernel,
        "place",
        0,
        4 * total * width,
        in_specs=[pl.BlockSpec(memory_space=pl.ANY)] * count,
        out_specs=pl.BlockSpec(memory_space=pl.ANY),
        out_shape=shaped((total, width), blocks[0].dtype),
        scratch_shapes=[*[pltpu.VMEM(b.shape, b.dtype) for b in blocks], pltpu.SemaphoreType.DMA((2, count))],
    )(*blocks)


def join(target, pieces):
    row = 0
    for piece in pieces:
        target[row : row + piece.shape[0]] = piece[...]
        row += piece.shape[0]


def down_kernel(rank, places, hidden, *refs):
    pieces, (chooser, cosine, sine_left, sine_right, weights, joint, latents, gains) = refs[:-8], refs[-8:]
    for k, piece in enumerate(pieces):
        weights[pl.ds(pl.multiple_of(places[k], 16), piece.shape[0])] = piece[...]
    lane = lax.broadcasted_iota(jnp.int32, (1, LANES), 1)
    rows = weights[:, weights.shape[1] - LANES :].astype(wide).T[ROPE : ROPE + 8]
    gains[...] = rows
    chosen = nn(rows.astype(low), chooser[...])
    gains[2:3, : rank + KVR] = chosen[2:3]
    values = hidden[...].astype(wide)
    unit = values * lax.rsqrt(jnp.mean(values * values, axis=-1, keepdims=True) + epsilon)
    normed = (unit * rows[0:1]).astype(low)
    for begin in range(0, weights.shape[1], 384):
        joint[:, begin : begin + 384] = nn(normed, weights[:, begin : begin + 384])
    for begin, end in ((0, rank), (rank, rank + KVR)):
        part = joint[:, begin:end]
        latents[:, begin:end] = (part * lax.rsqrt(jnp.mean(part * part, axis=-1, keepdims=True) + epsilon) * chosen[2:3, begin:end]).astype(low)
    raw = pltpu.roll(joint[:, rank + KVR :], NOPE, 1)
    turned = raw * cosine[...] + pltpu.roll(raw, LANES - ROPE // 2, 1) * sine_left[...] + pltpu.roll(raw, ROPE // 2, 1) * sine_right[...]
    latents[:, rank + KVR :] = jnp.where((lane >= NOPE) & (lane < NOPE + ROPE), turned, 0.0).astype(low)


def down_projections(hidden, pieces, places, chooser, rank, tables):
    rows, width = hidden.shape
    columns = pieces[0].shape[1]
    operands = (hidden, *pieces, chooser, *tables)
    return call(
        functools.partial(down_kernel, rank),
        "down_projections",
        2 * rows * width * columns,
        2 * width * columns,
        grid_spec=pltpu.PrefetchScalarGridSpec(
            num_scalar_prefetch=1,
            grid=(1,),
            in_specs=[whole(*value.shape) for value in operands],
            out_specs=[whole(width, columns), whole(rows, columns), whole(rows, columns), whole(8, width)],
        ),
        out_shape=[shaped((width, columns), low), shaped((rows, columns), wide), shaped((rows, columns), low), shaped((8, width), wide)],
    )(places, *operands)


def feed_kernel(pieces, *refs):
    feeds, (gate_w, upper_w, gate_out, upper_out, inner, feed) = refs[:pieces], refs[pieces:]

    @pl.when(pl.program_id(0) == 0)
    def _():
        join(feed, feeds)

    for begin in range(0, feed.shape[0], 256):
        rows = slice(begin, begin + 256)
        gate = nn(feed[rows], gate_w[...])
        upper = nn(feed[rows], upper_w[...])
        gate_out[rows] = gate.astype(low)
        upper_out[rows] = upper.astype(low)
        inner[rows] = (gate * jax.nn.sigmoid(gate) * upper).astype(low)


def feed_forward(feeds, gate_w, upper_w):
    tokens = sum(p.shape[0] for p in feeds)
    width, hidden_units = gate_w.shape
    size = 256
    column = lambda r: pl.BlockSpec((r, size), lambda i: (0, i))
    return call(
        functools.partial(feed_kernel, len(feeds)),
        "feed_forward",
        4 * tokens * width * hidden_units,
        4 * width * hidden_units,
        grid=(pl.cdiv(hidden_units, size),),
        in_specs=[*[whole(*p.shape) for p in feeds], column(width), column(width)],
        out_specs=[column(tokens), column(tokens), column(tokens), whole(tokens, width)],
        out_shape=[shaped((tokens, hidden_units), low)] * 3 + [shaped((tokens, width), low)],
    )(*feeds, gate_w, upper_w)


def unit_kernel(pieces, places, *refs):
    grads, (gate_in, upper_in, down_w, gate_grad, upper_grad, grad) = refs[:pieces], refs[pieces:]

    @pl.when(pl.program_id(0) == 0)
    def _():
        row = 0
        for piece in grads:
            grad[row : row + piece.shape[0]] = (residual_scale * piece[...].astype(wide)).astype(low)
            row += piece.shape[0]

    for begin in range(0, grad.shape[0], 256):
        rows = slice(begin, begin + 256)
        back = nn(grad[rows], down_w[...])
        gate = gate_in[rows].astype(wide)
        sigmoid = jax.nn.sigmoid(gate)
        gate_grad[rows] = (back * upper_in[rows].astype(wide) * sigmoid * (1.0 + gate * (1.0 - sigmoid))).astype(low)
        upper_grad[rows] = (back * gate * sigmoid).astype(low)


def unit_back(chunk, places, gate, upper, grad_all, down_w):
    tokens, hidden_units = gate.shape
    width = down_w.shape[0]
    size = 256
    column = lambda r: pl.BlockSpec((r, size), lambda i, order: (0, i))
    third, half = tokens // 4, tokens // 8
    near = [pl.BlockSpec((third, width), functools.partial(lambda k, i, order: (order[k] * 2 + chunk, 0), k)) for k in range(3)]
    far = [pl.BlockSpec((half, width), functools.partial(lambda k, i, order: (order[3] * 4 + 2 * chunk + k, 0), k)) for k in range(2)]
    return call(
        functools.partial(unit_kernel, 5),
        "unit_back",
        2 * tokens * width * hidden_units,
        2 * width * hidden_units,
        grid_spec=pltpu.PrefetchScalarGridSpec(
            num_scalar_prefetch=1,
            grid=(pl.cdiv(hidden_units, size),),
            in_specs=[*near, *far, column(tokens), column(tokens), column(width)],
            out_specs=[column(tokens), column(tokens), pl.BlockSpec((tokens, width), lambda i, order: (0, 0))],
        ),
        out_shape=[shaped((tokens, hidden_units), low)] * 2 + [shaped((tokens, width), low)],
    )(places, *[grad_all] * 5, gate, upper, down_w)


def back_kernel(factors, chunks, places, *refs):
    lefts, weights, outs = refs[: factors * chunks], refs[factors * chunks : factors * chunks + factors], refs[factors * chunks + factors :]
    for chunk, out in enumerate(outs):
        found = sum(nt(lefts[f * chunks + chunk][...], weights[f][...]) for f in range(factors)).astype(low)
        rows = out.shape[0] // 4
        for k in range(4):
            out[pl.ds(pl.multiple_of(places[k] * rows, 128), rows)] = found[k * rows : (k + 1) * rows]


def feed_back(name, places, lefts, weights):
    chunks = len(lefts[0])
    flat = [chunk for factor in lefts for chunk in factor]
    tokens, hidden_units = flat[0].shape
    width = weights[0].shape[0]
    size = 256
    return call(
        functools.partial(back_kernel, len(lefts), chunks),
        name,
        2 * len(flat) * tokens * width * hidden_units,
        2 * len(lefts) * width * hidden_units,
        grid_spec=pltpu.PrefetchScalarGridSpec(
            num_scalar_prefetch=1,
            grid=(width // size,),
            in_specs=[*[pl.BlockSpec(p.shape, lambda i, order: (0, 0)) for p in flat], *[pl.BlockSpec((size, hidden_units), lambda i, order: (i, 0))] * len(weights)],
            out_specs=[pl.BlockSpec((tokens, size), lambda i, order: (0, i))] * chunks,
        ),
        out_shape=[shaped((tokens, width), low)] * chunks,
    )(places, *flat, *weights)


def weight_kernel(chunks, groups, *refs):
    lefts = refs[:chunks]
    outs = refs[chunks + chunks * groups :]
    for g, out in enumerate(outs):
        rights = refs[chunks + g * chunks : chunks + (g + 1) * chunks]
        out[...] = sum(tn(left[...], right[...]) for left, right in zip(lefts, rights, strict=True)).astype(low)


def weight_gradients(name, lefts, rights, first=0, width=None):
    chunks, groups = len(lefts), len(rights)
    tokens = lefts[0].shape[0]
    width = width or lefts[0].shape[1]
    columns = rights[0][0].shape[1]
    size = 256
    return call(
        functools.partial(weight_kernel, chunks, groups),
        name,
        2 * groups * chunks * tokens * width * columns,
        2 * (groups * (width + chunks * tokens) * columns + chunks * tokens * width),
        grid=(width // size,),
        in_specs=[*[pl.BlockSpec((tokens, size), lambda i: (0, first // size + i))] * chunks, *[whole(tokens, columns)] * (chunks * groups)],
        out_specs=[pl.BlockSpec((size, columns), lambda i: (i, 0))] * groups,
        out_shape=[shaped((width, columns), low)] * groups,
    )(*lefts, *[r for group in rights for r in group])


def split_cores(core, found, own, other):
    rows = own.shape[1]

    @pl.when(core[0] == 0)
    def _():
        own[0] = found[:rows]
        other[0] = found[rows:]

    @pl.when(core[0] != 0)
    def _():
        own[0] = found[rows:]
        other[0] = found[:rows]


def split_kernel(chunks, core, *refs):
    lefts, rights, outs = refs[:chunks], refs[chunks : 2 * chunks], refs[2 * chunks :]
    split_cores(core, sum(tn(left[...], right[...]) for left, right in zip(lefts, rights, strict=True)).astype(low), *outs)


def split_gradient(name, lefts, rights):
    chunks = len(lefts)
    tokens, width = lefts[0].shape
    columns = rights[0].shape[1]
    size = width // 4
    return call(
        functools.partial(split_kernel, chunks),
        name,
        2 * chunks * tokens * width * columns,
        2 * (width * columns + chunks * tokens * (width + columns)),
        grid_spec=pltpu.PrefetchScalarGridSpec(
            num_scalar_prefetch=1,
            grid=(4,),
            in_specs=[*[pl.BlockSpec((tokens, size), lambda i, core: (0, i))] * chunks, *[pl.BlockSpec((tokens, columns), lambda i, core: (0, 0))] * chunks],
            out_specs=[pl.BlockSpec((1, size // 2, columns), lambda i, core: (i, 0, 0))] * 2,
        ),
        out_shape=[shaped((4, size // 2, columns), low)] * 2,
    )(this_core(), *lefts, *rights)


def latents_kernel(query_grad, expanded_grad, rotary, up_q, up_kv, out):
    rank = up_q.shape[0]
    out[:, :rank] = nt(query_grad[...], up_q[...]).astype(low)
    out[:, rank : rank + KVR] = nt(expanded_grad[...], up_kv[...]).astype(low)
    out[:, rank + KVR :] = rotary[...].astype(low)


def latents_back(query_grad, expanded_grad, rotary, up_q, up_kv):
    group, columns = query_grad.shape
    rank = up_q.shape[0]
    size = 256
    row = lambda w: pl.BlockSpec((size, w), lambda i: (i, 0))
    out_width = rank + KVR + LANES
    return call(
        latents_kernel,
        "latents_back",
        2 * group * columns * (rank + KVR),
        4 * group * columns,
        grid=(group // size,),
        in_specs=[row(columns), row(columns), row(LANES), whole(*up_q.shape), whole(*up_kv.shape)],
        out_specs=row(out_width),
        out_shape=shaped((group, out_width), low),
    )(query_grad, expanded_grad, rotary, up_q, up_kv)


def input_kernel(steps, rank, core, own, one, two, joint, gains, chooser, cosine, sine_left, sine_right, weights, hidden, feed_row, middle_grad, *refs):
    downs_grad, (input_gradient, joint_grad, mixed_row, inverse, total) = refs[:-5], refs[-5:]
    step = pl.program_id(0)
    size, columns = weights.shape
    lanes = pl.ds(pl.multiple_of(step * size, size), size)

    @pl.when(step == 0)
    def _():
        values = hidden[...].astype(wide)
        inverse[...] = jnp.broadcast_to(lax.rsqrt(jnp.mean(values * values, axis=-1, keepdims=True) + epsilon), inverse.shape)
        parts = []
        for begin, end in ((0, rank), (rank, rank + KVR)):
            grad = own[:, begin:end].astype(wide) + one[:, begin:end].astype(wide) + two[:, begin:end].astype(wide)
            part = joint[:, begin:end]
            turn = lax.rsqrt(jnp.mean(part * part, axis=-1, keepdims=True) + epsilon)
            unit = part * turn
            parts.append(jnp.sum(grad * unit, axis=0, keepdims=True))
            joint_grad[:, begin:end] = norm_back(grad, unit, turn, gains[2:3, begin:end]).astype(low)
        lane = lax.broadcasted_iota(jnp.int32, (1, LANES), 1)
        last = slice(rank + KVR, rank + KVR + LANES)
        grad = own[:, last].astype(wide) + one[:, last].astype(wide) + two[:, last].astype(wide)
        back = grad * cosine[...] - pltpu.roll(grad, LANES - ROPE // 2, 1) * sine_left[...] - pltpu.roll(grad, ROPE // 2, 1) * sine_right[...]
        back = jnp.where((lane >= NOPE) & (lane < NOPE + ROPE), back, 0.0)
        joint_grad[:, last] = pltpu.roll(back, LANES - NOPE, 1).astype(low)
        norms = jnp.broadcast_to(jnp.concatenate(parts, axis=1), (8, rank + KVR)).astype(low)
        mixed_row[...] = nt(norms, chooser[...])

    unit = hidden[:, lanes].astype(wide) * inverse[:, :1]
    normed = (unit * gains[0:1, lanes]).astype(low)
    back = nt(joint_grad[...], weights[...])
    total[:, lanes] = back
    found = tn(normed, joint_grad[...])
    gain_row = jnp.sum(back * unit, axis=0, keepdims=True)
    gap = lambda n: jnp.zeros((n, size), wide)
    rows = jnp.concatenate([gap(ROPE), gain_row, feed_row[:, lanes], mixed_row[0:1, lanes], gap(LANES - ROPE - 3)], axis=0)
    found = jnp.concatenate([found[:, : columns - LANES], found[:, columns - LANES :] + rows.T], axis=1).astype(low)
    if len(downs_grad) == 1:
        downs_grad[0][...] = found
    else:
        split_cores(core, found, *downs_grad)

    @pl.when(step == steps - 1)
    def _():
        turn = inverse[:, :1]
        input_gradient[...] = (middle_grad[...] + norm_back(total[...], hidden[...].astype(wide) * turn, turn, gains[0:1])).astype(low)


def input_back(terms, joint, gains, chooser, tables, weights, hidden, feed_row, middle_grad, split):
    rows, width = hidden.shape
    columns = weights.shape[1]
    steps = 4
    size = width // steps
    before = (*terms, joint, gains, chooser, *tables)
    if split:
        out_specs = [pl.BlockSpec((1, size // 2, columns), lambda i, core: (i, 0, 0))] * 2
        out_shape = [shaped((4, size // 2, columns), low)] * 2
    else:
        out_specs = [pl.BlockSpec((size, columns), lambda i, core: (i, 0))]
        out_shape = [shaped((width, columns), low)]
    return call(
        functools.partial(input_kernel, steps, columns - KVR - LANES),
        "input_back",
        4 * rows * width * columns,
        4 * width * columns,
        grid_spec=pltpu.PrefetchScalarGridSpec(
            num_scalar_prefetch=1,
            grid=(steps,),
            in_specs=[*[whole(*p.shape) for p in before], pl.BlockSpec((size, columns), lambda i, core: (i, 0)), whole(rows, width), whole(1, width), whole(rows, width)],
            out_specs=[*out_specs, whole(rows, width)],
            scratch_shapes=[pltpu.VMEM((rows, columns), low), pltpu.VMEM((8, width), wide), pltpu.VMEM((rows, LANES), wide), pltpu.VMEM((rows, width), wide)],
        ),
        out_shape=[*out_shape, shaped((rows, width), low)],
    )(this_core(), *before, weights, hidden, feed_row, middle_grad)


def after(value, *earlier):
    return lax.optimization_barrier((value, *earlier))[0]


def after_all(values, *earlier):
    return list(lax.optimization_barrier((tuple(values), earlier))[0])


def gather_near(block):
    return [block, lax.ppermute(block, "tensor", RIGHT), lax.ppermute(block, "tensor", LEFT)]


def gather_far(near):
    half = near[0].shape[0] // 2
    return [lax.ppermute(near[1][:half], "tensor", RIGHT), lax.ppermute(near[2][half:], "tensor", LEFT)]


def scatter_first(own, to_left, to_right, far_first, far_second):
    half = own.shape[0] // 2
    first = lax.ppermute(far_first, "tensor", LEFT)
    second = lax.ppermute(far_second, "tensor", RIGHT)
    return [jnp.concatenate([to_left[:half] + first, to_left[half:]]), jnp.concatenate([to_right[:half], to_right[half:] + second])]


def scatter_second(sent):
    return [lax.ppermute(sent[0], "tensor", LEFT), lax.ppermute(sent[1], "tensor", RIGHT)]


def add_up(*terms):
    return sum(term.astype(wide) for term in terms)


def exchange_line(blocks):
    own, to_left, to_right, far = blocks
    return [own, lax.ppermute(to_right, "tensor", RIGHT), lax.ppermute(to_left, "tensor", LEFT), lax.ppermute(far, "tensor", OPPOSITE)]


def line_order():
    here = lax.axis_index("tensor")
    return [here, (here + 3) % 4, (here + 1) % 4, (here + 2) % 4]


def this_core():
    return lax.axis_index("dp").astype(jnp.int32)[None] % 2


def flips(bit):
    return [(i, i ^ bit) for i in range(8)]


def cube_near(block):
    return [block, lax.ppermute(block, "dp", flips(2)), lax.ppermute(block, "dp", flips(4))]


def cube_far(near):
    half = near[0].shape[0] // 2
    return [lax.ppermute(near[1][:half], "dp", flips(4)), lax.ppermute(near[2][half:], "dp", flips(2))]


def cube_rows(rows):
    here = lax.axis_index("dp")
    places = [here, here ^ 2, here ^ 4, here ^ 6]
    first = [p * rows for p in (*places, places[3])]
    second = [(p ^ 1) * rows for p in (*places, places[3])]
    first[4] += rows // 2
    second[4] += rows // 2
    return first + second


def swap_cores(blocks):
    return [lax.ppermute(value, "dp", flips(1)) for value in blocks]


def scatter_chips(blocks):
    if blocks.ndim == 2:
        return lax.psum_scatter(blocks, "dp", scatter_dimension=0, tiled=True)
    chips, rows, columns = blocks.shape
    return lax.psum_scatter(blocks.reshape(chips * rows, columns), "dp", scatter_dimension=0, tiled=True, axis_index_groups=[[0, 2, 4, 6], [1, 3, 5, 7]])


def scatter_core(blocks):
    count, rows, columns = blocks.shape
    if count != 8:
        return [blocks]
    core = lax.axis_index("dp") % 2
    other = lax.dynamic_index_in_dim(blocks.reshape(4, 2, rows, columns), 1 - core, 1, keepdims=False)
    return [blocks, lax.ppermute(other, "dp", flips(1))]


def scatter_pair(halves, place):
    here = lax.axis_index("dp")
    pick = lambda array, at: lax.dynamic_index_in_dim(array, at, 0, keepdims=False)
    first = here ^ (2 * place) if halves[0].shape[0] == 8 else (here // 2) ^ place
    return add_up(pick(halves[0], first), pick(halves[1], (here // 2) ^ place))


def mix_kernel(one, two, out):
    out[...] = (one[...].astype(wide) + two[...].astype(wide)).astype(low)


def mix(one, two):
    chips, rows, columns = one.shape
    part = pl.BlockSpec((1, rows, columns), lambda i: (i, 0, 0))
    return call(mix_kernel, "mix", 0, 0, grid=(chips,), in_specs=[part, part], out_specs=part, out_shape=shaped(one.shape, low))(one, two)


def corner_kernel(chip, one, two, first, second):
    half = first.shape[0]
    found = (one[0].astype(wide) + two[0].astype(wide)).astype(low)
    first[...] = found[:half]
    second[...] = found[half:]


def side_kernel(lower, chip, one, two, extra, out):
    half = extra.shape[0]
    found = one[0].astype(wide) + two[0].astype(wide)
    more = extra[...].astype(wide)
    if lower:
        out[:half] = found[:half].astype(low)
        out[half:] = (found[half:] + more).astype(low)
    else:
        out[:half] = (found[:half] + more).astype(low)
        out[half:] = found[half:].astype(low)


def pick_call(kernel, name, halves, place, extras, outs):
    _, rows, columns = halves[0].shape
    chip = (lax.axis_index("dp").astype(jnp.int32) // 2) ^ place
    pick = pl.BlockSpec((1, rows, columns), lambda i, chip: (chip[0], 0, 0))
    fixed = lambda shape: pl.BlockSpec(shape, lambda i, chip: (0, 0))
    spec = pltpu.PrefetchScalarGridSpec(
        num_scalar_prefetch=1,
        grid=(1,),
        in_specs=[pick, pick, *[fixed(e.shape) for e in extras]],
        out_specs=[fixed(shape) for shape in outs],
    )
    return call(kernel, name, 0, 0, grid_spec=spec, out_shape=[shaped(shape, low) for shape in outs])(chip[None], *halves, *extras)


def corner_swap(corner):
    return [lax.ppermute(corner[0], "dp", flips(2)), lax.ppermute(corner[1], "dp", flips(4))]


def corner_sum(halves):
    _, rows, columns = halves[0].shape
    if halves[0].shape[0] == 4:
        return pick_call(corner_kernel, "corner", halves, 3, [], [(rows // 2, columns)] * 2)
    corner = scatter_pair(halves, 3).astype(low)
    return [corner[: rows // 2], corner[rows // 2 :]]


def scatter_corner(halves):
    if len(halves) == 1:
        return halves
    return corner_swap(corner_sum(halves))


def scatter_sides(halves, corners):
    if halves[0].shape[0] == 4:
        shape = halves[0].shape[1:]
        return [
            *pick_call(functools.partial(side_kernel, True), "side", halves, 1, [corners[1]], [shape]),
            *pick_call(functools.partial(side_kernel, False), "side", halves, 2, [corners[0]], [shape]),
        ]
    half = halves[0].shape[1] // 2
    across, along = scatter_pair(halves, 1), scatter_pair(halves, 2)
    across = jnp.concatenate([across[:half], across[half:] + corners[1]]).astype(low)
    along = jnp.concatenate([along[:half] + corners[0], along[half:]]).astype(low)
    return [across, along]


def scatter_swap(sides):
    return [lax.ppermute(sides[0], "dp", flips(2)), lax.ppermute(sides[1], "dp", flips(4))]


def scatter_last(halves, swapped):
    return add_up(scatter_pair(halves, 0), *swapped)


def scatter_rest(halves, corners):
    if len(halves) == 1:
        count, rows, columns = halves[0].shape
        return lax.psum_scatter(corners[0].reshape(count * rows, columns), "dp", scatter_dimension=0, tiled=True).astype(wide)
    return scatter_last(halves, scatter_swap(scatter_sides(halves, corners)))


def local(hidden_in, attention_gain, query_down, query_norm, latent_down, latent_norm, query_up, latent_up, output_weight, feed_gain, gate_weight, up_weight, down_weight, cotangent, document_lengths):
    replicas = lax.axis_size("dp")
    rows, width = hidden_in.shape
    group = rows * 4
    rank = query_down.shape[1]
    heads = query_up.shape[1] // (NOPE + ROPE)
    slice_rows = query_down.shape[0]
    order = line_order()
    joint_width = rank + KVR + LANES
    by_line = lambda array: [lax.dynamic_index_in_dim(array, p, 0, keepdims=False) for p in order]

    def column(value):
        return jnp.pad(value, (0, slice_rows - value.shape[0]))[:, None]

    norms = jnp.concatenate([query_norm, latent_norm])
    downs = jnp.concatenate([query_down, latent_down, column(attention_gain), column(feed_gain), column(norms)], axis=1)
    downs = jnp.pad(downs, ((0, 0), (0, joint_width - downs.shape[1])))
    parts = [slice(k * rows // 2, (k + 1) * rows // 2) for k in range(2)]
    if replicas == 8:
        downs = place(exchange_line([downs] * 4), lambda: [p * slice_rows for p in line_order()], 4 * slice_rows)
    out_near = gather_near(after(output_weight.T, downs))

    query_up_wide = jnp.pad(query_up.reshape(-1, heads, NOPE + ROPE), ((0, 0), (0, 0), (0, LANES - NOPE - ROPE))).reshape(-1, heads * LANES)
    ups_all = lax.all_gather(jnp.concatenate([query_up_wide, latent_up], axis=0), "dp", axis=0)
    up_q = ups_all[:, : query_up.shape[0]].reshape(rank, heads * LANES)
    up_kv = ups_all[:, query_up.shape[0] :].reshape(KVR, heads * LANES)

    grad_all = lax.all_gather(cotangent, "tensor", axis=0, tiled=True)
    segment, position = layout(document_lengths[0], group)
    cosine_half, sine_half = rotary_tables(position, ROPE)
    zeros = lambda n: jnp.zeros((group, n), wide)
    cosine_wide = jnp.concatenate([jnp.ones((group, NOPE), wide), cosine_half, cosine_half, zeros(ROPE)], axis=1)
    sine_left = jnp.concatenate([zeros(NOPE), -sine_half, zeros(ROPE // 2 + ROPE)], axis=1)
    sine_right = jnp.concatenate([zeros(NOPE + ROPE // 2), sine_half, zeros(ROPE)], axis=1)
    segment_col, segment_row = segment[:, None], segment[None, :]
    first_row = lax.axis_index("tensor") * rows
    local_tables = [lax.dynamic_slice_in_dim(t, first_row, rows, 0) for t in (cosine_wide, sine_left, sine_right)]
    a, b = query_norm.shape[0], norms.shape[0]
    lanes = jnp.arange(rank + KVR)
    source = jnp.where(lanes < rank, lanes // a * slice_rows + lanes % a, (lanes - rank) // (b - a) * slice_rows + a + (lanes - rank) % (b - a))
    chooser = (jnp.arange(width)[:, None] == source[None, :]).astype(low)
    ready = (chooser, cosine_wide, sine_left, sine_right, segment_col, *local_tables)
    if replicas == 8:
        near = after_all(cube_near(downs), *out_near)
        out_far = gather_far(after_all(out_near, near[1]))
        near = after_all(near + cube_far(near), *out_far)
        down_pieces = after_all(near + swap_cores(near), *ready)
        down_places = jnp.stack(cube_rows(near[0].shape[0])).astype(jnp.int32)
    else:
        down_pieces = [lax.all_gather(downs, ("dp", "tensor"), axis=0, tiled=True)]
        down_places = jnp.zeros((1,), jnp.int32)
        out_far = gather_far(out_near)
    gate_all = lax.all_gather(after(gate_weight, down_pieces[0]), "dp", axis=0, tiled=True)
    weights_down, joint, latents_own, gains = down_projections(hidden_in, down_pieces, down_places, chooser, rank, local_tables)
    feed_scale = gains[1:2]
    latents_near = gather_near(latents_own)
    latents_near = after_all(latents_near, up_q, up_kv)

    out_block = after(jnp.concatenate([*out_near, jnp.concatenate(out_far, axis=0)], axis=1), down_pieces[0])
    if replicas == 8:
        out_blocks = cube_near(out_block)
        latents_near = after_all(latents_near, *out_blocks)
        out_blocks += cube_far(out_blocks)
        out_soon = out_blocks
    else:
        out_all = lax.all_gather(out_block, "dp", axis=0, tiled=True)
        out_soon = [out_all]
    latents_far = gather_far(latents_near)

    def latent_rows():
        here = line_order()
        return [here[0] * rows, here[1] * rows, here[2] * rows, here[3] * rows, here[3] * rows + rows // 2]

    latents = place(after_all(latents_near + latents_far, *out_soon), latent_rows, group)
    upper_all = lax.all_gather(after(up_weight, latents), "dp", axis=0, tiled=True)
    down_all = lax.all_gather(after(down_weight.T, latents), "dp", axis=0, tiled=True)

    block = min(256, group)
    pairs = heads // 2
    by_pair = lambda r, w: pl.BlockSpec((r, w), lambda i: (0, i))
    attended, queries, expanded, log_total = call(
        functools.partial(attention_forward_kernel, rank, block),
        "attention_forward",
        20 * 10**9,
        15 * 10**6,
        grid=(pairs,),
        in_specs=[whole(group, joint_width), by_pair(rank, 2 * LANES), by_pair(KVR, 2 * LANES), whole(group, LANES), whole(group, LANES), whole(group, LANES), whole(group, 1), whole(1, group)],
        out_specs=[by_pair(group, LANES), by_pair(group, 2 * LANES), by_pair(group, 2 * LANES), whole(group, LANES)],
        out_shape=[shaped((group, heads * VD), low), shaped((group, heads * LANES), low), shaped((group, heads * LANES), low), shaped((group, LANES), wide)],
    )(latents, up_q, up_kv, cosine_wide, sine_left, sine_right, segment_col, segment_row)
    log_rows = log_total[:, :16].T

    if replicas == 8:
        out_other = after_all(swap_cores(out_blocks), attended)
        out_all = place(out_blocks + out_other, lambda: cube_rows(out_block.shape[0]), 8 * out_block.shape[0])

    attended_parts = lax.all_to_all(attended.reshape(4, rows, heads * VD), "tensor", 0, 0)
    attended_own = jnp.concatenate(by_line(attended_parts), axis=1)
    attended_own = after(attended_own, grad_all)
    middle = hidden_in.astype(wide) + residual_scale * nt(attended_own, out_all)
    inverse_middle = inverse_rms(middle)
    unit_middle = middle * inverse_middle
    feed_in = (unit_middle * feed_scale).astype(low)

    near_0 = gather_near(feed_in[parts[0]])
    far_0 = gather_far(near_0)
    near_1 = gather_near(after(feed_in[parts[1]], *far_0))
    places = jnp.stack(order).astype(jnp.int32)
    gate, upper, inner_0, feed_0 = feed_forward(near_0 + far_0, gate_all, upper_all)
    far_1 = gather_far(after_all(near_1, inner_0))
    gate_0, upper_0, grad_0 = unit_back(0, places, *after_all([gate, upper], *far_1), grad_all, down_all)
    (part_0,) = feed_back("feed_back", places, [[gate_0], [upper_0]], [gate_all, upper_all])
    gate, upper, inner_1, feed_1 = feed_forward(after_all(near_1 + far_1, part_0), gate_all, upper_all)
    gate_1, upper_1, grad_1 = unit_back(1, places, gate, upper, grad_all, down_all)
    (part_1,) = feed_back("feed_back", places, [[gate_1], [upper_1]], [gate_all, upper_all])
    down_lefts = after_all([grad_0, grad_1], part_1)
    if replicas == 8:
        down_own, down_grad = split_gradient("down_gradient", down_lefts, [inner_0, inner_1])
        down_core = [down_own, *swap_cores([down_grad])]
    else:
        (down_grad,) = weight_gradients("down_gradient", down_lefts, [[inner_0, inner_1]])
        down_core = scatter_core(down_grad.reshape(replicas, -1, down_grad.shape[1]))
    down_mixed = corner_sum(down_core) if replicas == 8 else down_core
    down_corner = corner_swap(down_mixed) if replicas == 8 else down_core
    gate_lefts = after_all([feed_0, feed_1], down_grad)
    if replicas == 8:
        gate_own, gate_grad = split_gradient("gate_gradient", gate_lefts, [gate_0, gate_1])
        upper_own, upper_grad = split_gradient("upper_gradient", after_all(gate_lefts, gate_grad, *down_mixed), [upper_0, upper_1])
        gate_chips = mix(gate_own, *swap_cores([gate_grad]))
        upper_chips = mix(upper_own, *swap_cores([upper_grad]))
    else:
        gate_grad, upper_grad = weight_gradients("gate_gradient", gate_lefts, [[gate_0, gate_1], [upper_0, upper_1]])
        gate_chips, upper_chips = gate_grad, upper_grad
    got_0 = lax.psum_scatter(part_0, "tensor", scatter_dimension=0, tiled=True)
    got_1 = lax.psum_scatter(part_1, "tensor", scatter_dimension=0, tiled=True)
    down_sides = scatter_sides(down_core, down_corner) if replicas == 8 else down_corner
    gate_sum = scatter_chips(gate_chips)
    got_0, got_1 = after_all([got_0, got_1], gate_chips, upper_chips, *down_sides)
    feed_in_grad = jnp.concatenate([got_0, got_1]).astype(wide)

    feed_gain_part = jnp.sum(feed_in_grad * unit_middle, axis=0, keepdims=True)
    middle_grad = cotangent.astype(wide) + norm_back(feed_in_grad, unit_middle, inverse_middle, feed_scale)
    branch_one_grad = (residual_scale * middle_grad).astype(low)
    attended_grad_own = nn(branch_one_grad, out_all).astype(low)
    attended_grads = jnp.zeros((4, rows, heads * VD), low)
    for k, p in enumerate(order):
        attended_grads = lax.dynamic_update_index_in_dim(attended_grads, attended_grad_own[:, k * heads * VD : (k + 1) * heads * VD], p, 0)
    out_left = after(branch_one_grad, attended_grad_own)
    if replicas == 8:
        out_own, out_grad = split_gradient("out_gradient", [out_left], [attended_own])
        out_core = [out_own, *swap_cores([out_grad])]
    else:
        out_grad = tn(out_left, attended_own).astype(low)
        out_core = scatter_core(out_grad.reshape(replicas, -1, 4 * heads * VD))
    attended_grad = lax.all_to_all(after(attended_grads, out_grad), "tensor", 0, 0).reshape(group, heads * VD)
    outs = feed_back("branch_two", places, [after_all([inner_0, inner_1], attended_grad_own)], [down_all])
    attended_grad = after(attended_grad, *outs, *out_core)
    branch_two = [lax.psum_scatter(after(outs[0], attended_grad), "tensor", scatter_dimension=0, tiled=True)]
    upper_sum = scatter_chips(after(upper_chips, attended_grad))
    out_corner = scatter_corner(out_core)
    down_swapped = scatter_swap(down_sides) if replicas == 8 else down_corner

    query_grad, expanded_grad, rotary_grad = call(
        functools.partial(attention_backward_kernel, block),
        "attention_backward",
        30 * 10**9,
        15 * 10**6,
        grid=(pairs,),
        in_specs=[by_pair(group, 2 * LANES), by_pair(group, 2 * LANES), pl.BlockSpec((group, LANES), lambda i: (0, (rank + KVR) // LANES)), whole(group, LANES), whole(group, LANES), whole(group, LANES), whole(group, 1), whole(1, group), whole(16, group), by_pair(group, LANES)],
        out_specs=[by_pair(group, 2 * LANES), by_pair(group, 2 * LANES), whole(group, LANES)],
        out_shape=[shaped((group, heads * LANES), low), shaped((group, heads * LANES), low), shaped((group, LANES), wide)],
        scratch_shapes=[pltpu.VMEM((group, LANES), wide), pltpu.VMEM((group, LANES), wide)],
    )(queries, expanded, latents, cosine_wide, sine_left, sine_right, segment_col, segment_row, log_rows, attended_grad)

    latents_part = latents_back(*after_all([query_grad, expanded_grad, rotary_grad], *down_swapped, *out_corner), up_q, up_kv)
    cut = by_line(latents_part.reshape(4, rows, joint_width))
    sent = scatter_first(*cut[:3], cut[3][: rows // 2], cut[3][rows // 2 :])

    turn = after(latents, *sent)
    (query_up_grad,) = weight_gradients("query_up_gradient", [turn], [[query_grad]], 0, rank)
    (latent_up_grad,) = weight_gradients("latent_up_gradient", [turn], [[expanded_grad]], rank, KVR)
    ups_grad = jnp.concatenate([query_up_grad.reshape(replicas, -1, heads * LANES), latent_up_grad.reshape(replicas, -1, heads * LANES)], axis=1)
    ups_core = scatter_core(ups_grad)
    out_swapped = scatter_swap(scatter_sides(after_all(out_core, cut[0]), out_corner)) if replicas == 8 else out_corner
    latents_terms = after_all([cut[0], *scatter_second(sent)], *ups_core, *out_swapped, *outs)
    branch_two.append(lax.psum_scatter(after(outs[1], *latents_terms), "tensor", scatter_dimension=0, tiled=True))
    ups_corner = scatter_corner(ups_core)
    *downs_grad, input_gradient = input_back(latents_terms, joint, gains, chooser, local_tables, weights_down, hidden_in, feed_gain_part, middle_grad, replicas == 8)
    downs_grad = after_all(downs_grad, *ups_corner)
    if replicas == 8:
        downs_core = [downs_grad[0], *swap_cores(downs_grad[1:])]
        downs_part = scatter_rest(downs_core, scatter_corner(downs_core)).astype(low).reshape(4, slice_rows, joint_width)
        downs_sum = sum(p.astype(wide) for p in exchange_line(by_line(downs_part)))
        out_part = scatter_last(out_core, out_swapped).astype(low)
    else:
        downs_sum = lax.psum_scatter(downs_grad[0], ("dp", "tensor"), scatter_dimension=0, tiled=True).astype(wide)
        out_part = scatter_rest(out_core, out_corner).astype(low)
    out_got = exchange_line([out_part[:, k * heads * VD : (k + 1) * heads * VD] for k in range(4)])
    ups_sum = scatter_rest(ups_core, ups_corner)
    gain_sums = downs_sum[:, rank + KVR + ROPE : rank + KVR + ROPE + 3].T

    output_sum = add_up(*out_got).T

    gate_sum, upper_sum, *branch_two = [v.astype(wide) for v in after_all([gate_sum, upper_sum, *branch_two], downs_sum)]
    layer_output = (middle + residual_scale * jnp.concatenate(branch_two)).astype(low)
    if replicas == 8:
        down_sum = scatter_last(after_all(down_core, *downs_grad), down_swapped).T
    else:
        down_sum = scatter_rest(down_core, down_corner).T
    query_up_sum = ups_sum[: query_up.shape[0]].reshape(-1, heads, LANES)[..., : NOPE + ROPE].reshape(query_up.shape)
    return (
        layer_output,
        input_gradient,
        gain_sums[0],
        downs_sum[:, :rank],
        gain_sums[2, :a],
        downs_sum[:, rank : rank + KVR + ROPE],
        gain_sums[2, a:b],
        query_up_sum,
        ups_sum[query_up.shape[0] :],
        output_sum,
        gain_sums[1],
        gate_sum,
        upper_sum,
        down_sum,
    )


def solution(mesh):
    return jax.shard_map(
        local,
        mesh=mesh,
        in_specs=(
            P(("dp", "tensor"), None),
            P(("dp", "tensor")),
            P(("dp", "tensor"), None),
            P(("dp", "tensor")),
            P(("dp", "tensor"), None),
            P(("dp", "tensor")),
            P("dp", "tensor"),
            P("dp", "tensor"),
            P("tensor", "dp"),
            P(("dp", "tensor")),
            P("dp", "tensor"),
            P("dp", "tensor"),
            P("tensor", "dp"),
            P(("dp", "tensor"), None),
            P("dp", None),
        ),
        out_specs=(
            P(("dp", "tensor"), None),
            P(("dp", "tensor"), None),
            P(("dp", "tensor")),
            P(("dp", "tensor"), None),
            P(("dp", "tensor")),
            P(("dp", "tensor"), None),
            P(("dp", "tensor")),
            P("dp", "tensor"),
            P("dp", "tensor"),
            P("tensor", "dp"),
            P(("dp", "tensor")),
            P("dp", "tensor"),
            P("dp", "tensor"),
            P("tensor", "dp"),
        ),
        check_vma=False,
    )
```
